32 devices in a mesh: dp: 16 (over z, x, core), tensor: 2 (over y).
Axes of the slice: x: 2, y: 2, z: 4, core: 2. Of those that a mesh axis runs over, the one named last changes fastest.
Arguments:
- hidden: bfloat16 [32, 1024, 1024], P('dp'), may hold values from -6 to 6
- segment_ids: int32 [32, 1024], P('dp'), may hold values from 0 to 3, never falling along the last dimension, each value on 1 to 800 neighbouring positions
- norm_gain: float32 [1024], replicated, may hold values from 0.1 to 1.9
- proj_gate: bfloat16 [1024, 2048], P(None, 'tensor'), may hold values from -0.1875 to 0.1875
- proj_value: bfloat16 [1024, 2048], P(None, 'tensor'), may hold values from -0.1875 to 0.1875
- proj_state: bfloat16 [1024, 256], replicated, may hold values from -0.1875 to 0.1875
- proj_step: bfloat16 [1024, 32], P(None, 'tensor'), may hold values from -0.1875 to 0.1875
- conv_value: float32 [4, 2048], P(None, 'tensor'), may hold values from -3 to 3
- conv_value_bias: float32 [2048], P('tensor'), may hold values from -3 to 3
- conv_state: float32 [4, 256], replicated, may hold values from -3 to 3
- conv_state_bias: float32 [256], replicated, may hold values from -3 to 3
- step_bias: float32 [32], P('tensor'), may hold values from -6 to -2
- decay_log: float32 [32], P('tensor'), may hold values from 0 to 2.77
- skip_gain: float32 [32], P('tensor'), may hold values from 0.5 to 1.5
- gate_gain: float32 [2048], P('tensor'), may hold values from 0.1 to 1.9
- proj_out: bfloat16 [1024, 2048], P(None, 'tensor'), may hold values from -0.125 to 0.125
- out_grad: bfloat16 [32, 1024, 1024], P('dp'), may hold values from -6 to 6
Outputs:
- block_out: bfloat16 [32, 1024, 1024], P('dp')
- grad_hidden: float32 [32, 1024, 1024], P('dp')
- grad_norm_gain: float32 [1024], replicated
- grad_proj_gate: float32 [1024, 2048], P('dp', 'tensor')
- grad_proj_value: float32 [1024, 2048], P('dp', 'tensor')
- grad_proj_state: float32 [1024, 256], P('dp')
- grad_proj_step: float32 [1024, 32], P('dp', 'tensor')
- grad_conv_value: float32 [4, 2048], P(None, 'tensor')
- grad_conv_value_bias: float32 [2048], P('tensor')
- grad_conv_state: float32 [4, 256], replicated
- grad_conv_state_bias: float32 [256], replicated
- grad_step_bias: float32 [32], P('tensor')
- grad_decay_log: float32 [32], P('tensor')
- grad_skip_gain: float32 [32], P('tensor')
- grad_gate_gain: float32 [2048], P('tensor')
- grad_proj_out: float32 [1024, 2048], P('dp', 'tensor')
The draws below stay inside these ranges and needn't reach their ends.
Inputs may be any that keep to these rules, and one draw needn't show every extreme that they name: `segment_ids`: tokens of a sequence with the same number form one document; numbers never fall along a sequence; each sequence holds 4 documents of 1 to 800 tokens, one of exactly 800.
All inputs are finite; a program needn't handle non-finite values.
Results may differ from the reference program's by a relative error of at most 0.019.
Values sent between devices are 32-bit elements; how exact they have to be, the bound alone decides.
A program may use at most 192 MiB of HBM per device.

```python
import math
import jax
import jax.numpy as jnp
import numpy as np
from jax import lax

D = 1024
HEADS = 32
HEAD_DIM = 64
STATE = 128
KERNEL = 4
LEN = 1024
DOCS = 4
INNER = 2048
MOST = 800
SEQUENCES = 32


def block_scale(key, shape, pieces, least, largest):
    loudness, own = 1.0, jax.random.fold_in(key, 6)
    for dim, blocks in pieces:
        steps = jnp.exp(jax.random.uniform(jax.random.fold_in(own, dim), (blocks,), jnp.float32, least / len(pieces), largest / len(pieces)))
        loudness = loudness * jnp.repeat(steps, shape[dim] // blocks).reshape([-1 if axis == dim else 1 for axis in range(len(shape))])
    return loudness


def length_profile(number_of, total, most, slope):
    portions = [(1 << 20) // math.isqrt(grade ** slope) + 1 for grade in range(2, number_of + 1)]
    surplus, holding = total - most - (number_of - 1), [1] * (number_of - 1)
    while surplus > 0:
        candidates = [i for i in range(number_of - 1) if holding[i] < most]
        pool, remaining = sum([portions[i] for i in candidates]), surplus
        for i in candidates:
            addition = min(most - holding[i], max(1, remaining * portions[i] // pool), surplus)
            holding[i] = holding[i] + addition
            surplus = surplus - addition
    return np.array([most] + holding)


def uneven(stream_key, number_of, total, reach, skew):
    if number_of == 2:
        one = jax.random.randint(stream_key, (), max(1, total - reach), min(reach, total - 1) + 1)
        return jnp.stack([one, total - one])
    tallies = jnp.asarray(length_profile(number_of, total, reach, skew), jnp.int32)
    couples = (number_of - 1) // 2
    giver, receiver = tallies[1:1 + 2 * couples:2], tallies[2:2 + 2 * couples:2]
    margin = jnp.minimum(giver - 1, reach - receiver)
    shifted = jax.random.randint(jax.random.fold_in(stream_key, 1), (couples,), 0, 1 << 20) % (margin + 1)
    tallies = tallies.at[1:1 + 2 * couples:2].set(giver - shifted).at[2:2 + 2 * couples:2].set(receiver + shifted)
    return tallies[jax.random.permutation(jax.random.fold_in(stream_key, 2), number_of)]


def noise(key, dims, scale, limit, cuts=(), kind=jnp.bfloat16):
    factor_of = block_scale(key, dims, cuts, -0.22, 0.18) if cuts else 1.0
    drawn = jax.random.normal(key, dims, jnp.float32) * scale * factor_of
    return jnp.minimum(jnp.maximum(drawn, -limit), limit).astype(kind)


def setup_inputs(seed: int = 0) -> dict:
    splits = jax.random.split(jax.random.key(seed), 18)
    hidden = noise(splits[0], (SEQUENCES, LEN, D), 1.0, 6.0, ((0, 16),))
    segment_ids = jax.vmap(lambda own: jnp.searchsorted(jnp.cumsum(uneven(own, DOCS, LEN, MOST, 0)), jnp.arange(LEN), side="right"))(jax.random.split(splits[1], SEQUENCES)).reshape((SEQUENCES, LEN)).astype(jnp.int32)
    norm_gain = jnp.clip(1.0 + 0.18 * jax.random.normal(splits[2], (D,), jnp.float32), 0.1, 1.9)
    proj_gate = noise(splits[3], (D, INNER), D ** -0.5, 0.1875, ((1, 2),))
    proj_value = noise(splits[4], (D, INNER), D ** -0.5, 0.1875, ((1, 2),))
    proj_state = noise(splits[5], (D, 2 * STATE), D ** -0.5, 0.1875)
    proj_step = noise(splits[6], (D, HEADS), D ** -0.5, 0.1875, ((1, 2),))
    conv_value = noise(splits[7], (KERNEL, INNER), KERNEL ** -0.5, 3.0, ((1, 2),), jnp.float32)
    conv_value_bias = noise(splits[8], (INNER,), 0.5, 3.0, ((0, 2),), jnp.float32)
    conv_state = noise(splits[9], (KERNEL, 2 * STATE), KERNEL ** -0.5, 3.0, (), jnp.float32)
    conv_state_bias = noise(splits[10], (2 * STATE,), 0.5, 3.0, (), jnp.float32)
    step_bias = jnp.clip(-6.0 + 4.0 * jax.random.uniform(splits[11], (HEADS,), jnp.float32) ** block_scale(splits[11], (HEADS,), ((0, 2),), -0.2, 0.2), -6.0, -2.0)
    decay_log = jnp.clip(2.77 * jax.random.uniform(splits[12], (HEADS,), jnp.float32) ** block_scale(splits[12], (HEADS,), ((0, 2),), -0.2, 0.2), 0.0, 2.77)
    skip_gain = jnp.clip(0.5 + 1.0 * jax.random.uniform(splits[13], (HEADS,), jnp.float32) ** block_scale(splits[13], (HEADS,), ((0, 2),), -0.2, 0.2), 0.5, 1.5)
    gate_gain = jnp.clip(1.0 + 0.18 * jax.random.normal(splits[14], (INNER,), jnp.float32), 0.1, 1.9)
    proj_out = noise(splits[15], (D, INNER), INNER ** -0.5, 0.125, ((1, 2),))
    out_grad = noise(splits[16], (SEQUENCES, LEN, D), 1.0, 6.0, ((0, 16),))
    return {"hidden": hidden, "segment_ids": segment_ids, "norm_gain": norm_gain, "proj_gate": proj_gate, "proj_value": proj_value, "proj_state": proj_state, "proj_step": proj_step, "conv_value": conv_value, "conv_value_bias": conv_value_bias, "conv_state": conv_state, "conv_state_bias": conv_state_bias, "step_bias": step_bias, "decay_log": decay_log, "skip_gain": skip_gain, "gate_gain": gate_gain, "proj_out": proj_out, "out_grad": out_grad}


epsilon = 1e-05
precise = lax.Precision.HIGHEST

@jax.custom_vjp
def low(v):
    return lax.optimization_barrier(v.astype(jnp.bfloat16)).astype(jnp.float32)

@jax.custom_vjp
def low_back(v):
    return v

def low_keep(v):
    return (low(v), None)

def low_pass(kept, grad):
    return (grad,)

def back_keep(v):
    return (v, None)

def back_low(kept, grad):
    return (low(grad),)
low.defvjp(low_keep, low_pass)
low_back.defvjp(back_keep, back_low)

def rounded_both(v):
    return low_back(low(v))

def lag_masks(segment_row):
    length = segment_row.shape[0]
    result = [jnp.ones((length,), jnp.float32)]
    for delay in range(1, KERNEL):
        earlier = jnp.concatenate([jnp.full((delay,), -1, jnp.int32), segment_row[:length - delay].astype(jnp.int32)])
        result.append((earlier == segment_row.astype(jnp.int32)).astype(jnp.float32))
    return result

def causal_conv(values, weight, conv_bias, doc_masks):
    length = values.shape[0]
    summed = conv_bias[None, :] + weight[KERNEL - 1][None, :] * values
    for delay in range(1, KERNEL):
        earlier = jnp.concatenate([jnp.zeros((delay, values.shape[1]), jnp.float32), values[:length - delay]], axis=0)
        summed = summed + weight[KERNEL - 1 - delay][None, :] * earlier * doc_masks[delay][:, None]
    return jax.nn.silu(summed)

def head_mix(values, states, step_raw, segment_row, step_bias, decay_log, skip_gain):
    length = values.shape[0]
    head_count = step_raw.shape[1]
    state_low = rounded_both(states)
    value_low = rounded_both(values)
    state_in = state_low[:, :STATE]
    state_out = state_low[:, STATE:]
    step_size = jax.nn.softplus(step_raw + step_bias[None, :])
    decay_rate = -jnp.exp(decay_log)
    running = jnp.cumsum(step_size * decay_rate[None, :], axis=0)
    places = jnp.arange(length)
    allowed = (places[:, None] >= places[None, :]) & (segment_row[:, None] == segment_row[None, :])
    affinity = jnp.dot(state_out, state_in.T, precision=precise)
    per_head = values.reshape(length, head_count, HEAD_DIM)
    low_head = value_low.reshape(length, head_count, HEAD_DIM)

    def one_head(items):
        run_col, step_col, head_values = items
        decays = jnp.exp(jnp.where(allowed, run_col[:, None] - run_col[None, :], -1e+30))
        mix_weights = rounded_both(decays * affinity * step_col[None, :])
        return jnp.dot(mix_weights, head_values, precision=precise)
    mixed_heads = lax.map(jax.checkpoint(one_head), (running.T, step_size.T, low_head.transpose(1, 0, 2)))
    mixed_out = mixed_heads.transpose(1, 0, 2) + skip_gain[None, :, None] * per_head
    return mixed_out.reshape(length, head_count * HEAD_DIM)

def residual_block(hidden_row, segment_row, norm_gain, proj_gate, proj_value, proj_state, proj_step, conv_value, conv_value_bias, conv_state, conv_state_bias, step_bias, decay_log, skip_gain, gate_gain, proj_out):
    row_scale = lax.rsqrt(lax.optimization_barrier(jnp.mean(hidden_row * hidden_row, axis=-1, keepdims=True)) + epsilon)
    normed = low(hidden_row * row_scale * norm_gain[None, :])
    gate_raw = low_back(jnp.dot(normed, proj_gate, precision=precise))
    value_raw = low_back(jnp.dot(normed, proj_value, precision=precise))
    state_raw = jnp.dot(normed, proj_state, precision=precise)
    step_raw = low_back(jnp.dot(normed, proj_step, precision=precise))
    doc_masks = lag_masks(segment_row)
    value_conv = causal_conv(value_raw, conv_value, conv_value_bias, doc_masks)
    state_conv = causal_conv(state_raw, conv_state, conv_state_bias, doc_masks)
    mixed_out = head_mix(value_conv, state_conv, step_raw, segment_row, step_bias, decay_log, skip_gain)
    gated = mixed_out * jax.nn.silu(gate_raw)
    gated_scale = lax.rsqrt(lax.optimization_barrier(jnp.mean(gated * gated, axis=-1, keepdims=True)) + epsilon)
    output_in = low(gated * gated_scale * gate_gain[None, :])
    return hidden_row + jnp.dot(output_in, proj_out.T, precision=precise)

def reference(hidden, segment_ids, norm_gain, proj_gate, proj_value, proj_state, proj_step, conv_value, conv_value_bias, conv_state, conv_state_bias, step_bias, decay_log, skip_gain, gate_gain, proj_out, out_grad):
    weights = tuple((w.astype(jnp.float32) for w in (norm_gain, proj_gate, proj_value, proj_state, proj_step, conv_value, conv_value_bias, conv_state, conv_state_bias, step_bias, decay_log, skip_gain, gate_gain, proj_out)))

    def per_sequence(totals, items):
        hidden_row, segment_row, cotangent = items

        def forward(inputs, *params):
            return residual_block(inputs, segment_row, *params)
        result, pullback = jax.vjp(forward, hidden_row.astype(jnp.float32), *weights)
        grads = pullback(cotangent.astype(jnp.float32))
        totals = tuple((t + g for t, g in zip(totals, grads[1:])))
        return (totals, (result.astype(jnp.bfloat16), grads[0]))
    zeros = tuple((jnp.zeros_like(w) for w in weights))
    totals, (block_out, grad_hidden) = lax.scan(per_sequence, zeros, (hidden, segment_ids, out_grad))
    g_norm, g_gate, g_value, g_state, g_step, g_conv_value, g_conv_value_bias, g_conv_state, g_conv_state_bias, g_step_bias, g_decay, g_skip, g_gate_gain, g_out = totals
    return (block_out, grad_hidden, g_norm, g_gate, g_value, g_state, g_step, g_conv_value, g_conv_value_bias, g_conv_state, g_conv_state_bias, g_step_bias, g_decay, g_skip, g_gate_gain, g_out)
```

```python
import functools

import jax
import jax.numpy as jnp
from jax import lax
from jax.experimental import pallas as pl
from jax.experimental.pallas import tpu as pltpu
from jax.sharding import PartitionSpec as P

HEAD_DIM = 64
STATE = 128
KERNEL = 4
VMEM_BYTES = 50 * 1024 * 1024

epsilon = 1e-05
precise = lax.Precision.HIGHEST


def lag_masks(segment_row):
    length = segment_row.shape[0]
    result = [jnp.ones((length,), jnp.float32)]
    for delay in range(1, KERNEL):
        earlier = jnp.concatenate(
            [jnp.full((delay,), -1, jnp.int32), segment_row[: length - delay]]
        )
        result.append((earlier == segment_row).astype(jnp.float32))
    return result


def causal_conv(values, weight, conv_bias, doc_masks):
    length = values.shape[0]
    summed = conv_bias[None, :] + weight[KERNEL - 1][None, :] * values
    for delay in range(1, KERNEL):
        earlier = jnp.concatenate(
            [jnp.zeros((delay, values.shape[1]), jnp.float32), values[: length - delay]], axis=0
        )
        summed = summed + weight[KERNEL - 1 - delay][None, :] * earlier * doc_masks[delay][:, None]
    return jax.nn.silu(summed)


CHUNK = 128
PAIR = 2 * HEAD_DIM
LOG2E = 1.4426950408889634
NN = (((1,), (0,)), ((), ()))
NT = (((1,), (1,)), ((), ()))
TN = (((0,), (0,)), ((), ()))
bf16 = jnp.bfloat16


def mxu(a, b, dims=NN):
    return lax.dot_general(a, b, dims, preferred_element_type=jnp.float32)


def sigmoid(z):
    return 0.5 * jnp.tanh(0.5 * z) + 0.5


def pair_wide(rows, at):
    top = jnp.broadcast_to(rows[at : at + 1], (HEAD_DIM, CHUNK))
    low = jnp.broadcast_to(rows[at + 1 : at + 2], (HEAD_DIM, CHUNK))
    return jnp.concatenate([top, low], axis=0)


def decay_block(rows, h):
    run = jnp.broadcast_to(rows[h : h + 1], (CHUNK, CHUNK))
    return jnp.exp2(jnp.minimum(run - run.T, 0.0))


def doc_block(masks):
    segment = jnp.broadcast_to(masks[3:4], (CHUNK, CHUNK))
    source = lax.broadcasted_iota(jnp.int32, (CHUNK, CHUNK), 0)
    target = lax.broadcasted_iota(jnp.int32, (CHUNK, CHUNK), 1)
    return ((segment == segment.T) & (source <= target)).astype(jnp.float32)


def shifted_taps(raw, before, masks):
    lane = lax.broadcasted_iota(jnp.int32, raw.shape, 1)
    taps = [raw]
    for k in range(1, KERNEL):
        moved = pltpu.roll(jnp.where(lane >= CHUNK - k, before, raw), k, 1)
        taps.append(moved * masks[k - 1 : k])
    return taps


def conv_sum(taps, conv_ref, part):
    total = conv_ref[KERNEL, part, :]
    for k in range(KERNEL):
        total = total + conv_ref[KERNEL - 1 - k, part, :] * taps[k]
    return total


def mix_kernel(
    raw_ref, gate_ref, dout_ref, rows_ref, mask_ref, into_ref, outt_ref, conv_ref, gain_ref,
    mixed_ref, entry_ref, sums_ref, held_ref, before_ref,
):
    @pl.when(pl.program_id(1) == 0)
    def _():
        held_ref[...] = jnp.zeros_like(held_ref)
        before_ref[...] = jnp.zeros_like(before_ref)

    masks = mask_ref[0]
    into, outt = into_ref[...], outt_ref[...]
    affinity = mxu(into, outt) * doc_block(masks)

    def body(p, sums):
        part = pl.ds(pl.multiple_of(p * PAIR, PAIR), PAIR)
        rows = rows_ref[0, p]
        raw = raw_ref[part, :].astype(jnp.float32)
        pre = conv_sum(shifted_taps(raw, before_ref[part, :], masks), conv_ref, part)
        value = pre * sigmoid(pre)
        scaled = value * pair_wide(rows, 2)
        low = scaled.astype(bf16)
        near = []
        for h in range(2):
            mixing = (decay_block(rows, h) * affinity).astype(bf16)
            near.append(mxu(low[h * HEAD_DIM : (h + 1) * HEAD_DIM], mixing))
        held = held_ref[part, :]
        held_low = held.astype(bf16)
        entry_ref[0, part, :] = held_low
        far = mxu(held_low, outt) * pair_wide(rows, 6)
        kept = (scaled * pair_wide(rows, 4)).astype(bf16)
        held_ref[part, :] = held * pair_wide(rows, 8) + mxu(kept, into)
        mixed = jnp.concatenate(near, axis=0) + far + pair_wide(rows, 10) * value
        mixed_ref[part, :] = mixed
        before_ref[part, :] = raw
        gate = gate_ref[part, :].astype(jnp.float32)
        gated = mixed * gate * sigmoid(gate)
        square = jnp.sum(gated * gated, axis=0, keepdims=True)
        inner = dout_ref[part, :].astype(jnp.float32) * gain_ref[part, :] * gated
        return sums[0] + square, sums[1] + jnp.sum(inner, axis=0, keepdims=True)

    zero = jnp.zeros((1, CHUNK), jnp.float32)
    square, inner = lax.fori_loop(0, raw_ref.shape[0] // PAIR, body, (zero, zero))
    sums_ref[0, 0:1, :] = square
    sums_ref[0, 1:2, :] = inner


def back_kernel(
    raw_ref, before_ref, mixed_ref, dmix_ref, entry_ref, rows_ref, mask_ref, into_ref, intot_ref,
    out_ref, outt_ref, conv_ref,
    draw_ref, drows_ref, dstate_ref, dconv_ref, dheld_ref, later_ref, latermask_ref, dfar_ref,
):
    step = pl.program_id(1)

    @pl.when((pl.program_id(0) == 0) & (step == 0))
    def _():
        dconv_ref[...] = jnp.zeros_like(dconv_ref)

    @pl.when(step == 0)
    def _():
        dheld_ref[...] = jnp.zeros_like(dheld_ref)
        later_ref[...] = jnp.zeros_like(later_ref)
        latermask_ref[...] = jnp.zeros_like(latermask_ref)

    first = step == pl.num_programs(1) - 1
    masks, later_masks = mask_ref[0], latermask_ref[...]
    into, intot, out, outt = into_ref[...], intot_ref[...], out_ref[...], outt_ref[...]
    allowed = doc_block(masks)
    affinity = mxu(into, outt) * allowed
    dfar_ref[...] = jnp.zeros_like(dfar_ref)
    lane = lax.broadcasted_iota(jnp.int32, (PAIR, CHUNK), 1)
    head_row = lax.broadcasted_iota(jnp.int32, (PAIR, CHUNK), 0) < HEAD_DIM

    def body(p, daffinity):
        part = pl.ds(pl.multiple_of(p * PAIR, PAIR), PAIR)
        rows = rows_ref[0, p]
        raw = raw_ref[part, :].astype(jnp.float32)
        before = jnp.where(first, 0.0, before_ref[part, :].astype(jnp.float32))
        taps = shifted_taps(raw, before, masks)
        pre = conv_sum(taps, conv_ref, part)
        gate = sigmoid(pre)
        value = pre * gate
        step_wide = pair_wide(rows, 2)
        skip_wide = pair_wide(rows, 10)
        keep_wide = pair_wide(rows, 4)
        scaled = value * step_wide
        low = scaled.astype(bf16)
        dmix_low = dmix_ref[part, :]
        dmix = dmix_low.astype(jnp.float32)
        halves = jnp.concatenate(
            [jnp.where(head_row, dmix, 0.0).astype(bf16), jnp.where(head_row, 0.0, dmix).astype(bf16)],
            axis=1,
        )
        dmixing = mxu(low, halves, TN)
        dnear = []
        for h in range(2):
            decay = decay_block(rows, h)
            mixing = (decay * affinity).astype(bf16)
            daffinity = daffinity + dmixing[:, h * CHUNK : (h + 1) * CHUNK] * decay
            dnear.append(mxu(dmix_low[h * HEAD_DIM : (h + 1) * HEAD_DIM], mixing, NT))
        dnear = jnp.concatenate(dnear, axis=0)
        held_low = entry_ref[0, part, :]
        dheld = dheld_ref[part, :]
        dheld_low = dheld.astype(bf16)
        carried = dheld * pair_wide(rows, 8)
        dfar = mxu(dheld_low, intot) * keep_wide
        kept = (scaled * keep_wide).astype(bf16)
        read = (dmix * pair_wide(rows, 6)).astype(bf16)
        dfar_ref[:, :STATE] += mxu(kept, dheld_low, TN)
        dfar_ref[:, STATE:] += mxu(read, held_low, TN)
        dheld_ref[part, :] = carried + mxu(read, out)
        dscaled = dnear + dfar
        scaled_low = low.astype(jnp.float32)
        far_product = scaled * dfar
        running = (
            dmix * (mixed_ref[part, :] - skip_wide * value) - scaled_low * dnear - far_product
        )
        products = (
            running, far_product, carried * held_low.astype(jnp.float32), dscaled * value,
            dmix * value,
        )
        for q, product in enumerate(products):
            for h in range(2):
                drows_ref[0, p, 2 * q + h : 2 * q + h + 1, :] = jnp.sum(
                    product[h * HEAD_DIM : (h + 1) * HEAD_DIM], axis=0, keepdims=True
                )
        dvalue = dscaled * step_wide + skip_wide * dmix
        dpre = dvalue * (gate * (1.0 + pre * (1.0 - gate)))
        later = later_ref[part, :]
        dconv_ref[KERNEL, part, :] += dpre
        dconv_ref[KERNEL - 1, part, :] += dpre * raw
        draw = conv_ref[KERNEL - 1, part, :] * dpre
        for k in range(1, KERNEL):
            dconv_ref[KERNEL - 1 - k, part, :] += dpre * taps[k]
            joined = jnp.where(
                lane < k, later * later_masks[k - 1 : k], dpre * masks[k - 1 : k]
            )
            draw = draw + conv_ref[KERNEL - 1 - k, part, :] * pltpu.roll(joined, CHUNK - k, 1)
        later_ref[part, :] = dpre
        draw_ref[part, :] = draw.astype(bf16)
        return daffinity

    daffinity = lax.fori_loop(
        0, raw_ref.shape[0] // PAIR, body, jnp.zeros((CHUNK, CHUNK), jnp.float32)
    )
    daffinity = (daffinity * allowed).astype(bf16)
    dstate_ref[:, :STATE] = dfar_ref[:, :STATE] + mxu(daffinity, out)
    dstate_ref[:, STATE:] = dfar_ref[:, STATE:] + mxu(daffinity, into, TN)
    latermask_ref[...] = masks


def spec(block, index):
    return pl.BlockSpec(block, index)


def mix_forward(seqs, raw, gate, dout, rows, masks, into, outt, conv, gain):
    ch, tokens = raw.shape
    chunks = tokens // seqs // CHUNK
    at = lambda s, c: (0, s * chunks + c)
    up = lambda s, c: (s * chunks + c, 0)
    slab = spec((ch, CHUNK), at)
    return pl.pallas_call(
        mix_kernel,
        grid=(seqs, chunks),
        in_specs=[
            slab, slab, slab,
            spec((1,) + rows.shape[1:], lambda s, c: (s * chunks + c, 0, 0, 0)),
            spec((1, 8, CHUNK), lambda s, c: (s * chunks + c, 0, 0)),
            spec((CHUNK, STATE), up),
            spec((STATE, CHUNK), at),
            spec(conv.shape, lambda s, c: (0, 0, 0)),
            spec((ch, CHUNK), lambda s, c: (0, 0)),
        ],
        out_specs=[
            slab,
            spec((1, ch, STATE), lambda s, c: (s * chunks + c, 0, 0)),
            spec((1, 8, CHUNK), lambda s, c: (s * chunks + c, 0, 0)),
        ],
        out_shape=[
            jax.ShapeDtypeStruct((ch, tokens), jnp.float32),
            jax.ShapeDtypeStruct((seqs * chunks, ch, STATE), bf16),
            jax.ShapeDtypeStruct((seqs * chunks, 8, CHUNK), jnp.float32),
        ],
        scratch_shapes=[
            pltpu.VMEM((ch, STATE), jnp.float32),
            pltpu.VMEM((ch, CHUNK), jnp.float32),
        ],
        compiler_params=pltpu.CompilerParams(vmem_limit_bytes=VMEM_BYTES),
        cost_estimate=pl.CostEstimate(
            flops=tokens * ch * 1024, bytes_accessed=tokens * ch * 18, transcendentals=tokens * ch * 4
        ),
        name="mix_forward",
    )(raw, gate, dout, rows, masks, into, outt, conv, gain)


def mix_backward(seqs, raw, mixed, dmix, entry, rows, masks, into, intot, out, outt, conv):
    ch, tokens = raw.shape
    chunks = tokens // seqs // CHUNK
    place = lambda s, c: s * chunks + chunks - 1 - c
    at = lambda s, c: (0, place(s, c))
    up = lambda s, c: (place(s, c), 0)
    slab = spec((ch, CHUNK), at)
    row_spec = spec((1,) + rows.shape[1:], lambda s, c: (place(s, c), 0, 0, 0))
    return pl.pallas_call(
        back_kernel,
        grid=(seqs, chunks),
        in_specs=[
            slab,
            spec((ch, CHUNK), lambda s, c: (0, jnp.maximum(place(s, c) - 1, 0))),
            slab, slab,
            spec((1, ch, STATE), lambda s, c: (place(s, c), 0, 0)),
            row_spec,
            spec((1, 8, CHUNK), lambda s, c: (place(s, c), 0, 0)),
            spec((CHUNK, STATE), up),
            spec((STATE, CHUNK), at),
            spec((CHUNK, STATE), up),
            spec((STATE, CHUNK), at),
            spec(conv.shape, lambda s, c: (0, 0, 0)),
        ],
        out_specs=[
            slab,
            row_spec,
            spec((CHUNK, 2 * STATE), up),
            spec(conv.shape, lambda s, c: (0, 0, 0)),
        ],
        out_shape=[
            jax.ShapeDtypeStruct((ch, tokens), bf16),
            jax.ShapeDtypeStruct(rows.shape, jnp.float32),
            jax.ShapeDtypeStruct((tokens, 2 * STATE), jnp.float32),
            jax.ShapeDtypeStruct(conv.shape, jnp.float32),
        ],
        scratch_shapes=[
            pltpu.VMEM((ch, STATE), jnp.float32),
            pltpu.VMEM((ch, CHUNK), jnp.float32),
            pltpu.VMEM((8, CHUNK), jnp.float32),
            pltpu.VMEM((CHUNK, 2 * STATE), jnp.float32),
        ],
        compiler_params=pltpu.CompilerParams(vmem_limit_bytes=VMEM_BYTES),
        cost_estimate=pl.CostEstimate(
            flops=tokens * ch * 2048, bytes_accessed=tokens * ch * 16, transcendentals=tokens * ch * 4
        ),
        name="mix_backward",
    )(raw, raw, mixed, dmix, entry, rows, masks, into, intot, out, outt, conv)


def wide_lanes(columns):
    return jnp.broadcast_to(columns[..., None], columns.shape + (CHUNK,))


def pair_rows(parts, seqs):
    heads, _, chunks, _ = parts[0].shape
    stacked = jnp.stack(parts + [jnp.zeros_like(parts[0])] * (8 - len(parts)))
    stacked = stacked.reshape(8, heads // 2, 2, seqs * chunks, CHUNK)
    return stacked.transpose(3, 1, 0, 2, 4).reshape(seqs * chunks, heads // 2, 16, CHUNK)


def unpair_rows(rows, q, seqs):
    steps, pairs = rows.shape[:2]
    part = rows[:, :, 2 * q : 2 * q + 2, :].transpose(1, 2, 0, 3)
    return part.reshape(2 * pairs, seqs, steps // seqs, CHUNK)


def step_rows(step_raw, step_bias, decay_log, skip_gain, segment_ids):
    seqs, length = segment_ids.shape
    chunks = length // CHUNK
    heads = step_raw.shape[0]
    rate = -jnp.exp(decay_log)
    size = jax.nn.softplus(step_raw + step_bias[:, None]).reshape(heads, seqs, chunks, CHUNK)
    places = jnp.arange(CHUNK)
    upper = (places[:, None] <= places[None, :]).astype(jnp.float32)
    running = jnp.einsum(
        "hqcs,st->hqct", size * rate[:, None, None, None], upper, precision=precise
    )
    segments = segment_ids.reshape(seqs, chunks, CHUNK)
    last = segments[:, :, -1]
    before = jnp.concatenate([jnp.full((seqs, 1), -1, jnp.int32), last[:, :-1]], axis=1)
    total = running[..., -1:]
    at_end = (segments == last[..., None]).astype(jnp.float32)
    from_start = (segments == before[..., None]).astype(jnp.float32)
    through = (last == before).astype(jnp.float32)[..., None]
    full = jnp.ones_like(running)
    parts = [
        running * LOG2E,
        size,
        jnp.exp(total - running) * at_end,
        jnp.exp(running) * from_start,
        jnp.exp(total) * through * full,
        skip_gain[:, None, None, None] * full,
    ]
    lags = [jnp.stack(lag_masks(row)[1:]) for row in segment_ids]
    lags = jnp.stack(lags).reshape(seqs, KERNEL - 1, chunks, CHUNK).transpose(0, 2, 1, 3)
    masks = jnp.concatenate(
        [
            lags,
            segments[:, :, None, :].astype(jnp.float32),
            jnp.zeros((seqs, chunks, 4, CHUNK), jnp.float32),
        ],
        axis=2,
    ).reshape(seqs * chunks, 8, CHUNK)
    return pair_rows(parts, seqs), masks


def step_grads(drows, step_raw, step_bias, decay_log, seqs):
    heads, tokens = step_raw.shape
    running, far, carried, direct, skip = [unpair_rows(drows, q, seqs) for q in range(5)]
    rate = -jnp.exp(decay_log)[:, None, None, None]
    biased = step_raw + step_bias[:, None]
    size = jax.nn.softplus(biased).reshape(running.shape)
    total = jnp.sum(far + carried, axis=-1, keepdims=True)
    places = jnp.arange(CHUNK)
    lower = (places[:, None] >= places[None, :]).astype(jnp.float32)
    ddrop = jnp.einsum("hqct,ts->hqcs", running, lower, precision=precise) + total
    dsize = direct + ddrop * rate
    draw = dsize.reshape(heads, tokens) * jax.nn.sigmoid(biased)
    every = (1, 2, 3)
    return (
        draw,
        jnp.sum(draw, axis=1),
        jnp.sum(ddrop * size * rate, axis=every),
        jnp.sum(skip, axis=every),
    )


def out_product(left, weight):
    return lax.dot_general(left, weight, (((0,), (1,)), ((), ())), preferred_element_type=jnp.float32)


def in_product(weight, tokens):
    return lax.dot_general(weight, tokens, (((0,), (1,)), ((), ())), preferred_element_type=jnp.float32)


def grad_product(tokens, channels):
    return lax.dot_general(
        tokens, channels, (((0,), (1,)), ((), ())), preferred_element_type=jnp.float32
    )


def right_product(left, weight):
    return lax.dot_general(
        left, weight, (((1,), (1,)), ((), ())), preferred_element_type=jnp.float32
    )


def token_product(left, right):
    return lax.dot_general(
        left, right, (((0,), (0,)), ((), ())), preferred_element_type=jnp.float32
    )


def tensor_others(part):
    count = lax.axis_size("tensor")
    if count == 2:
        return lax.ppermute(part, "tensor", [(0, 1), (1, 0)])
    return lax.psum(part, "tensor")


def tensor_join(part, others):
    return part + others if lax.axis_size("tensor") == 2 else others


def after(value, *earlier):
    return lax.optimization_barrier((value, *earlier))[0]


def local(
    hidden,
    segment_ids,
    norm_gain,
    proj_gate,
    proj_value,
    proj_state,
    proj_step,
    conv_value,
    conv_value_bias,
    conv_state,
    conv_state_bias,
    step_bias,
    decay_log,
    skip_gain,
    gate_gain,
    proj_out,
    out_grad,
):
    seq_count, length, width = hidden.shape
    local_inner = proj_gate.shape[1]
    state_width = proj_state.shape[1]
    tensor_count = lax.axis_size("tensor")
    inner_total = local_inner * tensor_count
    every = range(seq_count)

    wides = [hidden[s].astype(jnp.float32) for s in every]
    row_scales = [
        lax.rsqrt(jnp.mean(w * w, axis=-1, keepdims=True) + epsilon) for w in wides
    ]
    normeds = [
        (w * r * norm_gain[None, :]).astype(jnp.bfloat16) for w, r in zip(wides, row_scales)
    ]
    conv_wide = wide_lanes(jnp.concatenate([conv_value, conv_value_bias[None, :]], axis=0))
    gain_wide = wide_lanes(gate_gain)

    gates, douts, raws, steps, rows, masks, states = [], [], [], [], [], [], []
    state_backs, mixeds, entries, boths = [], [], [], []
    for s in every:
        gates.append(in_product(proj_gate, normeds[s]))
        raws.append(in_product(proj_value, normeds[s]))
        steps.append(in_product(proj_step, normeds[s]))
        douts.append(in_product(proj_out, out_grad[s]))
        state_raw = jnp.dot(normeds[s], proj_state, preferred_element_type=jnp.float32)
        state_conv, back = jax.vjp(
            functools.partial(causal_conv, doc_masks=lag_masks(segment_ids[s])),
            state_raw,
            conv_state,
            conv_state_bias,
        )
        state_backs.append(back)
        low = state_conv.astype(jnp.bfloat16)
        into, out = low[:, :STATE], low[:, STATE:]
        states.append((into, into.T, out, out.T))
        row, mask = step_rows(steps[s], step_bias, decay_log, skip_gain, segment_ids[s : s + 1])
        rows.append(row)
        masks.append(mask)
        mixed, entry, sums = mix_forward(
            1, raws[s], gates[s], douts[s], row, mask, into, out.T, conv_wide, gain_wide
        )
        mixeds.append(mixed)
        entries.append(entry)
        sums = sums[:, :2].transpose(1, 0, 2).reshape(2, length)
        boths.append(tensor_join(sums, tensor_others(sums)))

    branches, received, output_ins, d_gates, d_mixeds = [], [], [], [], []
    grad_gate_gain = jnp.zeros((local_inner,), jnp.float32)
    for s in every:
        gate, mixed, dout = gates[s], mixeds[s], douts[s]
        sigma = jax.nn.sigmoid(gate)
        gated = mixed * gate * sigma
        gated_scale = lax.rsqrt(boths[s][0:1] / inner_total + epsilon)
        gate_inner = boths[s][1:2]
        output_in = (gated * gated_scale * gate_gain[:, None]).astype(jnp.bfloat16)
        branches.append(out_product(output_in, proj_out))
        received.append(tensor_others(branches[s]))
        grad_gate_gain = grad_gate_gain + jnp.sum(dout * gated * gated_scale, axis=1)
        weighted = dout * gate_gain[:, None]
        d_gated = gated_scale * weighted - gated_scale**3 * gated * gate_inner / inner_total
        d_mixeds.append((d_gated * gate * sigma).astype(jnp.bfloat16))
        d_gates.append(
            (d_gated * mixed * sigma * (1.0 + gate * (1.0 - sigma))).astype(jnp.bfloat16)
        )
        output_ins.append(output_in)

    normed_all = jnp.concatenate(normeds, axis=0)
    early_part = jnp.stack(
        [
            grad_product(normed_all, jnp.concatenate(d_gates, axis=1)),
            grad_product(
                out_grad.reshape(seq_count * length, width), jnp.concatenate(output_ins, axis=1)
            ),
        ]
    )
    early = lax.psum_scatter(early_part, "dp", scatter_dimension=1, tiled=True)

    param_grads, d_values, d_states, d_steps = None, [], [], []
    parts, others, grad_hiddens = [], [], []
    waits = (early_part, *branches)
    grad_norm_gain = jnp.zeros((width,), jnp.float32)
    for s in every:
        d_value, d_rows, d_state, d_conv = mix_backward(
            1, raws[s], mixeds[s], after(d_mixeds[s], *waits), entries[s], rows[s], masks[s],
            *states[s], conv_wide,
        )
        d_step, g_sb, g_dl, g_sg = step_grads(d_rows, steps[s], step_bias, decay_log, 1)
        d_state = d_state.astype(jnp.bfloat16).astype(jnp.float32)
        d_state, g_cs, g_csb = state_backs[s](d_state)
        d_conv = jnp.sum(d_conv, axis=-1)
        grads = (d_conv[:KERNEL], d_conv[KERNEL], g_cs, g_csb, g_sb, g_dl, g_sg)
        param_grads = grads if s == 0 else [a + b for a, b in zip(param_grads, grads)]
        d_values.append(d_value)
        d_states.append(d_state.astype(jnp.bfloat16))
        d_steps.append(d_step.astype(jnp.bfloat16))
        part = (
            out_product(d_gates[s], proj_gate)
            + out_product(d_value, proj_value)
            + right_product(d_states[s], proj_state)
            + out_product(d_steps[s], proj_step)
        )
        grad_norm_gain = grad_norm_gain + jnp.sum(part * wides[s] * row_scales[s], axis=0)
        parts.append(part)
        if s < seq_count - 1:
            parts[s] = after(part, received[s])
            others.append(tensor_others(parts[s]))
            waits = (part, received[s])
    g_cv, g_cvb, g_cs, g_csb, g_sb, g_dl, g_sg = param_grads
    own = [g_cv, g_cvb, g_sb, g_dl, g_sg, grad_gate_gain]
    shared = [g_cs, g_csb, grad_norm_gain]
    own_flat = jnp.concatenate([g.reshape(-1) for g in own])
    place = lax.axis_index("tensor")
    mine = (jnp.arange(tensor_count) == place)[:, None]
    slots = jnp.where(mine, own_flat[None, :], 0.0).reshape(-1)
    packed = lax.psum(
        after(
            jnp.concatenate([slots] + [g.reshape(-1) for g in shared]),
            early,
            received[-1],
            *others,
        ),
        ("dp", "tensor"),
    )
    own_sum = lax.dynamic_slice(packed, (place * own_flat.shape[0],), (own_flat.shape[0],))
    shared_sum = packed[slots.shape[0] :]

    later_value = lax.psum_scatter(
        grad_product(normed_all, after(jnp.concatenate(d_values, axis=1), packed)),
        "dp",
        scatter_dimension=0,
        tiled=True,
    )
    later_rest = lax.psum_scatter(
        jnp.concatenate(
            [
                token_product(normed_all, jnp.concatenate(d_states, axis=0)),
                grad_product(normed_all, jnp.concatenate(d_steps, axis=1)),
            ],
            axis=1,
        ),
        "dp",
        scatter_dimension=0,
        tiled=True,
    )
    block_outs = []
    for s in every:
        if s == seq_count - 1:
            parts[s] = after(parts[s], packed)
            others.append(tensor_others(parts[s]))
        d_scaled = tensor_join(parts[s], others[s]) * norm_gain[None, :]
        row_scale, wide = row_scales[s], wides[s]
        norm_inner = jnp.sum(d_scaled * wide, axis=-1, keepdims=True)
        grad_hiddens.append(
            out_grad[s].astype(jnp.float32)
            + row_scale * d_scaled
            - row_scale**3 * wide * norm_inner / width
        )
        branch = tensor_join(branches[s], received[s])
        block_outs.append((wide + branch).astype(jnp.bfloat16))
    grad_proj_state = lax.psum(later_rest[:, :state_width], "tensor")

    def split(flat, like):
        result, edge = [], 0
        for g in like:
            result.append(flat[edge : edge + g.size].reshape(g.shape))
            edge += g.size
        return result

    r_cv, r_cvb, r_sb, r_dl, r_sg, r_gg = split(own_sum, own)
    r_cs, r_csb, r_ng = split(shared_sum, shared)
    return (
        jnp.stack(block_outs),
        jnp.stack(grad_hiddens),
        r_ng,
        early[0],
        later_value,
        grad_proj_state,
        later_rest[:, state_width:],
        r_cv,
        r_cvb,
        r_cs,
        r_csb,
        r_sb,
        r_dl,
        r_sg,
        r_gg,
        early[1],
    )


def solution(mesh):
    in_specs = (
        P("dp", None, None),
        P("dp", None),
        P(),
        P(None, "tensor"),
        P(None, "tensor"),
        P(),
        P(None, "tensor"),
        P(None, "tensor"),
        P("tensor"),
        P(),
        P(),
        P("tensor"),
        P("tensor"),
        P("tensor"),
        P("tensor"),
        P(None, "tensor"),
        P("dp", None, None),
    )
    out_specs = (
        P("dp", None, None),
        P("dp", None, None),
        P(),
        P("dp", "tensor"),
        P("dp", "tensor"),
        P("dp", None),
        P("dp", "tensor"),
        P(None, "tensor"),
        P("tensor"),
        P(),
        P(),
        P("tensor"),
        P("tensor"),
        P("tensor"),
        P("tensor"),
        P("dp", "tensor"),
    )
    return jax.shard_map(local, mesh=mesh, in_specs=in_specs, out_specs=out_specs, check_vma=False)
```

```python
import functools

import jax
import jax.numpy as jnp
from jax import lax
from jax.experimental import pallas as pl
from jax.experimental.pallas import tpu as pltpu
from jax.sharding import PartitionSpec as P

HEAD_DIM = 64
STATE = 128
KERNEL = 4
VMEM_BYTES = 50 * 1024 * 1024

epsilon = 1e-05
precise = lax.Precision.HIGHEST


def lag_masks(segment_row):
    length = segment_row.shape[0]
    result = [jnp.ones((length,), jnp.float32)]
    for delay in range(1, KERNEL):
        earlier = jnp.concatenate(
            [jnp.full((delay,), -1, jnp.int32), segment_row[: length - delay]]
        )
        result.append((earlier == segment_row).astype(jnp.float32))
    return result


def causal_conv(values, weight, conv_bias, doc_masks):
    length = values.shape[0]
    summed = conv_bias[None, :] + weight[KERNEL - 1][None, :] * values
    for delay in range(1, KERNEL):
        earlier = jnp.concatenate(
            [jnp.zeros((delay, values.shape[1]), jnp.float32), values[: length - delay]], axis=0
        )
        summed = summed + weight[KERNEL - 1 - delay][None, :] * earlier * doc_masks[delay][:, None]
    return jax.nn.silu(summed)


CHUNK = 128
PAIR = 2 * HEAD_DIM
LOG2E = 1.4426950408889634
NN = (((1,), (0,)), ((), ()))
NT = (((1,), (1,)), ((), ()))
TN = (((0,), (0,)), ((), ()))
bf16 = jnp.bfloat16


def mxu(a, b, dims=NN):
    return lax.dot_general(a, b, dims, preferred_element_type=jnp.float32)


def sigmoid(z):
    return 0.5 * jnp.tanh(0.5 * z) + 0.5


def pair_wide(rows, at):
    top = jnp.broadcast_to(rows[at : at + 1], (HEAD_DIM, CHUNK))
    low = jnp.broadcast_to(rows[at + 1 : at + 2], (HEAD_DIM, CHUNK))
    return jnp.concatenate([top, low], axis=0)


def decay_block(rows, h):
    run = jnp.broadcast_to(rows[h : h + 1], (CHUNK, CHUNK))
    return jnp.exp2(jnp.minimum(run - run.T, 0.0))


def doc_block(masks):
    segment = jnp.broadcast_to(masks[3:4], (CHUNK, CHUNK))
    source = lax.broadcasted_iota(jnp.int32, (CHUNK, CHUNK), 0)
    target = lax.broadcasted_iota(jnp.int32, (CHUNK, CHUNK), 1)
    return ((segment == segment.T) & (source <= target)).astype(jnp.float32)


def shifted_taps(raw, before, masks):
    lane = lax.broadcasted_iota(jnp.int32, raw.shape, 1)
    taps = [raw]
    for k in range(1, KERNEL):
        moved = pltpu.roll(jnp.where(lane >= CHUNK - k, before, raw), k, 1)
        taps.append(moved * masks[k - 1 : k])
    return taps


def conv_sum(taps, conv_ref, part):
    total = conv_ref[KERNEL, part, :]
    for k in range(KERNEL):
        total = total + conv_ref[KERNEL - 1 - k, part, :] * taps[k]
    return total


def mix_kernel(
    raw_ref, gate_ref, dout_ref, rows_ref, mask_ref, into_ref, outt_ref, conv_ref, gain_ref,
    mixed_ref, entry_ref, sums_ref, held_ref, before_ref,
):
    @pl.when(pl.program_id(1) == 0)
    def _():
        held_ref[...] = jnp.zeros_like(held_ref)
        before_ref[...] = jnp.zeros_like(before_ref)

    masks = mask_ref[0]
    into, outt = into_ref[...], outt_ref[...]
    affinity = mxu(into, outt) * doc_block(masks)

    def body(p, sums):
        part = pl.ds(pl.multiple_of(p * PAIR, PAIR), PAIR)
        rows = rows_ref[0, p]
        raw = raw_ref[part, :].astype(jnp.float32)
        pre = conv_sum(shifted_taps(raw, before_ref[part, :], masks), conv_ref, part)
        value = pre * sigmoid(pre)
        scaled = value * pair_wide(rows, 2)
        low = scaled.astype(bf16)
        near = []
        for h in range(2):
            mixing = (decay_block(rows, h) * affinity).astype(bf16)
            near.append(mxu(low[h * HEAD_DIM : (h + 1) * HEAD_DIM], mixing))
        held = held_ref[part, :]
        held_low = held.astype(bf16)
        entry_ref[0, part, :] = held_low
        far = mxu(held_low, outt) * pair_wide(rows, 6)
        kept = (scaled * pair_wide(rows, 4)).astype(bf16)
        held_ref[part, :] = held * pair_wide(rows, 8) + mxu(kept, into)
        mixed = jnp.concatenate(near, axis=0) + far + pair_wide(rows, 10) * value
        mixed_ref[part, :] = mixed
        before_ref[part, :] = raw
        gate = gate_ref[part, :].astype(jnp.float32)
        gated = mixed * gate * sigmoid(gate)
        square = jnp.sum(gated * gated, axis=0, keepdims=True)
        inner = dout_ref[part, :].astype(jnp.float32) * gain_ref[part, :] * gated
        return sums[0] + square, sums[1] + jnp.sum(inner, axis=0, keepdims=True)

    zero = jnp.zeros((1, CHUNK), jnp.float32)
    square, inner = lax.fori_loop(0, raw_ref.shape[0] // PAIR, body, (zero, zero))
    sums_ref[0, 0:1, :] = square
    sums_ref[0, 1:2, :] = inner


def back_kernel(
    raw_ref, before_ref, mixed_ref, dmix_ref, entry_ref, rows_ref, mask_ref, into_ref, intot_ref,
    out_ref, outt_ref, conv_ref,
    draw_ref, drows_ref, dstate_ref, dconv_ref, dheld_ref, later_ref, latermask_ref, dfar_ref,
):
    step = pl.program_id(1)

    @pl.when((pl.program_id(0) == 0) & (step == 0))
    def _():
        dconv_ref[...] = jnp.zeros_like(dconv_ref)

    @pl.when(step == 0)
    def _():
        dheld_ref[...] = jnp.zeros_like(dheld_ref)
        later_ref[...] = jnp.zeros_like(later_ref)
        latermask_ref[...] = jnp.zeros_like(latermask_ref)

    first = step == pl.num_programs(1) - 1
    masks, later_masks = mask_ref[0], latermask_ref[...]
    into, intot, out, outt = into_ref[...], intot_ref[...], out_ref[...], outt_ref[...]
    allowed = doc_block(masks)
    affinity = mxu(into, outt) * allowed
    dfar_ref[...] = jnp.zeros_like(dfar_ref)
    lane = lax.broadcasted_iota(jnp.int32, (PAIR, CHUNK), 1)
    head_row = lax.broadcasted_iota(jnp.int32, (PAIR, CHUNK), 0) < HEAD_DIM

    def body(p, daffinity):
        part = pl.ds(pl.multiple_of(p * PAIR, PAIR), PAIR)
        rows = rows_ref[0, p]
        raw = raw_ref[part, :].astype(jnp.float32)
        before = jnp.where(first, 0.0, before_ref[part, :].astype(jnp.float32))
        taps = shifted_taps(raw, before, masks)
        pre = conv_sum(taps, conv_ref, part)
        gate = sigmoid(pre)
        value = pre * gate
        step_wide = pair_wide(rows, 2)
        skip_wide = pair_wide(rows, 10)
        keep_wide = pair_wide(rows, 4)
        scaled = value * step_wide
        low = scaled.astype(bf16)
        dmix_low = dmix_ref[part, :]
        dmix = dmix_low.astype(jnp.float32)
        halves = jnp.concatenate(
            [jnp.where(head_row, dmix, 0.0).astype(bf16), jnp.where(head_row, 0.0, dmix).astype(bf16)],
            axis=1,
        )
        dmixing = mxu(low, halves, TN)
        dnear = []
        for h in range(2):
            decay = decay_block(rows, h)
            mixing = (decay * affinity).astype(bf16)
            daffinity = daffinity + dmixing[:, h * CHUNK : (h + 1) * CHUNK] * decay
            dnear.append(mxu(dmix_low[h * HEAD_DIM : (h + 1) * HEAD_DIM], mixing, NT))
        dnear = jnp.concatenate(dnear, axis=0)
        held_low = entry_ref[0, part, :]
        dheld = dheld_ref[part, :]
        dheld_low = dheld.astype(bf16)
        carried = dheld * pair_wide(rows, 8)
        dfar = mxu(dheld_low, intot) * keep_wide
        kept = (scaled * keep_wide).astype(bf16)
        read = (dmix * pair_wide(rows, 6)).astype(bf16)
        dfar_ref[:, :STATE] += mxu(kept, dheld_low, TN)
        dfar_ref[:, STATE:] += mxu(read, held_low, TN)
        dheld_ref[part, :] = carried + mxu(read, out)
        dscaled = dnear + dfar
        scaled_low = low.astype(jnp.float32)
        far_product = scaled * dfar
        running = (
            dmix * (mixed_ref[part, :] - skip_wide * value) - scaled_low * dnear - far_product
        )
        products = (
            running, far_product, carried * held_low.astype(jnp.float32), dscaled * value,
            dmix * value,
        )
        for q, product in enumerate(products):
            for h in range(2):
                drows_ref[0, p, 2 * q + h : 2 * q + h + 1, :] = jnp.sum(
                    product[h * HEAD_DIM : (h + 1) * HEAD_DIM], axis=0, keepdims=True
                )
        dvalue = dscaled * step_wide + skip_wide * dmix
        dpre = dvalue * (gate * (1.0 + pre * (1.0 - gate)))
        later = later_ref[part, :]
        dconv_ref[KERNEL, part, :] += dpre
        dconv_ref[KERNEL - 1, part, :] += dpre * raw
        draw = conv_ref[KERNEL - 1, part, :] * dpre
        for k in range(1, KERNEL):
            dconv_ref[KERNEL - 1 - k, part, :] += dpre * taps[k]
            joined = jnp.where(
                lane < k, later * later_masks[k - 1 : k], dpre * masks[k - 1 : k]
            )
            draw = draw + conv_ref[KERNEL - 1 - k, part, :] * pltpu.roll(joined, CHUNK - k, 1)
        later_ref[part, :] = dpre
        draw_ref[part, :] = draw.astype(bf16)
        return daffinity

    daffinity = lax.fori_loop(
        0, raw_ref.shape[0] // PAIR, body, jnp.zeros((CHUNK, CHUNK), jnp.float32)
    )
    daffinity = (daffinity * allowed).astype(bf16)
    dstate_ref[:, :STATE] = dfar_ref[:, :STATE] + mxu(daffinity, out)
    dstate_ref[:, STATE:] = dfar_ref[:, STATE:] + mxu(daffinity, into, TN)
    latermask_ref[...] = masks


def spec(block, index):
    return pl.BlockSpec(block, index)


def mix_forward(seqs, raw, gate, dout, rows, masks, into, outt, conv, gain):
    ch, tokens = raw.shape
    chunks = tokens // seqs // CHUNK
    at = lambda s, c: (0, s * chunks + c)
    up = lambda s, c: (s * chunks + c, 0)
    slab = spec((ch, CHUNK), at)
    return pl.pallas_call(
        mix_kernel,
        grid=(seqs, chunks),
        in_specs=[
            slab, slab, slab,
            spec((1,) + rows.shape[1:], lambda s, c: (s * chunks + c, 0, 0, 0)),
            spec((1, 8, CHUNK), lambda s, c: (s * chunks + c, 0, 0)),
            spec((CHUNK, STATE), up),
            spec((STATE, CHUNK), at),
            spec(conv.shape, lambda s, c: (0, 0, 0)),
            spec((ch, CHUNK), lambda s, c: (0, 0)),
        ],
        out_specs=[
            slab,
            spec((1, ch, STATE), lambda s, c: (s * chunks + c, 0, 0)),
            spec((1, 8, CHUNK), lambda s, c: (s * chunks + c, 0, 0)),
        ],
        out_shape=[
            jax.ShapeDtypeStruct((ch, tokens), jnp.float32),
            jax.ShapeDtypeStruct((seqs * chunks, ch, STATE), bf16),
            jax.ShapeDtypeStruct((seqs * chunks, 8, CHUNK), jnp.float32),
        ],
        scratch_shapes=[
            pltpu.VMEM((ch, STATE), jnp.float32),
            pltpu.VMEM((ch, CHUNK), jnp.float32),
        ],
        compiler_params=pltpu.CompilerParams(vmem_limit_bytes=VMEM_BYTES),
        cost_estimate=pl.CostEstimate(
            flops=tokens * ch * 1024, bytes_accessed=tokens * ch * 18, transcendentals=tokens * ch * 4
        ),
        name="mix_forward",
    )(raw, gate, dout, rows, masks, into, outt, conv, gain)


def mix_backward(seqs, raw, mixed, dmix, entry, rows, masks, into, intot, out, outt, conv):
    ch, tokens = raw.shape
    chunks = tokens // seqs // CHUNK
    place = lambda s, c: s * chunks + chunks - 1 - c
    at = lambda s, c: (0, place(s, c))
    up = lambda s, c: (place(s, c), 0)
    slab = spec((ch, CHUNK), at)
    row_spec = spec((1,) + rows.shape[1:], lambda s, c: (place(s, c), 0, 0, 0))
    return pl.pallas_call(
        back_kernel,
        grid=(seqs, chunks),
        in_specs=[
            slab,
            spec((ch, CHUNK), lambda s, c: (0, jnp.maximum(place(s, c) - 1, 0))),
            slab, slab,
            spec((1, ch, STATE), lambda s, c: (place(s, c), 0, 0)),
            row_spec,
            spec((1, 8, CHUNK), lambda s, c: (place(s, c), 0, 0)),
            spec((CHUNK, STATE), up),
            spec((STATE, CHUNK), at),
            spec((CHUNK, STATE), up),
            spec((STATE, CHUNK), at),
            spec(conv.shape, lambda s, c: (0, 0, 0)),
        ],
        out_specs=[
            slab,
            row_spec,
            spec((CHUNK, 2 * STATE), up),
            spec(conv.shape, lambda s, c: (0, 0, 0)),
        ],
        out_shape=[
            jax.ShapeDtypeStruct((ch, tokens), bf16),
            jax.ShapeDtypeStruct(rows.shape, jnp.float32),
            jax.ShapeDtypeStruct((tokens, 2 * STATE), jnp.float32),
            jax.ShapeDtypeStruct(conv.shape, jnp.float32),
        ],
        scratch_shapes=[
            pltpu.VMEM((ch, STATE), jnp.float32),
            pltpu.VMEM((ch, CHUNK), jnp.float32),
            pltpu.VMEM((8, CHUNK), jnp.float32),
            pltpu.VMEM((CHUNK, 2 * STATE), jnp.float32),
        ],
        compiler_params=pltpu.CompilerParams(vmem_limit_bytes=VMEM_BYTES),
        cost_estimate=pl.CostEstimate(
            flops=tokens * ch * 2048, bytes_accessed=tokens * ch * 16, transcendentals=tokens * ch * 4
        ),
        name="mix_backward",
    )(raw, raw, mixed, dmix, entry, rows, masks, into, intot, out, outt, conv)


def wide_lanes(columns):
    return jnp.broadcast_to(columns[..., None], columns.shape + (CHUNK,))


def pair_rows(parts, seqs):
    heads, _, chunks, _ = parts[0].shape
    stacked = jnp.stack(parts + [jnp.zeros_like(parts[0])] * (8 - len(parts)))
    stacked = stacked.reshape(8, heads // 2, 2, seqs * chunks, CHUNK)
    return stacked.transpose(3, 1, 0, 2, 4).reshape(seqs * chunks, heads // 2, 16, CHUNK)


def unpair_rows(rows, q, seqs):
    steps, pairs = rows.shape[:2]
    part = rows[:, :, 2 * q : 2 * q + 2, :].transpose(1, 2, 0, 3)
    return part.reshape(2 * pairs, seqs, steps // seqs, CHUNK)


def step_rows(step_raw, step_bias, decay_log, skip_gain, segment_ids):
    seqs, length = segment_ids.shape
    chunks = length // CHUNK
    heads = step_raw.shape[0]
    rate = -jnp.exp(decay_log)
    size = jax.nn.softplus(step_raw + step_bias[:, None]).reshape(heads, seqs, chunks, CHUNK)
    places = jnp.arange(CHUNK)
    upper = (places[:, None] <= places[None, :]).astype(jnp.float32)
    running = jnp.einsum(
        "hqcs,st->hqct", size * rate[:, None, None, None], upper, precision=precise
    )
    segments = segment_ids.reshape(seqs, chunks, CHUNK)
    last = segments[:, :, -1]
    before = jnp.concatenate([jnp.full((seqs, 1), -1, jnp.int32), last[:, :-1]], axis=1)
    total = running[..., -1:]
    at_end = (segments == last[..., None]).astype(jnp.float32)
    from_start = (segments == before[..., None]).astype(jnp.float32)
    through = (last == before).astype(jnp.float32)[..., None]
    full = jnp.ones_like(running)
    parts = [
        running * LOG2E,
        size,
        jnp.exp(total - running) * at_end,
        jnp.exp(running) * from_start,
        jnp.exp(total) * through * full,
        skip_gain[:, None, None, None] * full,
    ]
    lags = [jnp.stack(lag_masks(row)[1:]) for row in segment_ids]
    lags = jnp.stack(lags).reshape(seqs, KERNEL - 1, chunks, CHUNK).transpose(0, 2, 1, 3)
    masks = jnp.concatenate(
        [
            lags,
            segments[:, :, None, :].astype(jnp.float32),
            jnp.zeros((seqs, chunks, 4, CHUNK), jnp.float32),
        ],
        axis=2,
    ).reshape(seqs * chunks, 8, CHUNK)
    return pair_rows(parts, seqs), masks


def step_grads(drows, step_raw, step_bias, decay_log, seqs):
    heads, tokens = step_raw.shape
    running, far, carried, direct, skip = [unpair_rows(drows, q, seqs) for q in range(5)]
    rate = -jnp.exp(decay_log)[:, None, None, None]
    biased = step_raw + step_bias[:, None]
    size = jax.nn.softplus(biased).reshape(running.shape)
    total = jnp.sum(far + carried, axis=-1, keepdims=True)
    places = jnp.arange(CHUNK)
    lower = (places[:, None] >= places[None, :]).astype(jnp.float32)
    ddrop = jnp.einsum("hqct,ts->hqcs", running, lower, precision=precise) + total
    dsize = direct + ddrop * rate
    draw = dsize.reshape(heads, tokens) * jax.nn.sigmoid(biased)
    every = (1, 2, 3)
    return (
        draw,
        jnp.sum(draw, axis=1),
        jnp.sum(ddrop * size * rate, axis=every),
        jnp.sum(skip, axis=every),
    )


def finish_kernel(
    part_ref, other_ref, branch_ref, received_ref, hidden_ref, cotangent_ref, gain_ref, *rest
):
    out_ref, grad_ref = rest[-2:]
    wide = hidden_ref[0].astype(jnp.float32)
    width = wide.shape[1]
    row_scale = lax.rsqrt(jnp.mean(wide * wide, axis=-1, keepdims=True) + epsilon)
    scaled = (part_ref[...] + other_ref[...]) * gain_ref[...]
    inner = jnp.sum(scaled * wide, axis=-1, keepdims=True)
    grad_ref[0] = (
        cotangent_ref[0].astype(jnp.float32)
        + row_scale * scaled
        - wide * (row_scale * row_scale * row_scale * inner / width)
    )
    out_ref[0] = (wide + (branch_ref[...] + received_ref[...])).astype(bf16)


def finish(s, part, other, branch, received, hidden, out_grad, norm_gain, earlier):
    seqs, length, width = hidden.shape
    tile = 256
    flat = spec((tile, width), lambda i: (i, 0))
    deep = spec((1, tile, width), lambda i: (s, i, 0))
    held = [pl.BlockSpec(memory_space=pl.ANY)] * len(earlier)
    return pl.pallas_call(
        finish_kernel,
        grid=(length // tile,),
        in_specs=[flat] * 4 + [deep, deep, spec((1, width), lambda i: (0, 0))] + held,
        out_specs=[deep, deep],
        out_shape=[
            jax.ShapeDtypeStruct((seqs, length, width), bf16),
            jax.ShapeDtypeStruct((seqs, length, width), jnp.float32),
        ],
        input_output_aliases={7 + i: i for i in range(len(earlier))},
        compiler_params=pltpu.CompilerParams(vmem_limit_bytes=VMEM_BYTES),
        cost_estimate=pl.CostEstimate(
            flops=length * width * 20, bytes_accessed=length * width * 26, transcendentals=0
        ),
        name="finish",
    )(part, other, branch, received, hidden, out_grad, norm_gain[None, :], *earlier)


def out_product(left, weight):
    return lax.dot_general(left, weight, (((0,), (1,)), ((), ())), preferred_element_type=jnp.float32)


def in_product(weight, tokens):
    return lax.dot_general(weight, tokens, (((0,), (1,)), ((), ())), preferred_element_type=jnp.float32)


def grad_product(tokens, channels):
    return lax.dot_general(
        tokens, channels, (((0,), (1,)), ((), ())), preferred_element_type=jnp.float32
    )


def right_product(left, weight):
    return lax.dot_general(
        left, weight, (((1,), (1,)), ((), ())), preferred_element_type=jnp.float32
    )


def token_product(left, right):
    return lax.dot_general(
        left, right, (((0,), (0,)), ((), ())), preferred_element_type=jnp.float32
    )


def tensor_others(part):
    count = lax.axis_size("tensor")
    if count == 2:
        return lax.ppermute(part, "tensor", [(0, 1), (1, 0)])
    return lax.psum(part, "tensor")


def tensor_join(part, others):
    return part + others if lax.axis_size("tensor") == 2 else others


def only_others(part, others):
    return others if lax.axis_size("tensor") == 2 else others - part


def after(value, *earlier):
    return lax.optimization_barrier((value, *earlier))[0]


def assemble_kernel(quarter_ref, first_ref, second_ref, third_ref, fourth_ref, whole_ref):
    rows = first_ref.shape[0]
    pieces = (first_ref, second_ref, third_ref, fourth_ref)
    for piece_ref, flip in zip(pieces, (0, 2, 1, 3)):
        place = jnp.bitwise_xor(quarter_ref[0], flip)
        part = pl.ds(pl.multiple_of(place * rows, rows), rows)
        whole_ref[part, :] = piece_ref[...].astype(whole_ref.dtype)


def gather_first(weight):
    rows, columns = weight.shape[0] // 4, weight.shape[1]
    quarter = lax.rem(lax.axis_index("dp"), 4)
    mine = lax.dynamic_slice(weight, (quarter * rows, 0), (rows, columns))
    mine = lax.optimization_barrier(mine.astype(jnp.float32))
    return lax.ppermute(mine, "tensor", [(0, 1), (1, 0)])


def along_dp(piece, flip):
    return lax.ppermute(piece, "dp", [(j, j ^ flip) for j in range(lax.axis_size("dp"))])


def assemble(weight, *pieces):
    quarter = lax.rem(lax.axis_index("dp"), 4)
    return pl.pallas_call(
        assemble_kernel,
        in_specs=[pl.BlockSpec(memory_space=pltpu.SMEM)]
        + [pl.BlockSpec(memory_space=pltpu.VMEM)] * 4,
        out_specs=pl.BlockSpec(memory_space=pltpu.VMEM),
        out_shape=jax.ShapeDtypeStruct(weight.shape, weight.dtype),
        compiler_params=pltpu.CompilerParams(vmem_limit_bytes=VMEM_BYTES),
        cost_estimate=pl.CostEstimate(
            flops=weight.size, bytes_accessed=6 * weight.size, transcendentals=0
        ),
        name="assemble",
    )(quarter.reshape(1), *pieces)


def swap_small(arrays):
    flat = jnp.concatenate([a.astype(jnp.float32).reshape(-1) for a in arrays])
    flat = lax.ppermute(lax.optimization_barrier(flat), "tensor", [(0, 1), (1, 0)])
    flat = lax.optimization_barrier(flat)
    result, edge = [], 0
    for a in arrays:
        result.append(flat[edge : edge + a.size].reshape(a.shape).astype(a.dtype))
        edge += a.size
    return result


def unit_forward(weights, normed, cotangent, segments, states):
    step = in_product(weights["step"], normed)
    gate = in_product(weights["gate"], normed)
    raw = in_product(weights["value"], normed)
    dout = in_product(weights["out"], cotangent)
    rows, masks = step_rows(
        step, weights["step_bias"], weights["decay_log"], weights["skip_gain"], segments
    )
    into, _, _, outt = states
    mixed, entry, sums = mix_forward(
        1, raw, gate, dout, rows, masks, into, outt, weights["conv"], weights["gain_wide"]
    )
    sums = sums[:, :2].transpose(1, 0, 2).reshape(2, normed.shape[0])
    return dict(
        step=step, gate=gate, raw=raw, dout=dout, rows=rows, masks=masks, mixed=mixed,
        entry=entry, sums=sums, states=states,
    )


def unit_middle(unit, weights, both, inner_total):
    gate, mixed, dout = unit["gate"], unit["mixed"], unit["dout"]
    gain = weights["gate_gain"][:, None]
    sigma = sigmoid(gate)
    gated = mixed * gate * sigma
    gated_scale = lax.rsqrt(both[0:1] / inner_total + epsilon)
    output_in = (gated * gated_scale * gain).astype(bf16)
    d_gated = gated_scale * (dout * gain) - gated * (
        gated_scale**3 * both[1:2] / inner_total
    )
    d_mixed = (d_gated * gate * sigma).astype(bf16)
    d_gate = (d_gated * mixed * sigma * (1.0 + gate * (1.0 - sigma))).astype(bf16)
    grad_gain = jnp.sum(dout * gated * gated_scale, axis=1)
    return output_in, d_gate, d_mixed, grad_gain


def unit_backward(unit, weights, d_gate, d_mixed, state_back):
    d_value, d_rows, d_state, d_conv = mix_backward(
        1, unit["raw"], unit["mixed"], d_mixed, unit["entry"], unit["rows"], unit["masks"],
        *unit["states"], weights["conv"],
    )
    d_step, *step_params = step_grads(
        d_rows, unit["step"], weights["step_bias"], weights["decay_log"], 1
    )
    d_state, g_cs, g_csb = state_back(d_state.astype(bf16).astype(jnp.float32))
    d_state, d_step = d_state.astype(bf16), d_step.astype(bf16)
    return d_value, d_state, d_step, (d_conv, g_cs, g_csb, *step_params)


def normed_part(weights, d_gate, d_value, d_state, d_step):
    return (
        out_product(d_gate, weights["gate"])
        + out_product(d_value, weights["value"])
        + right_product(d_state, weights["state"])
        + out_product(d_step, weights["step"])
    )


def local(
    hidden,
    segment_ids,
    norm_gain,
    proj_gate,
    proj_value,
    proj_state,
    proj_step,
    conv_value,
    conv_value_bias,
    conv_state,
    conv_state_bias,
    step_bias,
    decay_log,
    skip_gain,
    gate_gain,
    proj_out,
    out_grad,
):
    seq_count, length, width = hidden.shape
    local_inner = proj_gate.shape[1]
    state_width = proj_state.shape[1]
    tensor_count = lax.axis_size("tensor")
    inner_total = local_inner * tensor_count
    every = range(seq_count)
    whole_from = seq_count
    if tensor_count == 2 and lax.axis_size("dp") % 4 == 0 and seq_count > 1:
        whole_from = seq_count - 1

    own = dict(
        gate=proj_gate, value=proj_value, out=proj_out, state=proj_state, step=proj_step,
        step_bias=step_bias, decay_log=decay_log, skip_gain=skip_gain, gate_gain=gate_gain,
    )
    own["conv"] = wide_lanes(jnp.concatenate([conv_value, conv_value_bias[None, :]], axis=0))
    own["gain_wide"] = wide_lanes(gate_gain)
    if whole_from < seq_count:
        c_w, c_b, step, s_b, d_l, s_g, g_g = swap_small(
            [conv_value, conv_value_bias, proj_step, step_bias, decay_log, skip_gain, gate_gain]
        )
        other = dict(
            state=proj_state, step=step, step_bias=s_b, decay_log=d_l, skip_gain=s_g, gate_gain=g_g
        )
        sent = dict(value=proj_value, gate=proj_gate, out=proj_out)
        first = {k: gather_first(w) for k, w in sent.items()}
        other["conv"] = wide_lanes(jnp.concatenate([c_w, c_b[None, :]], axis=0))
        other["gain_wide"] = wide_lanes(g_g)

    normeds, states, state_backs, units, boths = [], [], [], [], []
    for s in every:
        wide = hidden[s].astype(jnp.float32)
        row_scale = lax.rsqrt(jnp.mean(wide * wide, axis=-1, keepdims=True) + epsilon)
        normeds.append((wide * row_scale * norm_gain[None, :]).astype(bf16))
        state_raw = jnp.dot(normeds[s], proj_state, preferred_element_type=jnp.float32)
        state_conv, back = jax.vjp(
            functools.partial(causal_conv, doc_masks=lag_masks(segment_ids[s])),
            state_raw,
            conv_state,
            conv_state_bias,
        )
        state_backs.append(back)
        low = state_conv.astype(bf16)
        into, out = low[:, :STATE], low[:, STATE:]
        states.append((into, into.T, out, out.T))
        units.append(unit_forward(own, normeds[s], out_grad[s], segment_ids[s : s + 1], states[s]))
        if s < whole_from:
            sums = units[s]["sums"]
            boths.append(tensor_join(sums, tensor_others(sums)))
    branches, received, output_ins, d_gates, d_mixeds = [], [], [], [], []
    grad_gate_gain = jnp.zeros((local_inner,), jnp.float32)
    extras, middles = {}, {}
    if whole_from < seq_count:
        second = {k: along_dp(after(first[k], units[0]["mixed"]), 2) for k in sent}
        third = {k: along_dp(first[k], 1) for k in sent}
        fourth = {k: along_dp(after(second[k], units[-1]["mixed"]), 1) for k in sent}
    for s in every:
        if s == whole_from:
            for k in sent:
                pieces = (first[k], second[k], third[k], fourth[k])
                pieces = lax.optimization_barrier((*pieces, branches[0]))[:4]
                other[k] = assemble(sent[k], *pieces)
        if s >= whole_from:
            extras[s] = unit_forward(
                other, normeds[s], out_grad[s], segment_ids[s : s + 1], states[s]
            )
            boths.append(units[s]["sums"] + extras[s]["sums"])
            middles[s] = unit_middle(extras[s], other, boths[s], inner_total)
        output_in, d_gate, d_mixed, grad_gain = unit_middle(units[s], own, boths[s], inner_total)
        grad_gate_gain = grad_gate_gain + grad_gain
        output_ins.append(output_in)
        d_gates.append(d_gate)
        d_mixeds.append(d_mixed)
        branches.append(lax.optimization_barrier(out_product(output_in, proj_out)))
        if s < whole_from:
            received.append(tensor_others(branches[s]))
        else:
            received.append(lax.optimization_barrier(out_product(middles[s][0], other["out"])))

    normed_all = jnp.concatenate(normeds, axis=0)
    early_part = jnp.stack(
        [
            grad_product(normed_all, jnp.concatenate(d_gates, axis=1)),
            grad_product(
                out_grad.reshape(seq_count * length, width), jnp.concatenate(output_ins, axis=1)
            ),
        ]
    )
    early = lax.psum_scatter(early_part, "dp", scatter_dimension=1, tiled=True)

    backs, parts, others = [], [], []
    waits = (early_part, *branches)
    for s in every:
        back = unit_backward(units[s], own, d_gates[s], after(d_mixeds[s], *waits), state_backs[s])
        backs.append(back)
        parts.append(lax.optimization_barrier(normed_part(own, d_gates[s], *back[:3])))
        if s < whole_from:
            others.append(tensor_others(after(parts[s], received[s])))
            waits = (parts[s],)
    later_part = jnp.concatenate(
        [
            grad_product(normed_all, jnp.concatenate([b[0] for b in backs], axis=1)),
            token_product(normed_all, jnp.concatenate([b[1] for b in backs], axis=0)),
            grad_product(normed_all, jnp.concatenate([b[2] for b in backs], axis=1)),
        ],
        axis=1,
    )
    later_part = after(later_part, early)
    later = lax.psum_scatter(later_part, "dp", scatter_dimension=0, tiled=True)
    later_value = later[:, :local_inner]
    edge = local_inner + state_width
    state_part = later[:, local_inner:edge]
    grad_proj_state = tensor_join(state_part, tensor_others(state_part))
    waits = (later_part,)
    grad_norm_gain = jnp.zeros((width,), jnp.float32)
    for s in every:
        wide = hidden[s].astype(jnp.float32)
        row_scale = lax.rsqrt(jnp.mean(wide * wide, axis=-1, keepdims=True) + epsilon)
        grad_norm_gain = grad_norm_gain + jnp.sum(parts[s] * wide * row_scale, axis=0)
    for s in range(whole_from, seq_count):
        d_gate = middles[s][1]
        back = unit_backward(extras[s], other, d_gate, after(middles[s][2], *waits), state_backs[s])
        others.append(lax.optimization_barrier(normed_part(other, d_gate, *back[:3])))

    stacked = ()
    for s in reversed(every):
        stacked = finish(
            s, parts[s], only_others(parts[s], others[s]), branches[s],
            only_others(branches[s], received[s]), hidden, out_grad, norm_gain, stacked
        )
    param_grads = [sum(grads) for grads in zip(*[b[3] for b in backs])]
    d_conv, g_cs, g_csb, g_sb, g_dl, g_sg = param_grads
    d_conv = jnp.sum(d_conv, axis=-1)
    own_grads = [d_conv[:KERNEL], d_conv[KERNEL], g_sb, g_dl, g_sg, grad_gate_gain]
    shared = [g_cs, g_csb, grad_norm_gain]
    own_flat = jnp.concatenate([g.reshape(-1) for g in own_grads])
    place = lax.axis_index("tensor")
    mine = (jnp.arange(tensor_count) == place)[:, None]
    slots = jnp.where(mine, own_flat[None, :], 0.0).reshape(-1)
    packed = jnp.concatenate([slots] + [g.reshape(-1) for g in shared])
    packed = jnp.pad(packed, (0, -packed.shape[0] % 16384))
    packed = lax.psum(after(packed, later), ("dp", "tensor"))
    own_sum = lax.dynamic_slice(packed, (place * own_flat.shape[0],), (own_flat.shape[0],))
    shared_sum = packed[slots.shape[0] :]

    def split(flat, like):
        result, edge = [], 0
        for g in like:
            result.append(flat[edge : edge + g.size].reshape(g.shape))
            edge += g.size
        return result

    r_cv, r_cvb, r_sb, r_dl, r_sg, r_gg = split(own_sum, own_grads)
    r_cs, r_csb, r_ng = split(shared_sum, shared)
    return (
        *stacked,
        r_ng,
        early[0],
        later_value,
        grad_proj_state,
        later[:, edge:],
        r_cv,
        r_cvb,
        r_cs,
        r_csb,
        r_sb,
        r_dl,
        r_sg,
        r_gg,
        early[1],
    )


def solution(mesh):
    in_specs = (
        P("dp", None, None),
        P("dp", None),
        P(),
        P(None, "tensor"),
        P(None, "tensor"),
        P(),
        P(None, "tensor"),
        P(None, "tensor"),
        P("tensor"),
        P(),
        P(),
        P("tensor"),
        P("tensor"),
        P("tensor"),
        P("tensor"),
        P(None, "tensor"),
        P("dp", None, None),
    )
    out_specs = (
        P("dp", None, None),
        P("dp", None, None),
        P(),
        P("dp", "tensor"),
        P("dp", "tensor"),
        P("dp", None),
        P("dp", "tensor"),
        P(None, "tensor"),
        P("tensor"),
        P(),
        P(),
        P("tensor"),
        P("tensor"),
        P("tensor"),
        P("tensor"),
        P("dp", "tensor"),
    )
    return jax.shard_map(local, mesh=mesh, in_specs=in_specs, out_specs=out_specs, check_vma=False)
```

```python
import functools

import jax
import jax.numpy as jnp
from jax import lax
from jax.experimental import pallas as pl
from jax.experimental.pallas import tpu as pltpu
from jax.sharding import PartitionSpec as P

HEAD_DIM = 64
STATE = 128
KERNEL = 4
VMEM_BYTES = 50 * 1024 * 1024

epsilon = 1e-05
precise = lax.Precision.HIGHEST


def lag_masks(segment_row):
    length = segment_row.shape[0]
    result = [jnp.ones((length,), jnp.float32)]
    for delay in range(1, KERNEL):
        earlier = jnp.concatenate(
            [jnp.full((delay,), -1, jnp.int32), segment_row[: length - delay]]
        )
        result.append((earlier == segment_row).astype(jnp.float32))
    return result


def causal_conv(values, weight, conv_bias, doc_masks):
    length = values.shape[0]
    summed = conv_bias[None, :] + weight[KERNEL - 1][None, :] * values
    for delay in range(1, KERNEL):
        earlier = jnp.concatenate(
            [jnp.zeros((delay, values.shape[1]), jnp.float32), values[: length - delay]], axis=0
        )
        summed = summed + weight[KERNEL - 1 - delay][None, :] * earlier * doc_masks[delay][:, None]
    return jax.nn.silu(summed)


CHUNK = 128
PAIR = 2 * HEAD_DIM
LOG2E = 1.4426950408889634
NN = (((1,), (0,)), ((), ()))
NT = (((1,), (1,)), ((), ()))
TN = (((0,), (0,)), ((), ()))
bf16 = jnp.bfloat16


def mxu(a, b, dims=NN):
    return lax.dot_general(a, b, dims, preferred_element_type=jnp.float32)


def sigmoid(z):
    return 0.5 * jnp.tanh(0.5 * z) + 0.5


def pair_wide(rows, at):
    top = jnp.broadcast_to(rows[at : at + 1], (HEAD_DIM, CHUNK))
    low = jnp.broadcast_to(rows[at + 1 : at + 2], (HEAD_DIM, CHUNK))
    return jnp.concatenate([top, low], axis=0)


def decay_block(rows, h):
    run = jnp.broadcast_to(rows[h : h + 1], (CHUNK, CHUNK))
    return jnp.exp2(jnp.minimum(run - run.T, 0.0))


def doc_block(masks):
    segment = jnp.broadcast_to(masks[3:4], (CHUNK, CHUNK))
    source = lax.broadcasted_iota(jnp.int32, (CHUNK, CHUNK), 0)
    target = lax.broadcasted_iota(jnp.int32, (CHUNK, CHUNK), 1)
    return ((segment == segment.T) & (source <= target)).astype(jnp.float32)


def shifted_taps(raw, before, masks):
    lane = lax.broadcasted_iota(jnp.int32, raw.shape, 1)
    taps = [raw]
    for k in range(1, KERNEL):
        moved = pltpu.roll(jnp.where(lane >= CHUNK - k, before, raw), k, 1)
        taps.append(moved * masks[k - 1 : k])
    return taps


def conv_sum(taps, conv_ref, part):
    total = conv_ref[KERNEL, part, :]
    for k in range(KERNEL):
        total = total + conv_ref[KERNEL - 1 - k, part, :] * taps[k]
    return total


def mix_kernel(
    raw_ref, gate_ref, dout_ref, rows_ref, mask_ref, into_ref, outt_ref, conv_ref, gain_ref,
    mixed_ref, entry_ref, sums_ref, held_ref, before_ref,
):
    @pl.when(pl.program_id(1) == 0)
    def _():
        held_ref[...] = jnp.zeros_like(held_ref)
        before_ref[...] = jnp.zeros_like(before_ref)

    masks = mask_ref[0]
    into, outt = into_ref[...], outt_ref[...]
    affinity = mxu(into, outt) * doc_block(masks)

    def body(p, sums):
        part = pl.ds(pl.multiple_of(p * PAIR, PAIR), PAIR)
        rows = rows_ref[0, p]
        raw = raw_ref[part, :].astype(jnp.float32)
        pre = conv_sum(shifted_taps(raw, before_ref[part, :], masks), conv_ref, part)
        value = pre * sigmoid(pre)
        scaled = value * pair_wide(rows, 2)
        low = scaled.astype(bf16)
        near = []
        for h in range(2):
            mixing = (decay_block(rows, h) * affinity).astype(bf16)
            near.append(mxu(low[h * HEAD_DIM : (h + 1) * HEAD_DIM], mixing))
        held = held_ref[part, :]
        held_low = held.astype(bf16)
        entry_ref[0, part, :] = held_low
        far = mxu(held_low, outt) * pair_wide(rows, 6)
        kept = (scaled * pair_wide(rows, 4)).astype(bf16)
        held_ref[part, :] = held * pair_wide(rows, 8) + mxu(kept, into)
        mixed = jnp.concatenate(near, axis=0) + far + pair_wide(rows, 10) * value
        mixed_ref[part, :] = mixed
        before_ref[part, :] = raw
        gate = gate_ref[part, :].astype(jnp.float32)
        gated = mixed * gate * sigmoid(gate)
        square = jnp.sum(gated * gated, axis=0, keepdims=True)
        inner = dout_ref[part, :].astype(jnp.float32) * gain_ref[part, :] * gated
        return sums[0] + square, sums[1] + jnp.sum(inner, axis=0, keepdims=True)

    zero = jnp.zeros((1, CHUNK), jnp.float32)
    pairs = raw_ref.shape[0] // PAIR
    square, inner = lax.fori_loop(0, pairs, body, (zero, zero), unroll=min(8, pairs))
    sums_ref[0, 0:1, :] = square
    sums_ref[0, 1:2, :] = inner


def back_kernel(
    raw_ref, before_ref, mixed_ref, dmix_ref, entry_ref, rows_ref, mask_ref, into_ref, intot_ref,
    out_ref, outt_ref, conv_ref,
    draw_ref, drows_ref, dstate_ref, dconv_ref, dheld_ref, later_ref, latermask_ref, dfar_ref,
):
    step = pl.program_id(1)

    @pl.when((pl.program_id(0) == 0) & (step == 0))
    def _():
        dconv_ref[...] = jnp.zeros_like(dconv_ref)

    @pl.when(step == 0)
    def _():
        dheld_ref[...] = jnp.zeros_like(dheld_ref)
        later_ref[...] = jnp.zeros_like(later_ref)
        latermask_ref[...] = jnp.zeros_like(latermask_ref)

    first = step == pl.num_programs(1) - 1
    masks, later_masks = mask_ref[0], latermask_ref[...]
    into, intot, out, outt = into_ref[...], intot_ref[...], out_ref[...], outt_ref[...]
    allowed = doc_block(masks)
    affinity = mxu(into, outt) * allowed
    dfar_ref[...] = jnp.zeros_like(dfar_ref)
    lane = lax.broadcasted_iota(jnp.int32, (PAIR, CHUNK), 1)
    head_row = lax.broadcasted_iota(jnp.int32, (PAIR, CHUNK), 0) < HEAD_DIM

    def body(p, daffinity):
        part = pl.ds(pl.multiple_of(p * PAIR, PAIR), PAIR)
        rows = rows_ref[0, p]
        raw = raw_ref[part, :].astype(jnp.float32)
        before = jnp.where(first, 0.0, before_ref[part, :].astype(jnp.float32))
        taps = shifted_taps(raw, before, masks)
        pre = conv_sum(taps, conv_ref, part)
        gate = sigmoid(pre)
        value = pre * gate
        step_wide = pair_wide(rows, 2)
        skip_wide = pair_wide(rows, 10)
        keep_wide = pair_wide(rows, 4)
        scaled = value * step_wide
        low = scaled.astype(bf16)
        dmix_low = dmix_ref[part, :]
        dmix = dmix_low.astype(jnp.float32)
        halves = jnp.concatenate(
            [jnp.where(head_row, dmix, 0.0).astype(bf16), jnp.where(head_row, 0.0, dmix).astype(bf16)],
            axis=1,
        )
        dmixing = mxu(low, halves, TN)
        dnear = []
        for h in range(2):
            decay = decay_block(rows, h)
            mixing = (decay * affinity).astype(bf16)
            daffinity = daffinity + dmixing[:, h * CHUNK : (h + 1) * CHUNK] * decay
            dnear.append(mxu(dmix_low[h * HEAD_DIM : (h + 1) * HEAD_DIM], mixing, NT))
        dnear = jnp.concatenate(dnear, axis=0)
        held_low = entry_ref[0, part, :]
        dheld = dheld_ref[part, :]
        dheld_low = dheld.astype(bf16)
        carried = dheld * pair_wide(rows, 8)
        dfar = mxu(dheld_low, intot) * keep_wide
        kept = (scaled * keep_wide).astype(bf16)
        read = (dmix * pair_wide(rows, 6)).astype(bf16)
        dfar_ref[:, :STATE] += mxu(kept, dheld_low, TN)
        dfar_ref[:, STATE:] += mxu(read, held_low, TN)
        dheld_ref[part, :] = carried + mxu(read, out)
        dscaled = dnear + dfar
        scaled_low = low.astype(jnp.float32)
        far_product = scaled * dfar
        running = (
            dmix * (mixed_ref[part, :] - skip_wide * value) - scaled_low * dnear - far_product
        )
        products = (
            running, far_product, carried * held_low.astype(jnp.float32), dscaled * value,
            dmix * value,
        )
        for q, product in enumerate(products):
            for h in range(2):
                drows_ref[0, p, 2 * q + h : 2 * q + h + 1, :] = jnp.sum(
                    product[h * HEAD_DIM : (h + 1) * HEAD_DIM], axis=0, keepdims=True
                )
        dvalue = dscaled * step_wide + skip_wide * dmix
        dpre = dvalue * (gate * (1.0 + pre * (1.0 - gate)))
        later = later_ref[part, :]
        dconv_ref[KERNEL, part, :] += dpre
        dconv_ref[KERNEL - 1, part, :] += dpre * raw
        draw = conv_ref[KERNEL - 1, part, :] * dpre
        for k in range(1, KERNEL):
            dconv_ref[KERNEL - 1 - k, part, :] += dpre * taps[k]
            joined = jnp.where(
                lane < k, later * later_masks[k - 1 : k], dpre * masks[k - 1 : k]
            )
            draw = draw + conv_ref[KERNEL - 1 - k, part, :] * pltpu.roll(joined, CHUNK - k, 1)
        later_ref[part, :] = dpre
        draw_ref[part, :] = draw.astype(bf16)
        return daffinity

    zero = jnp.zeros((CHUNK, CHUNK), jnp.float32)
    daffinity = lax.fori_loop(0, raw_ref.shape[0] // PAIR, body, zero, unroll=2)
    daffinity = (daffinity * allowed).astype(bf16)
    dstate_ref[:, :STATE] = dfar_ref[:, :STATE] + mxu(daffinity, out)
    dstate_ref[:, STATE:] = dfar_ref[:, STATE:] + mxu(daffinity, into, TN)
    latermask_ref[...] = masks


def spec(block, index):
    return pl.BlockSpec(block, index)


def mix_forward(seqs, raw, gate, dout, rows, masks, into, outt, conv, gain):
    ch, tokens = raw.shape
    chunks = tokens // seqs // CHUNK
    at = lambda s, c: (0, s * chunks + c)
    up = lambda s, c: (s * chunks + c, 0)
    slab = spec((ch, CHUNK), at)
    return pl.pallas_call(
        mix_kernel,
        grid=(seqs, chunks),
        in_specs=[
            slab, slab, slab,
            spec((1,) + rows.shape[1:], lambda s, c: (s * chunks + c, 0, 0, 0)),
            spec((1, 8, CHUNK), lambda s, c: (s * chunks + c, 0, 0)),
            spec((CHUNK, STATE), up),
            spec((STATE, CHUNK), at),
            spec(conv.shape, lambda s, c: (0, 0, 0)),
            spec((ch, CHUNK), lambda s, c: (0, 0)),
        ],
        out_specs=[
            slab,
            spec((1, ch, STATE), lambda s, c: (s * chunks + c, 0, 0)),
            spec((1, 8, CHUNK), lambda s, c: (s * chunks + c, 0, 0)),
        ],
        out_shape=[
            jax.ShapeDtypeStruct((ch, tokens), jnp.float32),
            jax.ShapeDtypeStruct((seqs * chunks, ch, STATE), bf16),
            jax.ShapeDtypeStruct((seqs * chunks, 8, CHUNK), jnp.float32),
        ],
        scratch_shapes=[
            pltpu.VMEM((ch, STATE), jnp.float32),
            pltpu.VMEM((ch, CHUNK), jnp.float32),
        ],
        compiler_params=pltpu.CompilerParams(vmem_limit_bytes=VMEM_BYTES),
        cost_estimate=pl.CostEstimate(
            flops=tokens * ch * 1024, bytes_accessed=tokens * ch * 18, transcendentals=tokens * ch * 4
        ),
        name="mix_forward",
    )(raw, gate, dout, rows, masks, into, outt, conv, gain)


def mix_backward(seqs, raw, mixed, dmix, entry, rows, masks, into, intot, out, outt, conv):
    ch, tokens = raw.shape
    chunks = tokens // seqs // CHUNK
    place = lambda s, c: s * chunks + chunks - 1 - c
    at = lambda s, c: (0, place(s, c))
    up = lambda s, c: (place(s, c), 0)
    slab = spec((ch, CHUNK), at)
    row_spec = spec((1,) + rows.shape[1:], lambda s, c: (place(s, c), 0, 0, 0))
    return pl.pallas_call(
        back_kernel,
        grid=(seqs, chunks),
        in_specs=[
            slab,
            spec((ch, CHUNK), lambda s, c: (0, jnp.maximum(place(s, c) - 1, 0))),
            slab, slab,
            spec((1, ch, STATE), lambda s, c: (place(s, c), 0, 0)),
            row_spec,
            spec((1, 8, CHUNK), lambda s, c: (place(s, c), 0, 0)),
            spec((CHUNK, STATE), up),
            spec((STATE, CHUNK), at),
            spec((CHUNK, STATE), up),
            spec((STATE, CHUNK), at),
            spec(conv.shape, lambda s, c: (0, 0, 0)),
        ],
        out_specs=[
            slab,
            row_spec,
            spec((CHUNK, 2 * STATE), up),
            spec(conv.shape, lambda s, c: (0, 0, 0)),
        ],
        out_shape=[
            jax.ShapeDtypeStruct((ch, tokens), bf16),
            jax.ShapeDtypeStruct(rows.shape, jnp.float32),
            jax.ShapeDtypeStruct((tokens, 2 * STATE), jnp.float32),
            jax.ShapeDtypeStruct(conv.shape, jnp.float32),
        ],
        scratch_shapes=[
            pltpu.VMEM((ch, STATE), jnp.float32),
            pltpu.VMEM((ch, CHUNK), jnp.float32),
            pltpu.VMEM((8, CHUNK), jnp.float32),
            pltpu.VMEM((CHUNK, 2 * STATE), jnp.float32),
        ],
        compiler_params=pltpu.CompilerParams(vmem_limit_bytes=VMEM_BYTES),
        cost_estimate=pl.CostEstimate(
            flops=tokens, bytes_accessed=tokens, transcendentals=0
        ),
        name="mix_backward",
    )(raw, raw, mixed, dmix, entry, rows, masks, into, intot, out, outt, conv)


def wide_lanes(columns):
    return jnp.broadcast_to(columns[..., None], columns.shape + (CHUNK,))


def pair_rows(parts, seqs):
    heads, _, chunks, _ = parts[0].shape
    stacked = jnp.stack(parts + [jnp.zeros_like(parts[0])] * (8 - len(parts)))
    stacked = stacked.reshape(8, heads // 2, 2, seqs * chunks, CHUNK)
    return stacked.transpose(3, 1, 0, 2, 4).reshape(seqs * chunks, heads // 2, 16, CHUNK)


def unpair_rows(rows, q, seqs):
    steps, pairs = rows.shape[:2]
    part = rows[:, :, 2 * q : 2 * q + 2, :].transpose(1, 2, 0, 3)
    return part.reshape(2 * pairs, seqs, steps // seqs, CHUNK)


def step_rows(step_raw, step_bias, decay_log, skip_gain, segment_ids):
    seqs, length = segment_ids.shape
    chunks = length // CHUNK
    heads = step_raw.shape[0]
    rate = -jnp.exp(decay_log)
    size = jax.nn.softplus(step_raw + step_bias[:, None]).reshape(heads, seqs, chunks, CHUNK)
    places = jnp.arange(CHUNK)
    upper = (places[:, None] <= places[None, :]).astype(jnp.float32)
    running = jnp.einsum(
        "hqcs,st->hqct", size * rate[:, None, None, None], upper, precision=precise
    )
    segments = segment_ids.reshape(seqs, chunks, CHUNK)
    last = segments[:, :, -1]
    before = jnp.concatenate([jnp.full((seqs, 1), -1, jnp.int32), last[:, :-1]], axis=1)
    total = running[..., -1:]
    at_end = (segments == last[..., None]).astype(jnp.float32)
    from_start = (segments == before[..., None]).astype(jnp.float32)
    through = (last == before).astype(jnp.float32)[..., None]
    full = jnp.ones_like(running)
    parts = [
        running * LOG2E,
        size,
        jnp.exp(total - running) * at_end,
        jnp.exp(running) * from_start,
        jnp.exp(total) * through * full,
        skip_gain[:, None, None, None] * full,
    ]
    lags = [jnp.stack(lag_masks(row)[1:]) for row in segment_ids]
    lags = jnp.stack(lags).reshape(seqs, KERNEL - 1, chunks, CHUNK).transpose(0, 2, 1, 3)
    masks = jnp.concatenate(
        [
            lags,
            segments[:, :, None, :].astype(jnp.float32),
            jnp.zeros((seqs, chunks, 4, CHUNK), jnp.float32),
        ],
        axis=2,
    ).reshape(seqs * chunks, 8, CHUNK)
    return pair_rows(parts, seqs), masks


def step_grads(drows, step_raw, step_bias, decay_log, seqs):
    heads, tokens = step_raw.shape
    running, far, carried, direct, skip = [unpair_rows(drows, q, seqs) for q in range(5)]
    rate = -jnp.exp(decay_log)[:, None, None, None]
    biased = step_raw + step_bias[:, None]
    size = jax.nn.softplus(biased).reshape(running.shape)
    total = jnp.sum(far + carried, axis=-1, keepdims=True)
    places = jnp.arange(CHUNK)
    lower = (places[:, None] >= places[None, :]).astype(jnp.float32)
    ddrop = jnp.einsum("hqct,ts->hqcs", running, lower, precision=precise) + total
    dsize = direct + ddrop * rate
    draw = dsize.reshape(heads, tokens) * jax.nn.sigmoid(biased)
    every = (1, 2, 3)
    return (
        draw,
        jnp.sum(draw, axis=1),
        jnp.sum(ddrop * size * rate, axis=every),
        jnp.sum(skip, axis=every),
    )


def finish_kernel(
    part_ref, other_ref, branch_ref, received_ref, hidden_ref, cotangent_ref, gain_ref, *rest
):
    out_ref, grad_ref = rest[-2:]
    wide = hidden_ref[0].astype(jnp.float32)
    width = wide.shape[1]
    row_scale = lax.rsqrt(jnp.mean(wide * wide, axis=-1, keepdims=True) + epsilon)
    scaled = (part_ref[...] + other_ref[...]) * gain_ref[...]
    inner = jnp.sum(scaled * wide, axis=-1, keepdims=True)
    grad_ref[0] = (
        cotangent_ref[0].astype(jnp.float32)
        + row_scale * scaled
        - wide * (row_scale * row_scale * row_scale * inner / width)
    )
    out_ref[0] = (wide + (branch_ref[...] + received_ref[...])).astype(bf16)


def finish(s, part, other, branch, received, hidden, out_grad, norm_gain, earlier):
    seqs, length, width = hidden.shape
    tile = 256
    flat = spec((tile, width), lambda i: (i, 0))
    deep = spec((1, tile, width), lambda i: (s, i, 0))
    held = [pl.BlockSpec(memory_space=pl.ANY)] * len(earlier)
    return pl.pallas_call(
        finish_kernel,
        grid=(length // tile,),
        in_specs=[flat] * 4 + [deep, deep, spec((1, width), lambda i: (0, 0))] + held,
        out_specs=[deep, deep],
        out_shape=[
            jax.ShapeDtypeStruct((seqs, length, width), bf16),
            jax.ShapeDtypeStruct((seqs, length, width), jnp.float32),
        ],
        input_output_aliases={7 + i: i for i in range(len(earlier))},
        compiler_params=pltpu.CompilerParams(vmem_limit_bytes=VMEM_BYTES),
        cost_estimate=pl.CostEstimate(
            flops=length, bytes_accessed=length, transcendentals=0
        ),
        name="finish",
    )(part, other, branch, received, hidden, out_grad, norm_gain[None, :], *earlier)


def out_product(left, weight):
    return lax.dot_general(left, weight, (((0,), (1,)), ((), ())), preferred_element_type=jnp.float32)


def in_product(weight, tokens):
    return lax.dot_general(weight, tokens, (((0,), (1,)), ((), ())), preferred_element_type=jnp.float32)


def grad_product(tokens, channels):
    return lax.dot_general(
        tokens, channels, (((0,), (1,)), ((), ())), preferred_element_type=jnp.float32
    )


def right_product(left, weight):
    return lax.dot_general(
        left, weight, (((1,), (1,)), ((), ())), preferred_element_type=jnp.float32
    )


def token_product(left, right):
    return lax.dot_general(
        left, right, (((0,), (0,)), ((), ())), preferred_element_type=jnp.float32
    )


def tensor_others(part):
    count = lax.axis_size("tensor")
    if count == 2:
        return lax.ppermute(part, "tensor", [(0, 1), (1, 0)])
    return lax.psum(part, "tensor")


def tensor_join(part, others):
    return part + others if lax.axis_size("tensor") == 2 else others


def only_others(part, others):
    return others if lax.axis_size("tensor") == 2 else others - part


def after(value, *earlier):
    return lax.optimization_barrier((value, *earlier))[0]


def assemble_kernel(quarter_ref, first_ref, second_ref, third_ref, fourth_ref, whole_ref):
    rows = first_ref.shape[0]
    pieces = (first_ref, second_ref, third_ref, fourth_ref)
    for piece_ref, flip in zip(pieces, (0, 2, 1, 3)):
        place = jnp.bitwise_xor(quarter_ref[0], flip)
        part = pl.ds(pl.multiple_of(place * rows, rows), rows)
        whole_ref[part, :] = piece_ref[...].astype(whole_ref.dtype)


def gather_first(weight):
    rows, columns = weight.shape[0] // 4, weight.shape[1]
    quarter = lax.rem(lax.axis_index("dp"), 4)
    mine = lax.dynamic_slice(weight, (quarter * rows, 0), (rows, columns))
    mine = lax.optimization_barrier(mine.astype(jnp.float32))
    return lax.ppermute(mine, "tensor", [(0, 1), (1, 0)])


def along_dp(piece, flip):
    return lax.ppermute(piece, "dp", [(j, j ^ flip) for j in range(lax.axis_size("dp"))])


def assemble(weight, *pieces):
    quarter = lax.rem(lax.axis_index("dp"), 4)
    return pl.pallas_call(
        assemble_kernel,
        in_specs=[pl.BlockSpec(memory_space=pltpu.SMEM)]
        + [pl.BlockSpec(memory_space=pltpu.VMEM)] * 4,
        out_specs=pl.BlockSpec(memory_space=pltpu.VMEM),
        out_shape=jax.ShapeDtypeStruct(weight.shape, weight.dtype),
        compiler_params=pltpu.CompilerParams(vmem_limit_bytes=VMEM_BYTES),
        cost_estimate=pl.CostEstimate(
            flops=weight.size, bytes_accessed=6 * weight.size, transcendentals=0
        ),
        name="assemble",
    )(quarter.reshape(1), *pieces)


def sum_dp(value, *between):
    count = lax.axis_size("dp")
    if count & (count - 1) or not between:
        return lax.psum(value, "dp")
    flip, between = 1, list(between)
    while flip < count:
        arrived = along_dp(value, flip)
        if between:
            arrived = after(arrived, between.pop(0))
        value = value + arrived
        flip *= 2
    return value


def swap_small(arrays):
    flat = jnp.concatenate([a.astype(jnp.float32).reshape(-1) for a in arrays])
    flat = lax.ppermute(lax.optimization_barrier(flat), "tensor", [(0, 1), (1, 0)])
    flat = lax.optimization_barrier(flat)
    result, edge = [], 0
    for a in arrays:
        result.append(flat[edge : edge + a.size].reshape(a.shape).astype(a.dtype))
        edge += a.size
    return result


def unit_forward(weights, normed, cotangent, segments, states):
    step = in_product(weights["step"], normed)
    gate = in_product(weights["gate"], normed)
    raw = in_product(weights["value"], normed)
    dout = in_product(weights["out"], cotangent)
    rows, masks = step_rows(
        step, weights["step_bias"], weights["decay_log"], weights["skip_gain"], segments
    )
    into, _, _, outt = states
    mixed, entry, sums = mix_forward(
        1, raw, gate, dout, rows, masks, into, outt, weights["conv"], weights["gain_wide"]
    )
    sums = sums[:, :2].transpose(1, 0, 2).reshape(2, normed.shape[0])
    return dict(
        step=step, gate=gate, raw=raw, dout=dout, rows=rows, masks=masks, mixed=mixed,
        entry=entry, sums=sums, states=states,
    )


def unit_middle(unit, weights, both, inner_total):
    gate, mixed, dout = unit["gate"], unit["mixed"], unit["dout"]
    gain = weights["gate_gain"][:, None]
    sigma = sigmoid(gate)
    gated = mixed * gate * sigma
    gated_scale = lax.rsqrt(both[0:1] / inner_total + epsilon)
    output_in = (gated * gated_scale * gain).astype(bf16)
    d_gated = gated_scale * (dout * gain) - gated * (
        gated_scale**3 * both[1:2] / inner_total
    )
    d_mixed = (d_gated * gate * sigma).astype(bf16)
    d_gate = (d_gated * mixed * sigma * (1.0 + gate * (1.0 - sigma))).astype(bf16)
    grad_gain = jnp.sum(dout * gated * gated_scale, axis=1)
    return output_in, d_gate, d_mixed, grad_gain


def unit_backward(unit, weights, d_gate, d_mixed, state_back):
    d_value, d_rows, d_state, d_conv = mix_backward(
        1, unit["raw"], unit["mixed"], d_mixed, unit["entry"], unit["rows"], unit["masks"],
        *unit["states"], weights["conv"],
    )
    d_step, *step_params = step_grads(
        d_rows, unit["step"], weights["step_bias"], weights["decay_log"], 1
    )
    d_state, g_cs, g_csb = state_back(d_state.astype(bf16).astype(jnp.float32))
    d_state, d_step = d_state.astype(bf16), d_step.astype(bf16)
    return d_value, d_state, d_step, (d_conv, g_cs, g_csb, *step_params)


def normed_part(weights, d_gate, d_value, d_state, d_step):
    return (
        out_product(d_gate, weights["gate"])
        + out_product(d_value, weights["value"])
        + right_product(d_state, weights["state"])
        + out_product(d_step, weights["step"])
    )


def local(
    hidden,
    segment_ids,
    norm_gain,
    proj_gate,
    proj_value,
    proj_state,
    proj_step,
    conv_value,
    conv_value_bias,
    conv_state,
    conv_state_bias,
    step_bias,
    decay_log,
    skip_gain,
    gate_gain,
    proj_out,
    out_grad,
):
    seq_count, length, width = hidden.shape
    local_inner = proj_gate.shape[1]
    state_width = proj_state.shape[1]
    tensor_count = lax.axis_size("tensor")
    inner_total = local_inner * tensor_count
    every = range(seq_count)
    whole_from = seq_count
    if tensor_count == 2 and lax.axis_size("dp") % 4 == 0 and seq_count > 1:
        whole_from = seq_count - 1

    own = dict(
        gate=proj_gate, value=proj_value, out=proj_out, state=proj_state, step=proj_step,
        step_bias=step_bias, decay_log=decay_log, skip_gain=skip_gain, gate_gain=gate_gain,
    )
    own["conv"] = wide_lanes(jnp.concatenate([conv_value, conv_value_bias[None, :]], axis=0))
    own["gain_wide"] = wide_lanes(gate_gain)
    if whole_from < seq_count:
        c_w, c_b, step, s_b, d_l, s_g, g_g = swap_small(
            [conv_value, conv_value_bias, proj_step, step_bias, decay_log, skip_gain, gate_gain]
        )
        other = dict(
            state=proj_state, step=step, step_bias=s_b, decay_log=d_l, skip_gain=s_g, gate_gain=g_g
        )
        sent = dict(value=proj_value, gate=proj_gate, out=proj_out)
        first = {k: gather_first(w) for k, w in sent.items()}
        other["conv"] = wide_lanes(jnp.concatenate([c_w, c_b[None, :]], axis=0))
        other["gain_wide"] = wide_lanes(g_g)

    normeds, states, state_backs, units, boths = [], [], [], [], []
    for s in every:
        wide = hidden[s].astype(jnp.float32)
        row_scale = lax.rsqrt(jnp.mean(wide * wide, axis=-1, keepdims=True) + epsilon)
        normeds.append((wide * row_scale * norm_gain[None, :]).astype(bf16))
        state_raw = jnp.dot(normeds[s], proj_state, preferred_element_type=jnp.float32)
        state_conv, back = jax.vjp(
            functools.partial(causal_conv, doc_masks=lag_masks(segment_ids[s])),
            state_raw,
            conv_state,
            conv_state_bias,
        )
        state_backs.append(back)
        low = state_conv.astype(bf16)
        into, out = low[:, :STATE], low[:, STATE:]
        states.append((into, into.T, out, out.T))
        units.append(unit_forward(own, normeds[s], out_grad[s], segment_ids[s : s + 1], states[s]))
        if s < whole_from:
            sums = units[s]["sums"]
            boths.append(tensor_join(sums, tensor_others(sums)))
    branches, received, output_ins, d_gates, d_mixeds = [], [], [], [], []
    grad_gate_gain = jnp.zeros((local_inner,), jnp.float32)
    extras, middles = {}, {}
    if whole_from < seq_count:
        second = {k: along_dp(after(first[k], units[0]["mixed"]), 2) for k in sent}
        third = {k: along_dp(first[k], 1) for k in sent}
        fourth = {k: along_dp(after(second[k], units[-1]["mixed"]), 1) for k in sent}
    for s in every:
        if s == whole_from:
            for k in sent:
                pieces = (first[k], second[k], third[k], fourth[k])
                pieces = lax.optimization_barrier((*pieces, branches[0]))[:4]
                other[k] = assemble(sent[k], *pieces)
        if s >= whole_from:
            extras[s] = unit_forward(
                other, normeds[s], out_grad[s], segment_ids[s : s + 1], states[s]
            )
            boths.append(units[s]["sums"] + extras[s]["sums"])
            middles[s] = unit_middle(extras[s], other, boths[s], inner_total)
        output_in, d_gate, d_mixed, grad_gain = unit_middle(units[s], own, boths[s], inner_total)
        grad_gate_gain = grad_gate_gain + grad_gain
        output_ins.append(output_in)
        d_gates.append(d_gate)
        d_mixeds.append(d_mixed)
        branches.append(lax.optimization_barrier(out_product(output_in, proj_out)))
        if s < whole_from:
            received.append(tensor_others(branches[s]))
        else:
            received.append(lax.optimization_barrier(out_product(middles[s][0], other["out"])))

    normed_all = jnp.concatenate(normeds, axis=0)
    early_part = jnp.stack(
        [
            grad_product(normed_all, jnp.concatenate(d_gates, axis=1)),
            grad_product(
                out_grad.reshape(seq_count * length, width), jnp.concatenate(output_ins, axis=1)
            ),
        ]
    )
    early = lax.psum_scatter(early_part, "dp", scatter_dimension=1, tiled=True)

    backs, parts, others = [], [], []
    waits = (early_part, *branches, received[0])
    for s in every:
        back = unit_backward(units[s], own, d_gates[s], after(d_mixeds[s], *waits), state_backs[s])
        backs.append(back)
        parts.append(lax.optimization_barrier(normed_part(own, d_gates[s], *back[:3])))
        if s < whole_from:
            others.append(tensor_others(parts[s]))
            waits = (parts[s],)
    later_part = jnp.concatenate(
        [
            grad_product(normed_all, jnp.concatenate([b[0] for b in backs], axis=1)),
            token_product(normed_all, jnp.concatenate([b[1] for b in backs], axis=0)),
            grad_product(normed_all, jnp.concatenate([b[2] for b in backs], axis=1)),
        ],
        axis=1,
    )
    later_part = after(later_part, early)
    later = lax.psum_scatter(later_part, "dp", scatter_dimension=0, tiled=True)
    later_value = later[:, :local_inner]
    edge = local_inner + state_width
    state_part = later[:, local_inner:edge]
    waits, extra_backs = (later_part, *others), []
    grad_norm_gain = jnp.zeros((width,), jnp.float32)
    for s in every:
        wide = hidden[s].astype(jnp.float32)
        row_scale = lax.rsqrt(jnp.mean(wide * wide, axis=-1, keepdims=True) + epsilon)
        grad_norm_gain = grad_norm_gain + jnp.sum(parts[s] * wide * row_scale, axis=0)
    for s in range(whole_from, seq_count):
        d_gate = middles[s][1]
        back = unit_backward(extras[s], other, d_gate, after(middles[s][2], *waits), state_backs[s])
        extra_backs.append(back)
        others.append(lax.optimization_barrier(normed_part(other, d_gate, *back[:3])))

    param_grads = [sum(grads) for grads in zip(*[b[3] for b in backs])]
    d_conv, g_cs, g_csb, g_sb, g_dl, g_sg = param_grads
    d_conv = jnp.sum(d_conv, axis=-1)
    own_grads = [d_conv[:KERNEL], d_conv[KERNEL], g_sb, g_dl, g_sg, grad_gate_gain]
    shared = [g_cs, g_csb, grad_norm_gain]
    own_flat = jnp.concatenate([g.reshape(-1) for g in own_grads])
    shared_flat = jnp.concatenate([g.reshape(-1) for g in shared])
    arrived = tensor_others(shared_flat)
    between = []
    if whole_from < seq_count:
        arrived = after(arrived, *waits)
        between = [others[0], others[0], others[-1]]
    shared_flat = tensor_join(shared_flat, arrived)
    stacked = ()
    parts[0] = after(parts[0], later)
    for s in reversed(every):
        stacked = finish(
            s, parts[s], only_others(parts[s], others[s]), branches[s],
            only_others(branches[s], received[s]), hidden, out_grad, norm_gain, stacked
        )
        if between and s == every[-1]:
            between.append(stacked[0])
    packed = sum_dp(jnp.concatenate([own_flat, shared_flat]), *between)
    own_sum, shared_sum = packed[: own_flat.shape[0]], packed[own_flat.shape[0] :]

    grad_proj_state = tensor_join(state_part, tensor_others(state_part))

    def split(flat, like):
        result, edge = [], 0
        for g in like:
            result.append(flat[edge : edge + g.size].reshape(g.shape))
            edge += g.size
        return result

    r_cv, r_cvb, r_sb, r_dl, r_sg, r_gg = split(own_sum, own_grads)
    r_cs, r_csb, r_ng = split(shared_sum, shared)
    return (
        *stacked,
        r_ng,
        early[0],
        later_value,
        grad_proj_state,
        later[:, edge:],
        r_cv,
        r_cvb,
        r_cs,
        r_csb,
        r_sb,
        r_dl,
        r_sg,
        r_gg,
        early[1],
    )


def solution(mesh):
    in_specs = (
        P("dp", None, None),
        P("dp", None),
        P(),
        P(None, "tensor"),
        P(None, "tensor"),
        P(),
        P(None, "tensor"),
        P(None, "tensor"),
        P("tensor"),
        P(),
        P(),
        P("tensor"),
        P("tensor"),
        P("tensor"),
        P("tensor"),
        P(None, "tensor"),
        P("dp", None, None),
    )
    out_specs = (
        P("dp", None, None),
        P("dp", None, None),
        P(),
        P("dp", "tensor"),
        P("dp", "tensor"),
        P("dp", None),
        P("dp", "tensor"),
        P(None, "tensor"),
        P("tensor"),
        P(),
        P(),
        P("tensor"),
        P("tensor"),
        P("tensor"),
        P("tensor"),
        P("dp", "tensor"),
    )
    return jax.shard_map(local, mesh=mesh, in_specs=in_specs, out_specs=out_specs, check_vma=False)
```

```python
import functools

import jax
import jax.numpy as jnp
from jax import lax
from jax.experimental import pallas as pl
from jax.experimental.pallas import tpu as pltpu
from jax.sharding import PartitionSpec as P

HEAD_DIM = 64
STATE = 128
KERNEL = 4
VMEM_BYTES = 50 * 1024 * 1024

epsilon = 1e-05
precise = lax.Precision.HIGHEST


def lag_masks(segment_row):
    length = segment_row.shape[0]
    result = [jnp.ones((length,), jnp.float32)]
    for delay in range(1, KERNEL):
        earlier = jnp.concatenate(
            [jnp.full((delay,), -1, jnp.int32), segment_row[: length - delay]]
        )
        result.append((earlier == segment_row).astype(jnp.float32))
    return result


def causal_conv(values, weight, conv_bias, doc_masks):
    length = values.shape[0]
    summed = conv_bias[None, :] + weight[KERNEL - 1][None, :] * values
    for delay in range(1, KERNEL):
        earlier = jnp.concatenate(
            [jnp.zeros((delay, values.shape[1]), jnp.float32), values[: length - delay]], axis=0
        )
        summed = summed + weight[KERNEL - 1 - delay][None, :] * earlier * doc_masks[delay][:, None]
    return jax.nn.silu(summed)


CHUNK = 128
PAIR = 2 * HEAD_DIM
LOG2E = 1.4426950408889634
NN = (((1,), (0,)), ((), ()))
NT = (((1,), (1,)), ((), ()))
TN = (((0,), (0,)), ((), ()))
bf16 = jnp.bfloat16


def mxu(a, b, dims=NN):
    return lax.dot_general(a, b, dims, preferred_element_type=jnp.float32)


def sigmoid(z):
    return 0.5 * jnp.tanh(0.5 * z) + 0.5


def pair_wide(rows, at):
    top = jnp.broadcast_to(rows[at : at + 1], (HEAD_DIM, CHUNK))
    low = jnp.broadcast_to(rows[at + 1 : at + 2], (HEAD_DIM, CHUNK))
    return jnp.concatenate([top, low], axis=0)


def decay_block(rows, h):
    run = jnp.broadcast_to(rows[h : h + 1], (CHUNK, CHUNK))
    return jnp.exp2(jnp.minimum(run - run.T, 0.0))


def doc_block(masks):
    segment = jnp.broadcast_to(masks[3:4], (CHUNK, CHUNK))
    source = lax.broadcasted_iota(jnp.int32, (CHUNK, CHUNK), 0)
    target = lax.broadcasted_iota(jnp.int32, (CHUNK, CHUNK), 1)
    return ((segment == segment.T) & (source <= target)).astype(jnp.float32)


def shifted_taps(raw, before, masks):
    lane = lax.broadcasted_iota(jnp.int32, raw.shape, 1)
    taps = [raw]
    for k in range(1, KERNEL):
        moved = pltpu.roll(jnp.where(lane >= CHUNK - k, before, raw), k, 1)
        taps.append(moved * masks[k - 1 : k])
    return taps


def conv_sum(taps, conv_ref, part):
    total = conv_ref[KERNEL, part, :]
    for k in range(KERNEL):
        total = total + conv_ref[KERNEL - 1 - k, part, :] * taps[k]
    return total


def mix_kernel(
    raw_ref, gate_ref, dout_ref, rows_ref, mask_ref, into_ref, outt_ref, conv_ref, gain_ref,
    mixed_ref, entry_ref, sums_ref, held_ref, before_ref,
):
    @pl.when(pl.program_id(1) == 0)
    def _():
        held_ref[...] = jnp.zeros_like(held_ref)
        before_ref[...] = jnp.zeros_like(before_ref)

    masks = mask_ref[0]
    into, outt = into_ref[...], outt_ref[...]
    affinity = mxu(into, outt) * doc_block(masks)

    def body(p, sums):
        part = pl.ds(pl.multiple_of(p * PAIR, PAIR), PAIR)
        rows = rows_ref[0, p]
        raw = raw_ref[part, :].astype(jnp.float32)
        pre = conv_sum(shifted_taps(raw, before_ref[part, :], masks), conv_ref, part)
        value = pre * sigmoid(pre)
        scaled = value * pair_wide(rows, 2)
        low = scaled.astype(bf16)
        near = []
        for h in range(2):
            mixing = (decay_block(rows, h) * affinity).astype(bf16)
            near.append(mxu(low[h * HEAD_DIM : (h + 1) * HEAD_DIM], mixing))
        held = held_ref[part, :]
        held_low = held.astype(bf16)
        entry_ref[0, part, :] = held_low
        far = mxu(held_low, outt) * pair_wide(rows, 6)
        kept = (scaled * pair_wide(rows, 4)).astype(bf16)
        held_ref[part, :] = held * pair_wide(rows, 8) + mxu(kept, into)
        mixed = jnp.concatenate(near, axis=0) + far + pair_wide(rows, 10) * value
        mixed_ref[part, :] = mixed
        before_ref[part, :] = raw
        gate = gate_ref[part, :].astype(jnp.float32)
        gated = mixed * gate * sigmoid(gate)
        square = jnp.sum(gated * gated, axis=0, keepdims=True)
        inner = dout_ref[part, :].astype(jnp.float32) * gain_ref[part, :] * gated
        return sums[0] + square, sums[1] + jnp.sum(inner, axis=0, keepdims=True)

    zero = jnp.zeros((1, CHUNK), jnp.float32)
    pairs = raw_ref.shape[0] // PAIR
    square, inner = lax.fori_loop(0, pairs, body, (zero, zero), unroll=min(8, pairs))
    sums_ref[0, 0:1, :] = square
    sums_ref[0, 1:2, :] = inner


def back_kernel(
    raw_ref, before_ref, mixed_ref, dmix_ref, entry_ref, rows_ref, mask_ref, into_ref, intot_ref,
    out_ref, outt_ref, conv_ref,
    draw_ref, drows_ref, dstate_ref, dconv_ref, dheld_ref, later_ref, latermask_ref, dfar_ref,
):
    step = pl.program_id(1)

    @pl.when((pl.program_id(0) == 0) & (step == 0))
    def _():
        dconv_ref[...] = jnp.zeros_like(dconv_ref)

    @pl.when(step == 0)
    def _():
        dheld_ref[...] = jnp.zeros_like(dheld_ref)
        later_ref[...] = jnp.zeros_like(later_ref)
        latermask_ref[...] = jnp.zeros_like(latermask_ref)

    first = step == pl.num_programs(1) - 1
    masks, later_masks = mask_ref[0], latermask_ref[...]
    into, intot, out, outt = into_ref[...], intot_ref[...], out_ref[...], outt_ref[...]
    allowed = doc_block(masks)
    affinity = mxu(into, outt) * allowed
    dfar_ref[...] = jnp.zeros_like(dfar_ref)
    lane = lax.broadcasted_iota(jnp.int32, (PAIR, CHUNK), 1)
    head_row = lax.broadcasted_iota(jnp.int32, (PAIR, CHUNK), 0) < HEAD_DIM

    def body(p, daffinity):
        part = pl.ds(pl.multiple_of(p * PAIR, PAIR), PAIR)
        rows = rows_ref[0, p]
        raw = raw_ref[part, :].astype(jnp.float32)
        before = jnp.where(first, 0.0, before_ref[part, :].astype(jnp.float32))
        taps = shifted_taps(raw, before, masks)
        pre = conv_sum(taps, conv_ref, part)
        gate = sigmoid(pre)
        value = pre * gate
        step_wide = pair_wide(rows, 2)
        skip_wide = pair_wide(rows, 10)
        keep_wide = pair_wide(rows, 4)
        scaled = value * step_wide
        low = scaled.astype(bf16)
        dmix_low = dmix_ref[part, :]
        dmix = dmix_low.astype(jnp.float32)
        halves = jnp.concatenate(
            [jnp.where(head_row, dmix, 0.0).astype(bf16), jnp.where(head_row, 0.0, dmix).astype(bf16)],
            axis=1,
        )
        dmixing = mxu(low, halves, TN)
        dnear = []
        for h in range(2):
            decay = decay_block(rows, h)
            mixing = (decay * affinity).astype(bf16)
            daffinity = daffinity + dmixing[:, h * CHUNK : (h + 1) * CHUNK] * decay
            dnear.append(mxu(dmix_low[h * HEAD_DIM : (h + 1) * HEAD_DIM], mixing, NT))
        dnear = jnp.concatenate(dnear, axis=0)
        held_low = entry_ref[0, part, :]
        dheld = dheld_ref[part, :]
        dheld_low = dheld.astype(bf16)
        carried = dheld * pair_wide(rows, 8)
        dfar = mxu(dheld_low, intot) * keep_wide
        kept = (scaled * keep_wide).astype(bf16)
        read = (dmix * pair_wide(rows, 6)).astype(bf16)
        dfar_ref[:, :STATE] += mxu(kept, dheld_low, TN)
        dfar_ref[:, STATE:] += mxu(read, held_low, TN)
        dheld_ref[part, :] = carried + mxu(read, out)
        dscaled = dnear + dfar
        scaled_low = low.astype(jnp.float32)
        far_product = scaled * dfar
        running = (
            dmix * (mixed_ref[part, :] - skip_wide * value) - scaled_low * dnear - far_product
        )
        products = (
            running, far_product, carried * held_low.astype(jnp.float32), dscaled * value,
            dmix * value,
        )
        for q, product in enumerate(products):
            for h in range(2):
                drows_ref[0, p, 2 * q + h : 2 * q + h + 1, :] = jnp.sum(
                    product[h * HEAD_DIM : (h + 1) * HEAD_DIM], axis=0, keepdims=True
                )
        dvalue = dscaled * step_wide + skip_wide * dmix
        dpre = dvalue * (gate * (1.0 + pre * (1.0 - gate)))
        later = later_ref[part, :]
        dconv_ref[KERNEL, part, :] += dpre
        dconv_ref[KERNEL - 1, part, :] += dpre * raw
        draw = conv_ref[KERNEL - 1, part, :] * dpre
        for k in range(1, KERNEL):
            dconv_ref[KERNEL - 1 - k, part, :] += dpre * taps[k]
            joined = jnp.where(
                lane < k, later * later_masks[k - 1 : k], dpre * masks[k - 1 : k]
            )
            draw = draw + conv_ref[KERNEL - 1 - k, part, :] * pltpu.roll(joined, CHUNK - k, 1)
        later_ref[part, :] = dpre
        draw_ref[part, :] = draw.astype(bf16)
        return daffinity

    zero = jnp.zeros((CHUNK, CHUNK), jnp.float32)
    daffinity = lax.fori_loop(0, raw_ref.shape[0] // PAIR, body, zero, unroll=2)
    daffinity = (daffinity * allowed).astype(bf16)
    dstate_ref[:, :STATE] = dfar_ref[:, :STATE] + mxu(daffinity, out)
    dstate_ref[:, STATE:] = dfar_ref[:, STATE:] + mxu(daffinity, into, TN)
    latermask_ref[...] = masks


def spec(block, index):
    return pl.BlockSpec(block, index)


def mix_forward(seqs, raw, gate, dout, rows, masks, into, outt, conv, gain):
    ch, tokens = raw.shape
    chunks = tokens // seqs // CHUNK
    at = lambda s, c: (0, s * chunks + c)
    up = lambda s, c: (s * chunks + c, 0)
    slab = spec((ch, CHUNK), at)
    return pl.pallas_call(
        mix_kernel,
        grid=(seqs, chunks),
        in_specs=[
            slab, slab, slab,
            spec((1,) + rows.shape[1:], lambda s, c: (s * chunks + c, 0, 0, 0)),
            spec((1, 8, CHUNK), lambda s, c: (s * chunks + c, 0, 0)),
            spec((CHUNK, STATE), up),
            spec((STATE, CHUNK), at),
            spec(conv.shape, lambda s, c: (0, 0, 0)),
            spec((ch, CHUNK), lambda s, c: (0, 0)),
        ],
        out_specs=[
            slab,
            spec((1, ch, STATE), lambda s, c: (s * chunks + c, 0, 0)),
            spec((1, 8, CHUNK), lambda s, c: (s * chunks + c, 0, 0)),
        ],
        out_shape=[
            jax.ShapeDtypeStruct((ch, tokens), jnp.float32),
            jax.ShapeDtypeStruct((seqs * chunks, ch, STATE), bf16),
            jax.ShapeDtypeStruct((seqs * chunks, 8, CHUNK), jnp.float32),
        ],
        scratch_shapes=[
            pltpu.VMEM((ch, STATE), jnp.float32),
            pltpu.VMEM((ch, CHUNK), jnp.float32),
        ],
        compiler_params=pltpu.CompilerParams(vmem_limit_bytes=VMEM_BYTES),
        cost_estimate=pl.CostEstimate(
            flops=tokens, bytes_accessed=tokens, transcendentals=0
        ),
        name="mix_forward",
    )(raw, gate, dout, rows, masks, into, outt, conv, gain)


def mix_backward(seqs, raw, mixed, dmix, entry, rows, masks, into, intot, out, outt, conv):
    ch, tokens = raw.shape
    chunks = tokens // seqs // CHUNK
    place = lambda s, c: s * chunks + chunks - 1 - c
    at = lambda s, c: (0, place(s, c))
    up = lambda s, c: (place(s, c), 0)
    slab = spec((ch, CHUNK), at)
    row_spec = spec((1,) + rows.shape[1:], lambda s, c: (place(s, c), 0, 0, 0))
    return pl.pallas_call(
        back_kernel,
        grid=(seqs, chunks),
        in_specs=[
            slab,
            spec((ch, CHUNK), lambda s, c: (0, jnp.maximum(place(s, c) - 1, 0))),
            slab, slab,
            spec((1, ch, STATE), lambda s, c: (place(s, c), 0, 0)),
            row_spec,
            spec((1, 8, CHUNK), lambda s, c: (place(s, c), 0, 0)),
            spec((CHUNK, STATE), up),
            spec((STATE, CHUNK), at),
            spec((CHUNK, STATE), up),
            spec((STATE, CHUNK), at),
            spec(conv.shape, lambda s, c: (0, 0, 0)),
        ],
        out_specs=[
            slab,
            row_spec,
            spec((CHUNK, 2 * STATE), up),
            spec(conv.shape, lambda s, c: (0, 0, 0)),
        ],
        out_shape=[
            jax.ShapeDtypeStruct((ch, tokens), bf16),
            jax.ShapeDtypeStruct(rows.shape, jnp.float32),
            jax.ShapeDtypeStruct((tokens, 2 * STATE), jnp.float32),
            jax.ShapeDtypeStruct(conv.shape, jnp.float32),
        ],
        scratch_shapes=[
            pltpu.VMEM((ch, STATE), jnp.float32),
            pltpu.VMEM((ch, CHUNK), jnp.float32),
            pltpu.VMEM((8, CHUNK), jnp.float32),
            pltpu.VMEM((CHUNK, 2 * STATE), jnp.float32),
        ],
        compiler_params=pltpu.CompilerParams(vmem_limit_bytes=VMEM_BYTES),
        cost_estimate=pl.CostEstimate(
            flops=tokens, bytes_accessed=tokens, transcendentals=0
        ),
        name="mix_backward",
    )(raw, raw, mixed, dmix, entry, rows, masks, into, intot, out, outt, conv)


def wide_lanes(columns):
    return jnp.broadcast_to(columns[..., None], columns.shape + (CHUNK,))


def pair_rows(parts, seqs):
    heads, _, chunks, _ = parts[0].shape
    stacked = jnp.stack(parts + [jnp.zeros_like(parts[0])] * (8 - len(parts)))
    stacked = stacked.reshape(8, heads // 2, 2, seqs * chunks, CHUNK)
    return stacked.transpose(3, 1, 0, 2, 4).reshape(seqs * chunks, heads // 2, 16, CHUNK)


def unpair_rows(rows, q, seqs):
    steps, pairs = rows.shape[:2]
    part = rows[:, :, 2 * q : 2 * q + 2, :].transpose(1, 2, 0, 3)
    return part.reshape(2 * pairs, seqs, steps // seqs, CHUNK)


def step_rows(step_raw, step_bias, decay_log, skip_gain, segment_ids):
    seqs, length = segment_ids.shape
    chunks = length // CHUNK
    heads = step_raw.shape[0]
    rate = -jnp.exp(decay_log)
    size = jax.nn.softplus(step_raw + step_bias[:, None]).reshape(heads, seqs, chunks, CHUNK)
    places = jnp.arange(CHUNK)
    upper = (places[:, None] <= places[None, :]).astype(jnp.float32)
    running = jnp.einsum(
        "hqcs,st->hqct", size * rate[:, None, None, None], upper, precision=precise
    )
    segments = segment_ids.reshape(seqs, chunks, CHUNK)
    last = segments[:, :, -1]
    before = jnp.concatenate([jnp.full((seqs, 1), -1, jnp.int32), last[:, :-1]], axis=1)
    total = running[..., -1:]
    at_end = (segments == last[..., None]).astype(jnp.float32)
    from_start = (segments == before[..., None]).astype(jnp.float32)
    through = (last == before).astype(jnp.float32)[..., None]
    full = jnp.ones_like(running)
    parts = [
        running * LOG2E,
        size,
        jnp.exp(total - running) * at_end,
        jnp.exp(running) * from_start,
        jnp.exp(total) * through * full,
        skip_gain[:, None, None, None] * full,
    ]
    lags = [jnp.stack(lag_masks(row)[1:]) for row in segment_ids]
    lags = jnp.stack(lags).reshape(seqs, KERNEL - 1, chunks, CHUNK).transpose(0, 2, 1, 3)
    masks = jnp.concatenate(
        [
            lags,
            segments[:, :, None, :].astype(jnp.float32),
            jnp.zeros((seqs, chunks, 4, CHUNK), jnp.float32),
        ],
        axis=2,
    ).reshape(seqs * chunks, 8, CHUNK)
    return pair_rows(parts, seqs), masks


def step_grads(drows, step_raw, step_bias, decay_log, seqs):
    heads, tokens = step_raw.shape
    running, far, carried, direct, skip = [unpair_rows(drows, q, seqs) for q in range(5)]
    rate = -jnp.exp(decay_log)[:, None, None, None]
    biased = step_raw + step_bias[:, None]
    size = jax.nn.softplus(biased).reshape(running.shape)
    total = jnp.sum(far + carried, axis=-1, keepdims=True)
    places = jnp.arange(CHUNK)
    lower = (places[:, None] >= places[None, :]).astype(jnp.float32)
    ddrop = jnp.einsum("hqct,ts->hqcs", running, lower, precision=precise) + total
    dsize = direct + ddrop * rate
    draw = dsize.reshape(heads, tokens) * jax.nn.sigmoid(biased)
    every = (1, 2, 3)
    return (
        draw,
        jnp.sum(draw, axis=1),
        jnp.sum(ddrop * size * rate, axis=every),
        jnp.sum(skip, axis=every),
    )


def finish_kernel(
    part_ref, other_ref, branch_ref, received_ref, hidden_ref, cotangent_ref, gain_ref, *rest
):
    out_ref, grad_ref = rest[-2:]
    wide = hidden_ref[0].astype(jnp.float32)
    width = wide.shape[1]
    row_scale = lax.rsqrt(jnp.mean(wide * wide, axis=-1, keepdims=True) + epsilon)
    scaled = (part_ref[...] + other_ref[...]) * gain_ref[...]
    inner = jnp.sum(scaled * wide, axis=-1, keepdims=True)
    grad_ref[0] = (
        cotangent_ref[0].astype(jnp.float32)
        + row_scale * scaled
        - wide * (row_scale * row_scale * row_scale * inner / width)
    )
    out_ref[0] = (wide + (branch_ref[...] + received_ref[...])).astype(bf16)


def finish(s, part, other, branch, received, hidden, out_grad, norm_gain, earlier):
    seqs, length, width = hidden.shape
    tile = 256
    flat = spec((tile, width), lambda i: (i, 0))
    deep = spec((1, tile, width), lambda i: (s, i, 0))
    held = [pl.BlockSpec(memory_space=pl.ANY)] * len(earlier)
    return pl.pallas_call(
        finish_kernel,
        grid=(length // tile,),
        in_specs=[flat] * 4 + [deep, deep, spec((1, width), lambda i: (0, 0))] + held,
        out_specs=[deep, deep],
        out_shape=[
            jax.ShapeDtypeStruct((seqs, length, width), bf16),
            jax.ShapeDtypeStruct((seqs, length, width), jnp.float32),
        ],
        input_output_aliases={7 + i: i for i in range(len(earlier))},
        compiler_params=pltpu.CompilerParams(vmem_limit_bytes=VMEM_BYTES),
        cost_estimate=pl.CostEstimate(
            flops=length, bytes_accessed=length, transcendentals=0
        ),
        name="finish",
    )(part, other, branch, received, hidden, out_grad, norm_gain[None, :], *earlier)


def out_product(left, weight):
    return lax.dot_general(left, weight, (((0,), (1,)), ((), ())), preferred_element_type=jnp.float32)


def in_product(weight, tokens):
    return lax.dot_general(weight, tokens, (((0,), (1,)), ((), ())), preferred_element_type=jnp.float32)


def grad_product(tokens, channels):
    return lax.dot_general(
        tokens, channels, (((0,), (1,)), ((), ())), preferred_element_type=jnp.float32
    )


def right_product(left, weight):
    return lax.dot_general(
        left, weight, (((1,), (1,)), ((), ())), preferred_element_type=jnp.float32
    )


def token_product(left, right):
    return lax.dot_general(
        left, right, (((0,), (0,)), ((), ())), preferred_element_type=jnp.float32
    )


def tensor_others(part):
    count = lax.axis_size("tensor")
    if count == 2:
        return lax.ppermute(part, "tensor", [(0, 1), (1, 0)])
    return lax.psum(part, "tensor")


def tensor_join(part, others):
    return part + others if lax.axis_size("tensor") == 2 else others


def only_others(part, others):
    return others if lax.axis_size("tensor") == 2 else others - part


def after(value, *earlier):
    return lax.optimization_barrier((value, *earlier))[0]


def assemble_kernel(quarter_ref, first_ref, second_ref, third_ref, fourth_ref, whole_ref):
    rows = first_ref.shape[0]
    pieces = (first_ref, second_ref, third_ref, fourth_ref)
    for piece_ref, flip in zip(pieces, (0, 2, 1, 3)):
        place = jnp.bitwise_xor(quarter_ref[0], flip)
        part = pl.ds(pl.multiple_of(place * rows, rows), rows)
        whole_ref[part, :] = piece_ref[...].astype(whole_ref.dtype)


def gather_first(weight):
    rows, columns = weight.shape[0] // 4, weight.shape[1]
    quarter = lax.rem(lax.axis_index("dp"), 4)
    mine = lax.dynamic_slice(weight, (quarter * rows, 0), (rows, columns))
    mine = lax.optimization_barrier(mine.astype(jnp.float32))
    return lax.ppermute(mine, "tensor", [(0, 1), (1, 0)])


def along_dp(piece, flip):
    return lax.ppermute(piece, "dp", [(j, j ^ flip) for j in range(lax.axis_size("dp"))])


def assemble(weight, *pieces):
    quarter = lax.rem(lax.axis_index("dp"), 4)
    return pl.pallas_call(
        assemble_kernel,
        in_specs=[pl.BlockSpec(memory_space=pltpu.SMEM)]
        + [pl.BlockSpec(memory_space=pltpu.VMEM)] * 4,
        out_specs=pl.BlockSpec(memory_space=pltpu.VMEM),
        out_shape=jax.ShapeDtypeStruct(weight.shape, weight.dtype),
        compiler_params=pltpu.CompilerParams(vmem_limit_bytes=VMEM_BYTES),
        cost_estimate=pl.CostEstimate(
            flops=weight.size, bytes_accessed=6 * weight.size, transcendentals=0
        ),
        name="assemble",
    )(quarter.reshape(1), *pieces)


def sum_dp(value, *between):
    count = lax.axis_size("dp")
    if count & (count - 1) or not between:
        return lax.psum(value, "dp")
    flip, between = 1, list(between)
    while flip < count:
        arrived = along_dp(value, flip)
        if between:
            arrived = after(arrived, between.pop(0))
        value = value + arrived
        flip *= 2
    return value


def swap_small(arrays):
    flat = jnp.concatenate([a.astype(jnp.float32).reshape(-1) for a in arrays])
    flat = lax.ppermute(lax.optimization_barrier(flat), "tensor", [(0, 1), (1, 0)])
    flat = lax.optimization_barrier(flat)
    result, edge = [], 0
    for a in arrays:
        result.append(flat[edge : edge + a.size].reshape(a.shape).astype(a.dtype))
        edge += a.size
    return result


def unit_forward(weights, normed, cotangent, segments, states, earlier=(), between=()):
    step = in_product(weights["step"], normed)
    gate = in_product(weights["gate"], normed).astype(bf16)
    dout = in_product(weights["out"], cotangent).astype(bf16)
    raw = in_product(weights["value"], after(normed, *earlier)).astype(bf16)
    rows, masks = step_rows(
        step, weights["step_bias"], weights["decay_log"], weights["skip_gain"], segments
    )
    into, _, _, outt = states
    rows = after(rows, *between)
    mixed, entry, sums = mix_forward(
        1, raw, gate, dout, rows, masks, into, outt, weights["conv"], weights["gain_wide"]
    )
    sums = sums[:, :2].transpose(1, 0, 2).reshape(2, normed.shape[0])
    return dict(
        step=step, gate=gate, raw=raw, dout=dout, rows=rows, masks=masks, mixed=mixed,
        entry=entry, sums=sums, states=states,
    )


def unit_middle(unit, weights, both, inner_total):
    gate, mixed, dout = unit["gate"], unit["mixed"], unit["dout"]
    gate, dout = gate.astype(jnp.float32), dout.astype(jnp.float32)
    gain = weights["gate_gain"][:, None]
    sigma = sigmoid(gate)
    gated = mixed * gate * sigma
    gated_scale = lax.rsqrt(both[0:1] / inner_total + epsilon)
    output_in = (gated * gated_scale * gain).astype(bf16)
    d_gated = gated_scale * (dout * gain) - gated * (
        gated_scale**3 * both[1:2] / inner_total
    )
    d_mixed = (d_gated * gate * sigma).astype(bf16)
    d_gate = (d_gated * mixed * sigma * (1.0 + gate * (1.0 - sigma))).astype(bf16)
    grad_gain = jnp.sum(dout * gated * gated_scale, axis=1)
    return output_in, d_gate, d_mixed, grad_gain


def unit_backward(unit, weights, d_gate, d_mixed, state_back):
    d_value, d_rows, d_state, d_conv = mix_backward(
        1, unit["raw"], unit["mixed"], d_mixed, unit["entry"], unit["rows"], unit["masks"],
        *unit["states"], weights["conv"],
    )
    d_step, *step_params = step_grads(
        d_rows, unit["step"], weights["step_bias"], weights["decay_log"], 1
    )
    d_state, g_cs, g_csb = state_back(d_state.astype(bf16).astype(jnp.float32))
    d_state, d_step = d_state.astype(bf16), d_step.astype(bf16)
    return d_value, d_state, d_step, (d_conv, g_cs, g_csb, *step_params)


def normed_part(weights, d_gate, d_value, d_state, d_step):
    return (
        out_product(d_gate, weights["gate"])
        + out_product(d_value, weights["value"])
        + right_product(d_state, weights["state"])
        + out_product(d_step, weights["step"])
    )


def local(
    hidden,
    segment_ids,
    norm_gain,
    proj_gate,
    proj_value,
    proj_state,
    proj_step,
    conv_value,
    conv_value_bias,
    conv_state,
    conv_state_bias,
    step_bias,
    decay_log,
    skip_gain,
    gate_gain,
    proj_out,
    out_grad,
):
    seq_count, length, width = hidden.shape
    local_inner = proj_gate.shape[1]
    state_width = proj_state.shape[1]
    tensor_count = lax.axis_size("tensor")
    inner_total = local_inner * tensor_count
    every = range(seq_count)
    whole_from = seq_count
    if tensor_count == 2 and lax.axis_size("dp") % 4 == 0 and seq_count > 1:
        whole_from = seq_count - 1

    own = dict(
        gate=proj_gate, value=proj_value, out=proj_out, state=proj_state, step=proj_step,
        step_bias=step_bias, decay_log=decay_log, skip_gain=skip_gain, gate_gain=gate_gain,
    )
    own["conv"] = wide_lanes(jnp.concatenate([conv_value, conv_value_bias[None, :]], axis=0))
    own["gain_wide"] = wide_lanes(gate_gain)
    if whole_from < seq_count:
        c_w, c_b, step, s_b, d_l, s_g, g_g = swap_small(
            [conv_value, conv_value_bias, proj_step, step_bias, decay_log, skip_gain, gate_gain]
        )
        other = dict(
            state=proj_state, step=step, step_bias=s_b, decay_log=d_l, skip_gain=s_g, gate_gain=g_g
        )
        sent = dict(value=proj_value, gate=proj_gate, out=proj_out)
        first = {k: gather_first(w) for k, w in sent.items()}
        second = dict(value=along_dp(first["value"], 2))
        other["conv"] = wide_lanes(jnp.concatenate([c_w, c_b[None, :]], axis=0))
        other["gain_wide"] = wide_lanes(g_g)

    normeds, states, state_backs, units, boths = [], [], [], [], []
    for s in every:
        wide = hidden[s].astype(jnp.float32)
        row_scale = lax.rsqrt(jnp.mean(wide * wide, axis=-1, keepdims=True) + epsilon)
        normeds.append((wide * row_scale * norm_gain[None, :]).astype(bf16))
        state_raw = jnp.dot(normeds[s], proj_state, preferred_element_type=jnp.float32)
        state_conv, back = jax.vjp(
            functools.partial(causal_conv, doc_masks=lag_masks(segment_ids[s])),
            state_raw,
            conv_state,
            conv_state_bias,
        )
        state_backs.append(back)
        low = state_conv.astype(bf16)
        into, out = low[:, :STATE], low[:, STATE:]
        states.append((into, into.T, out, out.T))
        between = (second["value"],) if 0 < s == whole_from else ()
        units.append(
            unit_forward(
                own, normeds[s], out_grad[s], segment_ids[s : s + 1], states[s], between=between
            )
        )
        if s < whole_from:
            sums = units[s]["sums"]
            boths.append(tensor_join(sums, tensor_others(sums)))
    branches, received, output_ins, d_gates, d_mixeds = [], [], [], [], []
    grad_gate_gain = jnp.zeros((local_inner,), jnp.float32)
    extras, middles, arrivals = {}, {}, ()
    if whole_from < seq_count:
        second["gate"] = along_dp(after(first["gate"], units[0]["mixed"]), 2)
        second["out"] = along_dp(after(first["out"], units[-1]["mixed"]), 2)
        third = {k: along_dp(first[k], 1) for k in sent}
        fourth = {k: along_dp(second[k], 1) for k in sent}
        arrivals = (second["out"],)

    backs, parts, others = [], [], []

    def own_middle(s):
        output_in, d_gate, d_mixed, grad_gain = unit_middle(units[s], own, boths[s], inner_total)
        output_ins.append(output_in)
        d_gates.append(d_gate)
        d_mixeds.append(d_mixed)
        branches.append(lax.optimization_barrier(out_product(output_in, proj_out)))
        return grad_gain

    def own_backward(s, earlier, between=()):
        d_mixed = after(d_mixeds[s], *earlier)
        d_value, *rest = unit_backward(units[s], own, d_gates[s], d_mixed, state_backs[s])
        backs.append((after(d_value, *between), *rest))
        parts.append(lax.optimization_barrier(normed_part(own, d_gates[s], *backs[s][:3])))

    for s in range(whole_from):
        grad_gate_gain = grad_gate_gain + own_middle(s)
        received.append(tensor_others(branches[s]))
        earlier = (second["gate"],) if arrivals else ()
        own_backward(s, (branches[s], *earlier), arrivals)
        others.append(tensor_others(parts[s]))
    if whole_from < seq_count:
        for k in sent:
            pieces = (first[k], second[k], third[k], fourth[k])
            pieces = lax.optimization_barrier((*pieces, parts[0]))[:4]
            other[k] = assemble(sent[k], *pieces)
    for s in range(whole_from, seq_count):
        extras[s] = unit_forward(
            other, normeds[s], out_grad[s], segment_ids[s : s + 1], states[s], (received[0],)
        )
        boths.append(units[s]["sums"] + extras[s]["sums"])
        grad_gate_gain = grad_gate_gain + own_middle(s)
        middles[s] = unit_middle(extras[s], other, boths[s], inner_total)
        received.append(lax.optimization_barrier(out_product(middles[s][0], other["out"])))

    normed_all = jnp.concatenate(normeds, axis=0)
    early_part = jnp.stack(
        [
            grad_product(normed_all, jnp.concatenate(d_gates, axis=1)),
            grad_product(
                out_grad.reshape(seq_count * length, width), jnp.concatenate(output_ins, axis=1)
            ),
        ]
    )
    early = lax.psum_scatter(early_part, "dp", scatter_dimension=1, tiled=True)

    for s in range(whole_from, seq_count):
        own_backward(s, (early_part, branches[s]))
    later_part = jnp.concatenate(
        [
            grad_product(normed_all, jnp.concatenate([b[0] for b in backs], axis=1)),
            token_product(normed_all, jnp.concatenate([b[1] for b in backs], axis=0)),
            grad_product(normed_all, jnp.concatenate([b[2] for b in backs], axis=1)),
        ],
        axis=1,
    )
    later_part = after(later_part, early)
    later = lax.psum_scatter(later_part, "dp", scatter_dimension=0, tiled=True)
    later_value = later[:, :local_inner]
    edge = local_inner + state_width
    state_part = later[:, local_inner:edge]
    waits, extra_backs = (later_part, *others), []
    grad_norm_gain = jnp.zeros((width,), jnp.float32)
    for s in every:
        wide = hidden[s].astype(jnp.float32)
        row_scale = lax.rsqrt(jnp.mean(wide * wide, axis=-1, keepdims=True) + epsilon)
        grad_norm_gain = grad_norm_gain + jnp.sum(parts[s] * wide * row_scale, axis=0)
    for s in range(whole_from, seq_count):
        d_gate = middles[s][1]
        back = unit_backward(extras[s], other, d_gate, after(middles[s][2], *waits), state_backs[s])
        extra_backs.append(back)
        others.append(lax.optimization_barrier(normed_part(other, d_gate, *back[:3])))

    param_grads = [sum(grads) for grads in zip(*[b[3] for b in backs])]
    d_conv, g_cs, g_csb, g_sb, g_dl, g_sg = param_grads
    d_conv = jnp.sum(d_conv, axis=-1)
    own_grads = [d_conv[:KERNEL], d_conv[KERNEL], g_sb, g_dl, g_sg, grad_gate_gain]
    shared = [g_cs, g_csb, grad_norm_gain]
    own_flat = jnp.concatenate([g.reshape(-1) for g in own_grads])
    shared_flat = jnp.concatenate([g.reshape(-1) for g in shared])
    arrived = tensor_others(shared_flat)
    between = []
    if whole_from < seq_count:
        arrived = after(arrived, *waits)
        between = [others[0], others[0], others[-1]]
    shared_flat = tensor_join(shared_flat, arrived)
    stacked = ()
    parts[0] = after(parts[0], later)
    for s in reversed(every):
        stacked = finish(
            s, parts[s], only_others(parts[s], others[s]), branches[s],
            only_others(branches[s], received[s]), hidden, out_grad, norm_gain, stacked
        )
        if between and s == every[-1]:
            between.append(stacked[0])
    packed = sum_dp(jnp.concatenate([own_flat, shared_flat]), *between)
    own_sum, shared_sum = packed[: own_flat.shape[0]], packed[own_flat.shape[0] :]

    grad_proj_state = tensor_join(state_part, tensor_others(state_part))

    def split(flat, like):
        result, edge = [], 0
        for g in like:
            result.append(flat[edge : edge + g.size].reshape(g.shape))
            edge += g.size
        return result

    r_cv, r_cvb, r_sb, r_dl, r_sg, r_gg = split(own_sum, own_grads)
    r_cs, r_csb, r_ng = split(shared_sum, shared)
    return (
        *stacked,
        r_ng,
        early[0],
        later_value,
        grad_proj_state,
        later[:, edge:],
        r_cv,
        r_cvb,
        r_cs,
        r_csb,
        r_sb,
        r_dl,
        r_sg,
        r_gg,
        early[1],
    )


def solution(mesh):
    in_specs = (
        P("dp", None, None),
        P("dp", None),
        P(),
        P(None, "tensor"),
        P(None, "tensor"),
        P(),
        P(None, "tensor"),
        P(None, "tensor"),
        P("tensor"),
        P(),
        P(),
        P("tensor"),
        P("tensor"),
        P("tensor"),
        P("tensor"),
        P(None, "tensor"),
        P("dp", None, None),
    )
    out_specs = (
        P("dp", None, None),
        P("dp", None, None),
        P(),
        P("dp", "tensor"),
        P("dp", "tensor"),
        P("dp", None),
        P("dp", "tensor"),
        P(None, "tensor"),
        P("tensor"),
        P(),
        P(),
        P("tensor"),
        P("tensor"),
        P("tensor"),
        P("tensor"),
        P("dp", "tensor"),
    )
    return jax.shard_map(local, mesh=mesh, in_specs=in_specs, out_specs=out_specs, check_vma=False)
```

```python
import functools

import jax
import jax.numpy as jnp
from jax import lax
from jax.experimental import pallas as pl
from jax.experimental.pallas import tpu as pltpu
from jax.sharding import PartitionSpec as P

HEAD_DIM = 64
STATE = 128
KERNEL = 4
VMEM_BYTES = 50 * 1024 * 1024

epsilon = 1e-05
precise = lax.Precision.HIGHEST


def lag_masks(segment_row):
    length = segment_row.shape[0]
    result = [jnp.ones((length,), jnp.float32)]
    for delay in range(1, KERNEL):
        earlier = jnp.concatenate(
            [jnp.full((delay,), -1, jnp.int32), segment_row[: length - delay]]
        )
        result.append((earlier == segment_row).astype(jnp.float32))
    return result


def causal_conv(values, weight, conv_bias, doc_masks):
    length = values.shape[0]
    summed = conv_bias[None, :] + weight[KERNEL - 1][None, :] * values
    for delay in range(1, KERNEL):
        earlier = jnp.concatenate(
            [jnp.zeros((delay, values.shape[1]), jnp.float32), values[: length - delay]], axis=0
        )
        summed = summed + weight[KERNEL - 1 - delay][None, :] * earlier * doc_masks[delay][:, None]
    return jax.nn.silu(summed)


CHUNK = 128
PAIR = 2 * HEAD_DIM
LOG2E = 1.4426950408889634
NN = (((1,), (0,)), ((), ()))
NT = (((1,), (1,)), ((), ()))
TN = (((0,), (0,)), ((), ()))
bf16 = jnp.bfloat16


def mxu(a, b, dims=NN):
    return lax.dot_general(a, b, dims, preferred_element_type=jnp.float32)


def sigmoid(z):
    return 0.5 * jnp.tanh(0.5 * z) + 0.5


def pair_wide(rows, at):
    top = jnp.broadcast_to(rows[at : at + 1], (HEAD_DIM, CHUNK))
    low = jnp.broadcast_to(rows[at + 1 : at + 2], (HEAD_DIM, CHUNK))
    return jnp.concatenate([top, low], axis=0)


def decay_block(rows, h):
    run = jnp.broadcast_to(rows[h : h + 1], (CHUNK, CHUNK))
    return jnp.exp2(jnp.minimum(run - run.T, 0.0))


def doc_block(masks):
    segment = jnp.broadcast_to(masks[3:4], (CHUNK, CHUNK))
    source = lax.broadcasted_iota(jnp.int32, (CHUNK, CHUNK), 0)
    target = lax.broadcasted_iota(jnp.int32, (CHUNK, CHUNK), 1)
    return ((segment == segment.T) & (source <= target)).astype(jnp.float32)


def shifted_taps(raw, before, masks):
    lane = lax.broadcasted_iota(jnp.int32, raw.shape, 1)
    taps = [raw]
    for k in range(1, KERNEL):
        moved = pltpu.roll(jnp.where(lane >= CHUNK - k, before, raw), k, 1)
        taps.append(moved * masks[k - 1 : k])
    return taps


def conv_sum(taps, conv_ref, part):
    total = conv_ref[KERNEL, part, :]
    for k in range(KERNEL):
        total = total + conv_ref[KERNEL - 1 - k, part, :] * taps[k]
    return total


def mix_kernel(
    raw_ref, gate_ref, dout_ref, rows_ref, mask_ref, into_ref, outt_ref, conv_ref, gain_ref,
    mixed_ref, entry_ref, sums_ref, held_ref, before_ref,
):
    @pl.when(pl.program_id(1) == 0)
    def _():
        held_ref[...] = jnp.zeros_like(held_ref)
        before_ref[...] = jnp.zeros_like(before_ref)

    masks = mask_ref[0]
    into, outt = into_ref[...], outt_ref[...]
    affinity = mxu(into, outt) * doc_block(masks)

    def body(p, sums):
        part = pl.ds(pl.multiple_of(p * PAIR, PAIR), PAIR)
        rows = rows_ref[0, p]
        raw = raw_ref[part, :].astype(jnp.float32)
        pre = conv_sum(shifted_taps(raw, before_ref[part, :], masks), conv_ref, part)
        value = pre * sigmoid(pre)
        scaled = value * pair_wide(rows, 2)
        low = scaled.astype(bf16)
        near = []
        for h in range(2):
            mixing = (decay_block(rows, h) * affinity).astype(bf16)
            near.append(mxu(low[h * HEAD_DIM : (h + 1) * HEAD_DIM], mixing))
        held = held_ref[part, :]
        held_low = held.astype(bf16)
        entry_ref[0, part, :] = held_low
        far = mxu(held_low, outt) * pair_wide(rows, 6)
        kept = (scaled * pair_wide(rows, 4)).astype(bf16)
        held_ref[part, :] = held * pair_wide(rows, 8) + mxu(kept, into)
        mixed = jnp.concatenate(near, axis=0) + far + pair_wide(rows, 10) * value
        mixed_ref[part, :] = mixed
        before_ref[part, :] = raw
        gate = gate_ref[part, :].astype(jnp.float32)
        gated = mixed * gate * sigmoid(gate)
        square = jnp.sum(gated * gated, axis=0, keepdims=True)
        inner = dout_ref[part, :].astype(jnp.float32) * gain_ref[part, :] * gated
        return sums[0] + square, sums[1] + jnp.sum(inner, axis=0, keepdims=True)

    zero = jnp.zeros((1, CHUNK), jnp.float32)
    pairs = raw_ref.shape[0] // PAIR
    square, inner = lax.fori_loop(0, pairs, body, (zero, zero), unroll=min(8, pairs))
    sums_ref[0, 0:1, :] = square
    sums_ref[0, 1:2, :] = inner


def back_kernel(
    raw_ref, before_ref, mixed_ref, dmix_ref, entry_ref, rows_ref, mask_ref, into_ref, intot_ref,
    out_ref, outt_ref, conv_ref,
    draw_ref, drows_ref, dstate_ref, dconv_ref, dheld_ref, later_ref, latermask_ref, dfar_ref,
):
    step = pl.program_id(1)

    @pl.when((pl.program_id(0) == 0) & (step == 0))
    def _():
        dconv_ref[...] = jnp.zeros_like(dconv_ref)

    @pl.when(step == 0)
    def _():
        dheld_ref[...] = jnp.zeros_like(dheld_ref)
        later_ref[...] = jnp.zeros_like(later_ref)
        latermask_ref[...] = jnp.zeros_like(latermask_ref)

    first = step == pl.num_programs(1) - 1
    masks, later_masks = mask_ref[0], latermask_ref[...]
    into, intot, out, outt = into_ref[...], intot_ref[...], out_ref[...], outt_ref[...]
    allowed = doc_block(masks)
    affinity = mxu(into, outt) * allowed
    dfar_ref[...] = jnp.zeros_like(dfar_ref)
    lane = lax.broadcasted_iota(jnp.int32, (PAIR, CHUNK), 1)
    head_row = lax.broadcasted_iota(jnp.int32, (PAIR, CHUNK), 0) < HEAD_DIM

    def body(p, daffinity):
        part = pl.ds(pl.multiple_of(p * PAIR, PAIR), PAIR)
        rows = rows_ref[0, p]
        raw = raw_ref[part, :].astype(jnp.float32)
        before = jnp.where(first, 0.0, before_ref[part, :].astype(jnp.float32))
        taps = shifted_taps(raw, before, masks)
        pre = conv_sum(taps, conv_ref, part)
        gate = sigmoid(pre)
        value = pre * gate
        step_wide = pair_wide(rows, 2)
        skip_wide = pair_wide(rows, 10)
        keep_wide = pair_wide(rows, 4)
        scaled = value * step_wide
        low = scaled.astype(bf16)
        dmix_low = dmix_ref[part, :]
        dmix = dmix_low.astype(jnp.float32)
        halves = jnp.concatenate(
            [jnp.where(head_row, dmix, 0.0).astype(bf16), jnp.where(head_row, 0.0, dmix).astype(bf16)],
            axis=1,
        )
        dmixing = mxu(low, halves, TN)
        dnear = []
        for h in range(2):
            decay = decay_block(rows, h)
            mixing = (decay * affinity).astype(bf16)
            daffinity = daffinity + dmixing[:, h * CHUNK : (h + 1) * CHUNK] * decay
            dnear.append(mxu(dmix_low[h * HEAD_DIM : (h + 1) * HEAD_DIM], mixing, NT))
        dnear = jnp.concatenate(dnear, axis=0)
        held_low = entry_ref[0, part, :]
        dheld = dheld_ref[part, :]
        dheld_low = dheld.astype(bf16)
        carried = dheld * pair_wide(rows, 8)
        dfar = mxu(dheld_low, intot) * keep_wide
        kept = (scaled * keep_wide).astype(bf16)
        read = (dmix * pair_wide(rows, 6)).astype(bf16)
        dfar_ref[:, :STATE] += mxu(kept, dheld_low, TN)
        dfar_ref[:, STATE:] += mxu(read, held_low, TN)
        dheld_ref[part, :] = carried + mxu(read, out)
        dscaled = dnear + dfar
        scaled_low = low.astype(jnp.float32)
        far_product = scaled * dfar
        running = (
            dmix * (mixed_ref[part, :] - skip_wide * value) - scaled_low * dnear - far_product
        )
        products = (
            running, far_product, carried * held_low.astype(jnp.float32), dscaled * value,
            dmix * value,
        )
        for q, product in enumerate(products):
            for h in range(2):
                drows_ref[0, p, 2 * q + h : 2 * q + h + 1, :] = jnp.sum(
                    product[h * HEAD_DIM : (h + 1) * HEAD_DIM], axis=0, keepdims=True
                )
        dvalue = dscaled * step_wide + skip_wide * dmix
        dpre = dvalue * (gate * (1.0 + pre * (1.0 - gate)))
        later = later_ref[part, :]
        dconv_ref[KERNEL, part, :] += dpre
        dconv_ref[KERNEL - 1, part, :] += dpre * raw
        draw = conv_ref[KERNEL - 1, part, :] * dpre
        for k in range(1, KERNEL):
            dconv_ref[KERNEL - 1 - k, part, :] += dpre * taps[k]
            joined = jnp.where(
                lane < k, later * later_masks[k - 1 : k], dpre * masks[k - 1 : k]
            )
            draw = draw + conv_ref[KERNEL - 1 - k, part, :] * pltpu.roll(joined, CHUNK - k, 1)
        later_ref[part, :] = dpre
        draw_ref[part, :] = draw.astype(bf16)
        return daffinity

    zero = jnp.zeros((CHUNK, CHUNK), jnp.float32)
    daffinity = lax.fori_loop(0, raw_ref.shape[0] // PAIR, body, zero, unroll=2)
    daffinity = (daffinity * allowed).astype(bf16)
    dstate_ref[:, :STATE] = dfar_ref[:, :STATE] + mxu(daffinity, out)
    dstate_ref[:, STATE:] = dfar_ref[:, STATE:] + mxu(daffinity, into, TN)
    latermask_ref[...] = masks


def spec(block, index):
    return pl.BlockSpec(block, index)


def mix_forward(seqs, raw, gate, dout, rows, masks, into, outt, conv, gain):
    ch, tokens = raw.shape
    chunks = tokens // seqs // CHUNK
    at = lambda s, c: (0, s * chunks + c)
    up = lambda s, c: (s * chunks + c, 0)
    slab = spec((ch, CHUNK), at)
    return pl.pallas_call(
        mix_kernel,
        grid=(seqs, chunks),
        in_specs=[
            slab, slab, slab,
            spec((1,) + rows.shape[1:], lambda s, c: (s * chunks + c, 0, 0, 0)),
            spec((1, 8, CHUNK), lambda s, c: (s * chunks + c, 0, 0)),
            spec((CHUNK, STATE), up),
            spec((STATE, CHUNK), at),
            spec(conv.shape, lambda s, c: (0, 0, 0)),
            spec((ch, CHUNK), lambda s, c: (0, 0)),
        ],
        out_specs=[
            slab,
            spec((1, ch, STATE), lambda s, c: (s * chunks + c, 0, 0)),
            spec((1, 8, CHUNK), lambda s, c: (s * chunks + c, 0, 0)),
        ],
        out_shape=[
            jax.ShapeDtypeStruct((ch, tokens), jnp.float32),
            jax.ShapeDtypeStruct((seqs * chunks, ch, STATE), bf16),
            jax.ShapeDtypeStruct((seqs * chunks, 8, CHUNK), jnp.float32),
        ],
        scratch_shapes=[
            pltpu.VMEM((ch, STATE), jnp.float32),
            pltpu.VMEM((ch, CHUNK), jnp.float32),
        ],
        compiler_params=pltpu.CompilerParams(vmem_limit_bytes=VMEM_BYTES),
        cost_estimate=pl.CostEstimate(
            flops=tokens, bytes_accessed=tokens, transcendentals=0
        ),
        name="mix_forward",
    )(raw, gate, dout, rows, masks, into, outt, conv, gain)


def mix_backward(seqs, raw, mixed, dmix, entry, rows, masks, into, intot, out, outt, conv):
    ch, tokens = raw.shape
    chunks = tokens // seqs // CHUNK
    place = lambda s, c: s * chunks + chunks - 1 - c
    at = lambda s, c: (0, place(s, c))
    up = lambda s, c: (place(s, c), 0)
    slab = spec((ch, CHUNK), at)
    row_spec = spec((1,) + rows.shape[1:], lambda s, c: (place(s, c), 0, 0, 0))
    return pl.pallas_call(
        back_kernel,
        grid=(seqs, chunks),
        in_specs=[
            slab,
            spec((ch, CHUNK), lambda s, c: (0, jnp.maximum(place(s, c) - 1, 0))),
            slab, slab,
            spec((1, ch, STATE), lambda s, c: (place(s, c), 0, 0)),
            row_spec,
            spec((1, 8, CHUNK), lambda s, c: (place(s, c), 0, 0)),
            spec((CHUNK, STATE), up),
            spec((STATE, CHUNK), at),
            spec((CHUNK, STATE), up),
            spec((STATE, CHUNK), at),
            spec(conv.shape, lambda s, c: (0, 0, 0)),
        ],
        out_specs=[
            slab,
            row_spec,
            spec((CHUNK, 2 * STATE), up),
            spec(conv.shape, lambda s, c: (0, 0, 0)),
        ],
        out_shape=[
            jax.ShapeDtypeStruct((ch, tokens), bf16),
            jax.ShapeDtypeStruct(rows.shape, jnp.float32),
            jax.ShapeDtypeStruct((tokens, 2 * STATE), jnp.float32),
            jax.ShapeDtypeStruct(conv.shape, jnp.float32),
        ],
        scratch_shapes=[
            pltpu.VMEM((ch, STATE), jnp.float32),
            pltpu.VMEM((ch, CHUNK), jnp.float32),
            pltpu.VMEM((8, CHUNK), jnp.float32),
            pltpu.VMEM((CHUNK, 2 * STATE), jnp.float32),
        ],
        compiler_params=pltpu.CompilerParams(vmem_limit_bytes=VMEM_BYTES),
        cost_estimate=pl.CostEstimate(
            flops=tokens, bytes_accessed=tokens, transcendentals=0
        ),
        name="mix_backward",
    )(raw, raw, mixed, dmix, entry, rows, masks, into, intot, out, outt, conv)


def wide_lanes(columns):
    return jnp.broadcast_to(columns[..., None], columns.shape + (CHUNK,))


def pair_rows(parts, seqs):
    heads, _, chunks, _ = parts[0].shape
    stacked = jnp.stack(parts + [jnp.zeros_like(parts[0])] * (8 - len(parts)))
    stacked = stacked.reshape(8, heads // 2, 2, seqs * chunks, CHUNK)
    return stacked.transpose(3, 1, 0, 2, 4).reshape(seqs * chunks, heads // 2, 16, CHUNK)


def unpair_rows(rows, q, seqs):
    steps, pairs = rows.shape[:2]
    part = rows[:, :, 2 * q : 2 * q + 2, :].transpose(1, 2, 0, 3)
    return part.reshape(2 * pairs, seqs, steps // seqs, CHUNK)


def step_rows(step_raw, step_bias, decay_log, skip_gain, segment_ids):
    seqs, length = segment_ids.shape
    chunks = length // CHUNK
    heads = step_raw.shape[0]
    rate = -jnp.exp(decay_log)
    size = jax.nn.softplus(step_raw + step_bias[:, None]).reshape(heads, seqs, chunks, CHUNK)
    places = jnp.arange(CHUNK)
    upper = (places[:, None] <= places[None, :]).astype(jnp.float32)
    running = jnp.einsum(
        "hqcs,st->hqct", size * rate[:, None, None, None], upper, precision=precise
    )
    segments = segment_ids.reshape(seqs, chunks, CHUNK)
    last = segments[:, :, -1]
    before = jnp.concatenate([jnp.full((seqs, 1), -1, jnp.int32), last[:, :-1]], axis=1)
    total = running[..., -1:]
    at_end = (segments == last[..., None]).astype(jnp.float32)
    from_start = (segments == before[..., None]).astype(jnp.float32)
    through = (last == before).astype(jnp.float32)[..., None]
    full = jnp.ones_like(running)
    parts = [
        running * LOG2E,
        size,
        jnp.exp(total - running) * at_end,
        jnp.exp(running) * from_start,
        jnp.exp(total) * through * full,
        skip_gain[:, None, None, None] * full,
    ]
    lags = [jnp.stack(lag_masks(row)[1:]) for row in segment_ids]
    lags = jnp.stack(lags).reshape(seqs, KERNEL - 1, chunks, CHUNK).transpose(0, 2, 1, 3)
    masks = jnp.concatenate(
        [
            lags,
            segments[:, :, None, :].astype(jnp.float32),
            jnp.zeros((seqs, chunks, 4, CHUNK), jnp.float32),
        ],
        axis=2,
    ).reshape(seqs * chunks, 8, CHUNK)
    return pair_rows(parts, seqs), masks


def step_grads(drows, step_raw, step_bias, decay_log, seqs):
    heads, tokens = step_raw.shape
    running, far, carried, direct, skip = [unpair_rows(drows, q, seqs) for q in range(5)]
    rate = -jnp.exp(decay_log)[:, None, None, None]
    biased = step_raw + step_bias[:, None]
    size = jax.nn.softplus(biased).reshape(running.shape)
    total = jnp.sum(far + carried, axis=-1, keepdims=True)
    places = jnp.arange(CHUNK)
    lower = (places[:, None] >= places[None, :]).astype(jnp.float32)
    ddrop = jnp.einsum("hqct,ts->hqcs", running, lower, precision=precise) + total
    dsize = direct + ddrop * rate
    draw = dsize.reshape(heads, tokens) * jax.nn.sigmoid(biased)
    every = (1, 2, 3)
    return (
        draw,
        jnp.sum(draw, axis=1),
        jnp.sum(ddrop * size * rate, axis=every),
        jnp.sum(skip, axis=every),
    )


def finish_kernel(
    part_ref, other_ref, branch_ref, received_ref, hidden_ref, cotangent_ref, gain_ref, *rest
):
    out_ref, grad_ref = rest[-2:]
    wide = hidden_ref[0].astype(jnp.float32)
    width = wide.shape[1]
    row_scale = lax.rsqrt(jnp.mean(wide * wide, axis=-1, keepdims=True) + epsilon)
    scaled = (part_ref[...] + other_ref[...]) * gain_ref[...]
    inner = jnp.sum(scaled * wide, axis=-1, keepdims=True)
    grad_ref[0] = (
        cotangent_ref[0].astype(jnp.float32)
        + row_scale * scaled
        - wide * (row_scale * row_scale * row_scale * inner / width)
    )
    out_ref[0] = (wide + (branch_ref[...] + received_ref[...])).astype(bf16)


def finish(s, part, other, branch, received, hidden, out_grad, norm_gain, earlier):
    seqs, length, width = hidden.shape
    tile = 256
    flat = spec((tile, width), lambda i: (i, 0))
    deep = spec((1, tile, width), lambda i: (s, i, 0))
    held = [pl.BlockSpec(memory_space=pl.ANY)] * len(earlier)
    return pl.pallas_call(
        finish_kernel,
        grid=(length // tile,),
        in_specs=[flat] * 4 + [deep, deep, spec((1, width), lambda i: (0, 0))] + held,
        out_specs=[deep, deep],
        out_shape=[
            jax.ShapeDtypeStruct((seqs, length, width), bf16),
            jax.ShapeDtypeStruct((seqs, length, width), jnp.float32),
        ],
        input_output_aliases={7 + i: i for i in range(len(earlier))},
        compiler_params=pltpu.CompilerParams(vmem_limit_bytes=VMEM_BYTES),
        cost_estimate=pl.CostEstimate(
            flops=length, bytes_accessed=length, transcendentals=0
        ),
        name="finish",
    )(part, other, branch, received, hidden, out_grad, norm_gain[None, :], *earlier)


def middle_kernel(scale, gate_ref, mixed_ref, dout_ref, both_ref, gain_ref, *out_refs):
    in_ref, dgate_ref, dmix_ref, dgain_ref = out_refs

    @pl.when(pl.program_id(0) == 0)
    def _():
        dgain_ref[...] = jnp.zeros_like(dgain_ref)

    gated_scale = lax.rsqrt(both_ref[0:1, :] * scale + epsilon)
    pull = gated_scale * gated_scale * gated_scale * both_ref[1:2, :] * scale

    def body(p, carry):
        part = pl.ds(pl.multiple_of(p * PAIR, PAIR), PAIR)
        gate = gate_ref[part, :].astype(jnp.float32)
        mixed = mixed_ref[part, :]
        gain = gain_ref[part, :]
        sigma = sigmoid(gate)
        active = gate * sigma
        gated = mixed * active
        scaled = gated * gated_scale
        dout = dout_ref[part, :].astype(jnp.float32)
        in_ref[part, :] = (scaled * gain).astype(bf16)
        dgain_ref[part, :] += dout * scaled
        d_gated = gated_scale * (dout * gain) - gated * pull
        dmix_ref[part, :] = (d_gated * active).astype(bf16)
        dgate_ref[part, :] = (d_gated * mixed * (sigma + active * (1.0 - sigma))).astype(bf16)
        return carry

    pairs = gate_ref.shape[0] // PAIR
    lax.fori_loop(0, pairs, body, 0, unroll=min(4, pairs))


def middle(gate, mixed, dout, both, gain_wide, inner_total):
    ch, tokens = gate.shape
    slab = spec((ch, CHUNK), lambda i: (0, i))
    still = spec((ch, CHUNK), lambda i: (0, 0))
    shape = jax.ShapeDtypeStruct((ch, tokens), bf16)
    *result, gain_grad = pl.pallas_call(
        functools.partial(middle_kernel, 1.0 / inner_total),
        grid=(tokens // CHUNK,),
        in_specs=[slab, slab, slab, spec((2, CHUNK), lambda i: (0, i)), still],
        out_specs=[slab, slab, slab, still],
        out_shape=[shape, shape, shape, jax.ShapeDtypeStruct((ch, CHUNK), jnp.float32)],
        compiler_params=pltpu.CompilerParams(vmem_limit_bytes=VMEM_BYTES),
        cost_estimate=pl.CostEstimate(flops=tokens, bytes_accessed=tokens, transcendentals=0),
        name="gated_middle",
    )(gate, mixed, dout, both, gain_wide)
    return (*result, jnp.sum(gain_grad, axis=1))


def out_product(left, weight):
    return lax.dot_general(left, weight, (((0,), (1,)), ((), ())), preferred_element_type=jnp.float32)


def in_product(weight, tokens):
    return lax.dot_general(weight, tokens, (((0,), (1,)), ((), ())), preferred_element_type=jnp.float32)


def grad_product(tokens, channels):
    return lax.dot_general(
        tokens, channels, (((0,), (1,)), ((), ())), preferred_element_type=jnp.float32
    )


def right_product(left, weight):
    return lax.dot_general(
        left, weight, (((1,), (1,)), ((), ())), preferred_element_type=jnp.float32
    )


def token_product(left, right):
    return lax.dot_general(
        left, right, (((0,), (0,)), ((), ())), preferred_element_type=jnp.float32
    )


def tensor_others(part):
    count = lax.axis_size("tensor")
    if count == 2:
        return lax.ppermute(part, "tensor", [(0, 1), (1, 0)])
    return lax.psum(part, "tensor")


def tensor_join(part, others):
    return part + others if lax.axis_size("tensor") == 2 else others


def only_others(part, others):
    return others if lax.axis_size("tensor") == 2 else others - part


def after(value, *earlier):
    return lax.optimization_barrier((value, *earlier))[0]


def assemble_kernel(quarter_ref, first_ref, second_ref, third_ref, fourth_ref, whole_ref):
    rows = first_ref.shape[0]
    pieces = (first_ref, second_ref, third_ref, fourth_ref)
    for piece_ref, flip in zip(pieces, (0, 2, 1, 3)):
        place = jnp.bitwise_xor(quarter_ref[0], flip)
        part = pl.ds(pl.multiple_of(place * rows, rows), rows)
        whole_ref[part, :] = piece_ref[...].astype(whole_ref.dtype)


def gather_first(weight):
    rows, columns = weight.shape[0] // 4, weight.shape[1]
    quarter = lax.rem(lax.axis_index("dp"), 4)
    mine = lax.dynamic_slice(weight, (quarter * rows, 0), (rows, columns))
    mine = lax.optimization_barrier(mine.astype(jnp.float32))
    return lax.ppermute(mine, "tensor", [(0, 1), (1, 0)])


def along_dp(piece, flip):
    return lax.ppermute(piece, "dp", [(j, j ^ flip) for j in range(lax.axis_size("dp"))])


def assemble(weight, *pieces):
    quarter = lax.rem(lax.axis_index("dp"), 4)
    return pl.pallas_call(
        assemble_kernel,
        in_specs=[pl.BlockSpec(memory_space=pltpu.SMEM)]
        + [pl.BlockSpec(memory_space=pltpu.VMEM)] * 4,
        out_specs=pl.BlockSpec(memory_space=pltpu.VMEM),
        out_shape=jax.ShapeDtypeStruct(weight.shape, weight.dtype),
        compiler_params=pltpu.CompilerParams(vmem_limit_bytes=VMEM_BYTES),
        cost_estimate=pl.CostEstimate(
            flops=weight.size, bytes_accessed=6 * weight.size, transcendentals=0
        ),
        name="assemble",
    )(quarter.reshape(1), *pieces)


def sum_dp(value, *between):
    count = lax.axis_size("dp")
    if count & (count - 1) or not between:
        return lax.psum(value, "dp")
    flip, between = 1, list(between)
    while flip < count:
        arrived = along_dp(value, flip)
        if between:
            arrived = after(arrived, between.pop(0))
        value = value + arrived
        flip *= 2
    return value


def swap_small(arrays):
    flat = jnp.concatenate([a.astype(jnp.float32).reshape(-1) for a in arrays])
    flat = lax.ppermute(lax.optimization_barrier(flat), "tensor", [(0, 1), (1, 0)])
    flat = lax.optimization_barrier(flat)
    result, edge = [], 0
    for a in arrays:
        result.append(flat[edge : edge + a.size].reshape(a.shape).astype(a.dtype))
        edge += a.size
    return result


def unit_forward(weights, normed, cotangent, segments, states, earlier=()):
    step = in_product(weights["step"], normed)
    gate = in_product(weights["gate"], normed).astype(bf16)
    dout = in_product(weights["out"], cotangent).astype(bf16)
    raw = in_product(weights["value"], after(normed, *earlier)).astype(bf16)
    rows, masks = step_rows(
        step, weights["step_bias"], weights["decay_log"], weights["skip_gain"], segments
    )
    into, _, _, outt = states
    mixed, entry, sums = mix_forward(
        1, raw, gate, dout, rows, masks, into, outt, weights["conv"], weights["gain_wide"]
    )
    sums = sums[:, :2].transpose(1, 0, 2).reshape(2, normed.shape[0])
    return dict(
        step=step, gate=gate, raw=raw, dout=dout, rows=rows, masks=masks, mixed=mixed,
        entry=entry, sums=sums, states=states,
    )


def unit_middle(unit, weights, both, inner_total):
    return middle(
        unit["gate"], unit["mixed"], unit["dout"], both, weights["gain_wide"], inner_total
    )


def unit_backward(unit, weights, d_gate, d_mixed, state_back, between=()):
    d_value, d_rows, d_state, d_conv = mix_backward(
        1, unit["raw"], unit["mixed"], d_mixed, unit["entry"], unit["rows"], unit["masks"],
        *unit["states"], weights["conv"],
    )
    d_value, d_rows, d_state, d_conv = lax.optimization_barrier(
        (d_value, d_rows, d_state, d_conv, *between)
    )[:4]
    d_step, *step_params = step_grads(
        d_rows, unit["step"], weights["step_bias"], weights["decay_log"], 1
    )
    d_state, g_cs, g_csb = state_back(d_state.astype(bf16).astype(jnp.float32))
    d_state, d_step = d_state.astype(bf16), d_step.astype(bf16)
    return d_value, d_state, d_step, (d_conv, g_cs, g_csb, *step_params)


def normed_part(weights, d_gate, d_value, d_state, d_step):
    return (
        out_product(d_gate, weights["gate"])
        + out_product(d_value, weights["value"])
        + right_product(d_state, weights["state"])
        + out_product(d_step, weights["step"])
    )


def local(
    hidden,
    segment_ids,
    norm_gain,
    proj_gate,
    proj_value,
    proj_state,
    proj_step,
    conv_value,
    conv_value_bias,
    conv_state,
    conv_state_bias,
    step_bias,
    decay_log,
    skip_gain,
    gate_gain,
    proj_out,
    out_grad,
):
    seq_count, length, width = hidden.shape
    local_inner = proj_gate.shape[1]
    state_width = proj_state.shape[1]
    tensor_count = lax.axis_size("tensor")
    inner_total = local_inner * tensor_count
    every = range(seq_count)
    whole_from = seq_count
    if tensor_count == 2 and lax.axis_size("dp") % 4 == 0 and seq_count > 1:
        whole_from = seq_count - 1

    own = dict(
        gate=proj_gate, value=proj_value, out=proj_out, state=proj_state, step=proj_step,
        step_bias=step_bias, decay_log=decay_log, skip_gain=skip_gain, gate_gain=gate_gain,
    )
    own["conv"] = wide_lanes(jnp.concatenate([conv_value, conv_value_bias[None, :]], axis=0))
    own["gain_wide"] = wide_lanes(gate_gain)
    if whole_from < seq_count:
        c_w, c_b, step, s_b, d_l, s_g, g_g = swap_small(
            [conv_value, conv_value_bias, proj_step, step_bias, decay_log, skip_gain, gate_gain]
        )
        other = dict(
            state=proj_state, step=step, step_bias=s_b, decay_log=d_l, skip_gain=s_g, gate_gain=g_g
        )
        sent = dict(value=proj_value, gate=proj_gate, out=proj_out)
        first = {k: gather_first(w) for k, w in sent.items()}
        second = {k: along_dp(first[k], 2) for k in ("value", "gate")}
        other["conv"] = wide_lanes(jnp.concatenate([c_w, c_b[None, :]], axis=0))
        other["gain_wide"] = wide_lanes(g_g)

    normeds, states, state_backs, units, boths = [], [], [], [], []
    for s in every:
        wide = hidden[s].astype(jnp.float32)
        row_scale = lax.rsqrt(jnp.mean(wide * wide, axis=-1, keepdims=True) + epsilon)
        normeds.append((wide * row_scale * norm_gain[None, :]).astype(bf16))
        state_raw = jnp.dot(normeds[s], proj_state, preferred_element_type=jnp.float32)
        state_conv, back = jax.vjp(
            functools.partial(causal_conv, doc_masks=lag_masks(segment_ids[s])),
            state_raw,
            conv_state,
            conv_state_bias,
        )
        state_backs.append(back)
        low = state_conv.astype(bf16)
        into, out = low[:, :STATE], low[:, STATE:]
        states.append((into, into.T, out, out.T))
        units.append(unit_forward(own, normeds[s], out_grad[s], segment_ids[s : s + 1], states[s]))
        if s < whole_from:
            sums = units[s]["sums"]
            boths.append(tensor_join(sums, tensor_others(sums)))
    branches, received, output_ins, d_gates, d_mixeds = [], [], [], [], []
    grad_gate_gain = jnp.zeros((local_inner,), jnp.float32)
    extras, middles = {}, {}
    if whole_from < seq_count:
        third, fourth = {}, {}

    backs, parts, others = [], [], []

    def own_middle(s):
        output_in, d_gate, d_mixed, grad_gain = unit_middle(units[s], own, boths[s], inner_total)
        output_ins.append(output_in)
        d_gates.append(d_gate)
        d_mixeds.append(d_mixed)
        branches.append(lax.optimization_barrier(out_product(output_in, proj_out)))
        return grad_gain

    def own_backward(s, earlier, last_hops=False):
        d_mixed = after(d_mixeds[s], *earlier)
        between = tuple(second.values()) if last_hops else ()
        d_value, *rest = unit_backward(
            units[s], own, d_gates[s], d_mixed, state_backs[s], between
        )
        if last_hops:
            second["out"] = along_dp(after(first["out"], d_value), 2)
            for k in sent:
                third[k] = along_dp(after(first[k], d_value), 1)
                fourth[k] = along_dp(after(second[k], units[-1]["mixed"]), 1)
            d_value = after(d_value, second["out"])
        backs.append((d_value, *rest))
        parts.append(lax.optimization_barrier(normed_part(own, d_gates[s], *backs[s][:3])))

    for s in range(whole_from):
        grad_gate_gain = grad_gate_gain + own_middle(s)
        received.append(tensor_others(branches[s]))
        gathers = whole_from < seq_count and s == whole_from - 1
        own_backward(s, (branches[s],), gathers)
        others.append(tensor_others(parts[s]))
    if whole_from < seq_count:
        for k in sent:
            pieces = (first[k], second[k], third[k], fourth[k])
            pieces = lax.optimization_barrier((*pieces, parts[0]))[:4]
            other[k] = assemble(sent[k], *pieces)
    for s in range(whole_from, seq_count):
        extras[s] = unit_forward(
            other, normeds[s], out_grad[s], segment_ids[s : s + 1], states[s], (received[0],)
        )
        boths.append(units[s]["sums"] + extras[s]["sums"])
        grad_gate_gain = grad_gate_gain + own_middle(s)
        middles[s] = unit_middle(extras[s], other, boths[s], inner_total)
        received.append(lax.optimization_barrier(out_product(middles[s][0], other["out"])))

    normed_all = jnp.concatenate(normeds, axis=0)
    early_part = jnp.stack(
        [
            grad_product(normed_all, jnp.concatenate(d_gates, axis=1)),
            grad_product(
                out_grad.reshape(seq_count * length, width), jnp.concatenate(output_ins, axis=1)
            ),
        ]
    )
    early = lax.psum_scatter(early_part, "dp", scatter_dimension=1, tiled=True)

    for s in range(whole_from, seq_count):
        own_backward(s, (early_part, branches[s]))
    later_part = jnp.concatenate(
        [
            grad_product(normed_all, jnp.concatenate([b[0] for b in backs], axis=1)),
            token_product(normed_all, jnp.concatenate([b[1] for b in backs], axis=0)),
            grad_product(normed_all, jnp.concatenate([b[2] for b in backs], axis=1)),
        ],
        axis=1,
    )
    waits, extra_backs = (later_part, *others), []
    for s in range(whole_from, seq_count):
        d_gate = middles[s][1]
        back = unit_backward(extras[s], other, d_gate, after(middles[s][2], *waits), state_backs[s])
        extra_backs.append(back)
    later_part = after(later_part, early, *[back[0] for back in extra_backs])
    later = lax.psum_scatter(later_part, "dp", scatter_dimension=0, tiled=True)
    later_value = later[:, :local_inner]
    edge = local_inner + state_width
    state_part = later[:, local_inner:edge]
    for s, back in zip(range(whole_from, seq_count), extra_backs):
        d_value = after(back[0], later_part)
        others.append(
            lax.optimization_barrier(normed_part(other, middles[s][1], d_value, *back[1:3]))
        )
    grad_norm_gain = jnp.zeros((width,), jnp.float32)
    for s in every:
        wide = hidden[s].astype(jnp.float32)
        row_scale = lax.rsqrt(jnp.mean(wide * wide, axis=-1, keepdims=True) + epsilon)
        grad_norm_gain = grad_norm_gain + jnp.sum(parts[s] * wide * row_scale, axis=0)
    param_grads = [sum(grads) for grads in zip(*[b[3] for b in backs])]
    d_conv, g_cs, g_csb, g_sb, g_dl, g_sg = param_grads
    d_conv = jnp.sum(d_conv, axis=-1)
    own_grads = [d_conv[:KERNEL], d_conv[KERNEL], g_sb, g_dl, g_sg, grad_gate_gain]
    shared = [g_cs, g_csb, grad_norm_gain]
    own_flat = jnp.concatenate([g.reshape(-1) for g in own_grads])
    shared_flat = jnp.concatenate([g.reshape(-1) for g in shared])
    arrived = tensor_others(shared_flat)
    between = []
    if whole_from < seq_count:
        arrived = after(arrived, *waits)
        between = [others[0], others[0], others[-1]]
    shared_flat = tensor_join(shared_flat, arrived)
    stacked = ()
    for s in reversed(every):
        stacked = finish(
            s, parts[s], only_others(parts[s], others[s]), branches[s],
            only_others(branches[s], received[s]), hidden, out_grad, norm_gain, stacked
        )
        if between and s == every[-1]:
            between.append(stacked[0])
    packed = sum_dp(jnp.concatenate([own_flat, shared_flat]), *between)
    own_sum, shared_sum = packed[: own_flat.shape[0]], packed[own_flat.shape[0] :]

    grad_proj_state = tensor_join(state_part, tensor_others(state_part))

    def split(flat, like):
        result, edge = [], 0
        for g in like:
            result.append(flat[edge : edge + g.size].reshape(g.shape))
            edge += g.size
        return result

    r_cv, r_cvb, r_sb, r_dl, r_sg, r_gg = split(own_sum, own_grads)
    r_cs, r_csb, r_ng = split(shared_sum, shared)
    return (
        *stacked,
        r_ng,
        early[0],
        later_value,
        grad_proj_state,
        later[:, edge:],
        r_cv,
        r_cvb,
        r_cs,
        r_csb,
        r_sb,
        r_dl,
        r_sg,
        r_gg,
        early[1],
    )


def solution(mesh):
    in_specs = (
        P("dp", None, None),
        P("dp", None),
        P(),
        P(None, "tensor"),
        P(None, "tensor"),
        P(),
        P(None, "tensor"),
        P(None, "tensor"),
        P("tensor"),
        P(),
        P(),
        P("tensor"),
        P("tensor"),
        P("tensor"),
        P("tensor"),
        P(None, "tensor"),
        P("dp", None, None),
    )
    out_specs = (
        P("dp", None, None),
        P("dp", None, None),
        P(),
        P("dp", "tensor"),
        P("dp", "tensor"),
        P("dp", None),
        P("dp", "tensor"),
        P(None, "tensor"),
        P("tensor"),
        P(),
        P(),
        P("tensor"),
        P("tensor"),
        P("tensor"),
        P("tensor"),
        P("dp", "tensor"),
    )
    return jax.shard_map(local, mesh=mesh, in_specs=in_specs, out_specs=out_specs, check_vma=False)
```

```python
import functools

import jax
import jax.numpy as jnp
from jax import lax
from jax.experimental import pallas as pl
from jax.experimental.pallas import tpu as pltpu
from jax.sharding import PartitionSpec as P

HEAD_DIM = 64
STATE = 128
KERNEL = 4
VMEM_BYTES = 50 * 1024 * 1024

epsilon = 1e-05
precise = lax.Precision.HIGHEST


def lag_masks(segment_row):
    length = segment_row.shape[0]
    result = [jnp.ones((length,), jnp.float32)]
    for delay in range(1, KERNEL):
        earlier = jnp.concatenate(
            [jnp.full((delay,), -1, jnp.int32), segment_row[: length - delay]]
        )
        result.append((earlier == segment_row).astype(jnp.float32))
    return result


def causal_conv(values, weight, conv_bias, doc_masks):
    length = values.shape[0]
    summed = conv_bias[None, :] + weight[KERNEL - 1][None, :] * values
    for delay in range(1, KERNEL):
        earlier = jnp.concatenate(
            [jnp.zeros((delay, values.shape[1]), jnp.float32), values[: length - delay]], axis=0
        )
        summed = summed + weight[KERNEL - 1 - delay][None, :] * earlier * doc_masks[delay][:, None]
    return jax.nn.silu(summed)


CHUNK = 128
PAIR = 2 * HEAD_DIM
LOG2E = 1.4426950408889634
NN = (((1,), (0,)), ((), ()))
NT = (((1,), (1,)), ((), ()))
TN = (((0,), (0,)), ((), ()))
bf16 = jnp.bfloat16


def mxu(a, b, dims=NN):
    return lax.dot_general(a, b, dims, preferred_element_type=jnp.float32)


def sigmoid(z):
    return 0.5 * jnp.tanh(0.5 * z) + 0.5


def pair_wide(rows, at):
    top = jnp.broadcast_to(rows[at : at + 1], (HEAD_DIM, CHUNK))
    low = jnp.broadcast_to(rows[at + 1 : at + 2], (HEAD_DIM, CHUNK))
    return jnp.concatenate([top, low], axis=0)


def decay_block(rows, h):
    run = jnp.broadcast_to(rows[h : h + 1], (CHUNK, CHUNK))
    return jnp.exp2(jnp.minimum(run - run.T, 0.0))


def doc_block(masks):
    segment = jnp.broadcast_to(masks[3:4], (CHUNK, CHUNK))
    source = lax.broadcasted_iota(jnp.int32, (CHUNK, CHUNK), 0)
    target = lax.broadcasted_iota(jnp.int32, (CHUNK, CHUNK), 1)
    return ((segment == segment.T) & (source <= target)).astype(jnp.float32)


def shifted_taps(raw, before, masks):
    lane = lax.broadcasted_iota(jnp.int32, raw.shape, 1)
    taps = [raw]
    for k in range(1, KERNEL):
        moved = pltpu.roll(jnp.where(lane >= CHUNK - k, before, raw), k, 1)
        taps.append(moved * masks[k - 1 : k])
    return taps


def conv_sum(taps, conv_ref, part):
    total = conv_ref[KERNEL, part, :]
    for k in range(KERNEL):
        total = total + conv_ref[KERNEL - 1 - k, part, :] * taps[k]
    return total


def mix_kernel(
    raw_ref, gate_ref, dout_ref, rows_ref, mask_ref, into_ref, outt_ref, conv_ref, gain_ref,
    mixed_ref, entry_ref, sums_ref, held_ref, before_ref,
):
    @pl.when(pl.program_id(1) == 0)
    def _():
        held_ref[...] = jnp.zeros_like(held_ref)
        before_ref[...] = jnp.zeros_like(before_ref)

    masks = mask_ref[0]
    into, outt = into_ref[...], outt_ref[...]
    affinity = mxu(into, outt) * doc_block(masks)

    def body(p, sums):
        part = pl.ds(pl.multiple_of(p * PAIR, PAIR), PAIR)
        rows = rows_ref[0, p]
        raw = raw_ref[part, :].astype(jnp.float32)
        pre = conv_sum(shifted_taps(raw, before_ref[part, :], masks), conv_ref, part)
        value = pre * sigmoid(pre)
        scaled = value * pair_wide(rows, 2)
        low = scaled.astype(bf16)
        near = []
        for h in range(2):
            mixing = (decay_block(rows, h) * affinity).astype(bf16)
            near.append(mxu(low[h * HEAD_DIM : (h + 1) * HEAD_DIM], mixing))
        held = held_ref[part, :]
        held_low = held.astype(bf16)
        entry_ref[0, part, :] = held_low
        far = mxu(held_low, outt) * pair_wide(rows, 6)
        kept = (scaled * pair_wide(rows, 4)).astype(bf16)
        held_ref[part, :] = held * pair_wide(rows, 8) + mxu(kept, into)
        mixed = jnp.concatenate(near, axis=0) + far + pair_wide(rows, 10) * value
        mixed_ref[part, :] = mixed
        before_ref[part, :] = raw
        gate = gate_ref[part, :].astype(jnp.float32)
        gated = mixed * gate * sigmoid(gate)
        square = jnp.sum(gated * gated, axis=0, keepdims=True)
        inner = dout_ref[part, :].astype(jnp.float32) * gain_ref[part, :] * gated
        return sums[0] + square, sums[1] + jnp.sum(inner, axis=0, keepdims=True)

    zero = jnp.zeros((1, CHUNK), jnp.float32)
    pairs = raw_ref.shape[0] // PAIR
    square, inner = lax.fori_loop(0, pairs, body, (zero, zero), unroll=min(8, pairs))
    sums_ref[0, 0:1, :] = square
    sums_ref[0, 1:2, :] = inner


def back_kernel(
    raw_ref, before_ref, mixed_ref, dmix_ref, entry_ref, rows_ref, mask_ref, into_ref, intot_ref,
    out_ref, outt_ref, conv_ref,
    draw_ref, drows_ref, dstate_ref, dconv_ref, dheld_ref, later_ref, latermask_ref, dfar_ref,
):
    step = pl.program_id(1)

    @pl.when((pl.program_id(0) == 0) & (step == 0))
    def _():
        dconv_ref[...] = jnp.zeros_like(dconv_ref)

    @pl.when(step == 0)
    def _():
        dheld_ref[...] = jnp.zeros_like(dheld_ref)
        later_ref[...] = jnp.zeros_like(later_ref)
        latermask_ref[...] = jnp.zeros_like(latermask_ref)

    first = step == pl.num_programs(1) - 1
    masks, later_masks = mask_ref[0], latermask_ref[...]
    into, intot, out, outt = into_ref[...], intot_ref[...], out_ref[...], outt_ref[...]
    allowed = doc_block(masks)
    affinity = mxu(into, outt) * allowed
    dfar_ref[...] = jnp.zeros_like(dfar_ref)
    lane = lax.broadcasted_iota(jnp.int32, (PAIR, CHUNK), 1)
    head_row = lax.broadcasted_iota(jnp.int32, (PAIR, CHUNK), 0) < HEAD_DIM

    def body(p, daffinity):
        part = pl.ds(pl.multiple_of(p * PAIR, PAIR), PAIR)
        rows = rows_ref[0, p]
        raw = raw_ref[part, :].astype(jnp.float32)
        before = jnp.where(first, 0.0, before_ref[part, :].astype(jnp.float32))
        taps = shifted_taps(raw, before, masks)
        pre = conv_sum(taps, conv_ref, part)
        gate = sigmoid(pre)
        value = pre * gate
        step_wide = pair_wide(rows, 2)
        skip_wide = pair_wide(rows, 10)
        keep_wide = pair_wide(rows, 4)
        scaled = value * step_wide
        low = scaled.astype(bf16)
        dmix_low = dmix_ref[part, :]
        dmix = dmix_low.astype(jnp.float32)
        halves = jnp.concatenate(
            [jnp.where(head_row, dmix, 0.0).astype(bf16), jnp.where(head_row, 0.0, dmix).astype(bf16)],
            axis=1,
        )
        dmixing = mxu(low, halves, TN)
        dnear = []
        for h in range(2):
            decay = decay_block(rows, h)
            mixing = (decay * affinity).astype(bf16)
            daffinity = daffinity + dmixing[:, h * CHUNK : (h + 1) * CHUNK] * decay
            dnear.append(mxu(dmix_low[h * HEAD_DIM : (h + 1) * HEAD_DIM], mixing, NT))
        dnear = jnp.concatenate(dnear, axis=0)
        held_low = entry_ref[0, part, :]
        dheld = dheld_ref[part, :]
        dheld_low = dheld.astype(bf16)
        carried = dheld * pair_wide(rows, 8)
        dfar = mxu(dheld_low, intot) * keep_wide
        kept = (scaled * keep_wide).astype(bf16)
        read = (dmix * pair_wide(rows, 6)).astype(bf16)
        dfar_ref[:, :STATE] += mxu(kept, dheld_low, TN)
        dfar_ref[:, STATE:] += mxu(read, held_low, TN)
        dheld_ref[part, :] = carried + mxu(read, out)
        dscaled = dnear + dfar
        scaled_low = low.astype(jnp.float32)
        far_product = scaled * dfar
        running = (
            dmix * (mixed_ref[part, :] - skip_wide * value) - scaled_low * dnear - far_product
        )
        products = (
            running, far_product, carried * held_low.astype(jnp.float32), dscaled * value,
            dmix * value,
        )
        for q, product in enumerate(products):
            for h in range(2):
                drows_ref[0, p, 2 * q + h : 2 * q + h + 1, :] = jnp.sum(
                    product[h * HEAD_DIM : (h + 1) * HEAD_DIM], axis=0, keepdims=True
                )
        dvalue = dscaled * step_wide + skip_wide * dmix
        dpre = dvalue * (gate * (1.0 + pre * (1.0 - gate)))
        later = later_ref[part, :]
        dconv_ref[KERNEL, part, :] += dpre
        dconv_ref[KERNEL - 1, part, :] += dpre * raw
        draw = conv_ref[KERNEL - 1, part, :] * dpre
        for k in range(1, KERNEL):
            dconv_ref[KERNEL - 1 - k, part, :] += dpre * taps[k]
            joined = jnp.where(
                lane < k, later * later_masks[k - 1 : k], dpre * masks[k - 1 : k]
            )
            draw = draw + conv_ref[KERNEL - 1 - k, part, :] * pltpu.roll(joined, CHUNK - k, 1)
        later_ref[part, :] = dpre
        draw_ref[part, :] = draw.astype(bf16)
        return daffinity

    zero = jnp.zeros((CHUNK, CHUNK), jnp.float32)
    daffinity = lax.fori_loop(0, raw_ref.shape[0] // PAIR, body, zero, unroll=2)
    daffinity = (daffinity * allowed).astype(bf16)
    dstate_ref[:, :STATE] = dfar_ref[:, :STATE] + mxu(daffinity, out)
    dstate_ref[:, STATE:] = dfar_ref[:, STATE:] + mxu(daffinity, into, TN)
    latermask_ref[...] = masks


def spec(block, index):
    return pl.BlockSpec(block, index)


def mix_forward(seqs, raw, gate, dout, rows, masks, into, outt, conv, gain):
    ch, tokens = raw.shape
    chunks = tokens // seqs // CHUNK
    at = lambda s, c: (0, s * chunks + c)
    up = lambda s, c: (s * chunks + c, 0)
    slab = spec((ch, CHUNK), at)
    return pl.pallas_call(
        mix_kernel,
        grid=(seqs, chunks),
        in_specs=[
            slab, slab, slab,
            spec((1,) + rows.shape[1:], lambda s, c: (s * chunks + c, 0, 0, 0)),
            spec((1, 8, CHUNK), lambda s, c: (s * chunks + c, 0, 0)),
            spec((CHUNK, STATE), up),
            spec((STATE, CHUNK), at),
            spec(conv.shape, lambda s, c: (0, 0, 0)),
            spec((ch, CHUNK), lambda s, c: (0, 0)),
        ],
        out_specs=[
            slab,
            spec((1, ch, STATE), lambda s, c: (s * chunks + c, 0, 0)),
            spec((1, 8, CHUNK), lambda s, c: (s * chunks + c, 0, 0)),
        ],
        out_shape=[
            jax.ShapeDtypeStruct((ch, tokens), jnp.float32),
            jax.ShapeDtypeStruct((seqs * chunks, ch, STATE), bf16),
            jax.ShapeDtypeStruct((seqs * chunks, 8, CHUNK), jnp.float32),
        ],
        scratch_shapes=[
            pltpu.VMEM((ch, STATE), jnp.float32),
            pltpu.VMEM((ch, CHUNK), jnp.float32),
        ],
        compiler_params=pltpu.CompilerParams(vmem_limit_bytes=VMEM_BYTES),
        cost_estimate=pl.CostEstimate(
            flops=tokens, bytes_accessed=tokens, transcendentals=0
        ),
        name="mix_forward",
    )(raw, gate, dout, rows, masks, into, outt, conv, gain)


def mix_backward(seqs, raw, mixed, dmix, entry, rows, masks, into, intot, out, outt, conv):
    ch, tokens = raw.shape
    chunks = tokens // seqs // CHUNK
    place = lambda s, c: s * chunks + chunks - 1 - c
    at = lambda s, c: (0, place(s, c))
    up = lambda s, c: (place(s, c), 0)
    slab = spec((ch, CHUNK), at)
    row_spec = spec((1,) + rows.shape[1:], lambda s, c: (place(s, c), 0, 0, 0))
    return pl.pallas_call(
        back_kernel,
        grid=(seqs, chunks),
        in_specs=[
            slab,
            spec((ch, CHUNK), lambda s, c: (0, jnp.maximum(place(s, c) - 1, 0))),
            slab, slab,
            spec((1, ch, STATE), lambda s, c: (place(s, c), 0, 0)),
            row_spec,
            spec((1, 8, CHUNK), lambda s, c: (place(s, c), 0, 0)),
            spec((CHUNK, STATE), up),
            spec((STATE, CHUNK), at),
            spec((CHUNK, STATE), up),
            spec((STATE, CHUNK), at),
            spec(conv.shape, lambda s, c: (0, 0, 0)),
        ],
        out_specs=[
            slab,
            row_spec,
            spec((CHUNK, 2 * STATE), up),
            spec(conv.shape, lambda s, c: (0, 0, 0)),
        ],
        out_shape=[
            jax.ShapeDtypeStruct((ch, tokens), bf16),
            jax.ShapeDtypeStruct(rows.shape, jnp.float32),
            jax.ShapeDtypeStruct((tokens, 2 * STATE), jnp.float32),
            jax.ShapeDtypeStruct(conv.shape, jnp.float32),
        ],
        scratch_shapes=[
            pltpu.VMEM((ch, STATE), jnp.float32),
            pltpu.VMEM((ch, CHUNK), jnp.float32),
            pltpu.VMEM((8, CHUNK), jnp.float32),
            pltpu.VMEM((CHUNK, 2 * STATE), jnp.float32),
        ],
        compiler_params=pltpu.CompilerParams(vmem_limit_bytes=VMEM_BYTES),
        cost_estimate=pl.CostEstimate(
            flops=tokens, bytes_accessed=tokens, transcendentals=0
        ),
        name="mix_backward",
    )(raw, raw, mixed, dmix, entry, rows, masks, into, intot, out, outt, conv)


def wide_lanes(columns):
    return jnp.broadcast_to(columns[..., None], columns.shape + (CHUNK,))


def pair_rows(parts, seqs):
    heads, _, chunks, _ = parts[0].shape
    stacked = jnp.stack(parts + [jnp.zeros_like(parts[0])] * (8 - len(parts)))
    stacked = stacked.reshape(8, heads // 2, 2, seqs * chunks, CHUNK)
    return stacked.transpose(3, 1, 0, 2, 4).reshape(seqs * chunks, heads // 2, 16, CHUNK)


def unpair_rows(rows, q, seqs):
    steps, pairs = rows.shape[:2]
    part = rows[:, :, 2 * q : 2 * q + 2, :].transpose(1, 2, 0, 3)
    return part.reshape(2 * pairs, seqs, steps // seqs, CHUNK)


def step_rows(step_raw, step_bias, decay_log, skip_gain, segment_ids):
    seqs, length = segment_ids.shape
    chunks = length // CHUNK
    heads = step_raw.shape[0]
    rate = -jnp.exp(decay_log)
    size = jax.nn.softplus(step_raw + step_bias[:, None]).reshape(heads, seqs, chunks, CHUNK)
    places = jnp.arange(CHUNK)
    upper = (places[:, None] <= places[None, :]).astype(jnp.float32)
    running = jnp.einsum(
        "hqcs,st->hqct", size * rate[:, None, None, None], upper, precision=precise
    )
    segments = segment_ids.reshape(seqs, chunks, CHUNK)
    last = segments[:, :, -1]
    before = jnp.concatenate([jnp.full((seqs, 1), -1, jnp.int32), last[:, :-1]], axis=1)
    total = running[..., -1:]
    at_end = (segments == last[..., None]).astype(jnp.float32)
    from_start = (segments == before[..., None]).astype(jnp.float32)
    through = (last == before).astype(jnp.float32)[..., None]
    full = jnp.ones_like(running)
    parts = [
        running * LOG2E,
        size,
        jnp.exp(total - running) * at_end,
        jnp.exp(running) * from_start,
        jnp.exp(total) * through * full,
        skip_gain[:, None, None, None] * full,
    ]
    lags = [jnp.stack(lag_masks(row)[1:]) for row in segment_ids]
    lags = jnp.stack(lags).reshape(seqs, KERNEL - 1, chunks, CHUNK).transpose(0, 2, 1, 3)
    masks = jnp.concatenate(
        [
            lags,
            segments[:, :, None, :].astype(jnp.float32),
            jnp.zeros((seqs, chunks, 4, CHUNK), jnp.float32),
        ],
        axis=2,
    ).reshape(seqs * chunks, 8, CHUNK)
    return pair_rows(parts, seqs), masks


def step_grads(drows, step_raw, step_bias, decay_log, seqs):
    heads, tokens = step_raw.shape
    running, far, carried, direct, skip = [unpair_rows(drows, q, seqs) for q in range(5)]
    rate = -jnp.exp(decay_log)[:, None, None, None]
    biased = step_raw + step_bias[:, None]
    size = jax.nn.softplus(biased).reshape(running.shape)
    total = jnp.sum(far + carried, axis=-1, keepdims=True)
    places = jnp.arange(CHUNK)
    lower = (places[:, None] >= places[None, :]).astype(jnp.float32)
    ddrop = jnp.einsum("hqct,ts->hqcs", running, lower, precision=precise) + total
    dsize = direct + ddrop * rate
    draw = dsize.reshape(heads, tokens) * jax.nn.sigmoid(biased)
    every = (1, 2, 3)
    return (
        draw,
        jnp.sum(draw, axis=1),
        jnp.sum(ddrop * size * rate, axis=every),
        jnp.sum(skip, axis=every),
    )


def finish_kernel(
    part_ref, other_ref, branch_ref, received_ref, hidden_ref, cotangent_ref, gain_ref, *rest
):
    out_ref, grad_ref = rest[-2:]
    wide = hidden_ref[0].astype(jnp.float32)
    width = wide.shape[1]
    row_scale = lax.rsqrt(jnp.mean(wide * wide, axis=-1, keepdims=True) + epsilon)
    scaled = (part_ref[...] + other_ref[...]) * gain_ref[...]
    inner = jnp.sum(scaled * wide, axis=-1, keepdims=True)
    grad_ref[0] = (
        cotangent_ref[0].astype(jnp.float32)
        + row_scale * scaled
        - wide * (row_scale * row_scale * row_scale * inner / width)
    )
    out_ref[0] = (wide + (branch_ref[...] + received_ref[...])).astype(bf16)


def finish(s, part, other, branch, received, hidden, out_grad, norm_gain, earlier):
    seqs, length, width = hidden.shape
    tile = 256
    flat = spec((tile, width), lambda i: (i, 0))
    deep = spec((1, tile, width), lambda i: (s, i, 0))
    held = [pl.BlockSpec(memory_space=pl.ANY)] * len(earlier)
    return pl.pallas_call(
        finish_kernel,
        grid=(length // tile,),
        in_specs=[flat] * 4 + [deep, deep, spec((1, width), lambda i: (0, 0))] + held,
        out_specs=[deep, deep],
        out_shape=[
            jax.ShapeDtypeStruct((seqs, length, width), bf16),
            jax.ShapeDtypeStruct((seqs, length, width), jnp.float32),
        ],
        input_output_aliases={7 + i: i for i in range(len(earlier))},
        compiler_params=pltpu.CompilerParams(vmem_limit_bytes=VMEM_BYTES),
        cost_estimate=pl.CostEstimate(
            flops=length, bytes_accessed=length, transcendentals=0
        ),
        name="finish",
    )(part, other, branch, received, hidden, out_grad, norm_gain[None, :], *earlier)


def middle_kernel(scale, gate_ref, mixed_ref, dout_ref, both_ref, gain_ref, *out_refs):
    in_ref, dgate_ref, dmix_ref, dgain_ref = out_refs

    @pl.when(pl.program_id(0) == 0)
    def _():
        dgain_ref[...] = jnp.zeros_like(dgain_ref)

    gated_scale = lax.rsqrt(both_ref[0:1, :] * scale + epsilon)
    pull = gated_scale * gated_scale * gated_scale * both_ref[1:2, :] * scale

    def body(p, carry):
        part = pl.ds(pl.multiple_of(p * PAIR, PAIR), PAIR)
        gate = gate_ref[part, :].astype(jnp.float32)
        mixed = mixed_ref[part, :]
        gain = gain_ref[part, :]
        sigma = sigmoid(gate)
        active = gate * sigma
        gated = mixed * active
        scaled = gated * gated_scale
        dout = dout_ref[part, :].astype(jnp.float32)
        in_ref[part, :] = (scaled * gain).astype(bf16)
        dgain_ref[part, :] += dout * scaled
        d_gated = gated_scale * (dout * gain) - gated * pull
        dmix_ref[part, :] = (d_gated * active).astype(bf16)
        dgate_ref[part, :] = (d_gated * mixed * (sigma + active * (1.0 - sigma))).astype(bf16)
        return carry

    pairs = gate_ref.shape[0] // PAIR
    lax.fori_loop(0, pairs, body, 0, unroll=min(4, pairs))


def middle(gate, mixed, dout, both, gain_wide, inner_total):
    ch, tokens = gate.shape
    slab = spec((ch, CHUNK), lambda i: (0, i))
    still = spec((ch, CHUNK), lambda i: (0, 0))
    shape = jax.ShapeDtypeStruct((ch, tokens), bf16)
    *result, gain_grad = pl.pallas_call(
        functools.partial(middle_kernel, 1.0 / inner_total),
        grid=(tokens // CHUNK,),
        in_specs=[slab, slab, slab, spec((2, CHUNK), lambda i: (0, i)), still],
        out_specs=[slab, slab, slab, still],
        out_shape=[shape, shape, shape, jax.ShapeDtypeStruct((ch, CHUNK), jnp.float32)],
        compiler_params=pltpu.CompilerParams(vmem_limit_bytes=VMEM_BYTES),
        cost_estimate=pl.CostEstimate(flops=tokens, bytes_accessed=tokens, transcendentals=0),
        name="gated_middle",
    )(gate, mixed, dout, both, gain_wide)
    return (*result, jnp.sum(gain_grad, axis=1))


def out_product(left, weight):
    return lax.dot_general(left, weight, (((0,), (1,)), ((), ())), preferred_element_type=jnp.float32)


def in_product(weight, tokens):
    return lax.dot_general(weight, tokens, (((0,), (1,)), ((), ())), preferred_element_type=jnp.float32)


def grad_product(tokens, channels):
    return lax.dot_general(
        tokens, channels, (((0,), (1,)), ((), ())), preferred_element_type=jnp.float32
    )


def right_product(left, weight):
    return lax.dot_general(
        left, weight, (((1,), (1,)), ((), ())), preferred_element_type=jnp.float32
    )


def token_product(left, right):
    return lax.dot_general(
        left, right, (((0,), (0,)), ((), ())), preferred_element_type=jnp.float32
    )


def tensor_others(part):
    count = lax.axis_size("tensor")
    if count == 2:
        return lax.ppermute(part, "tensor", [(0, 1), (1, 0)])
    return lax.psum(part, "tensor")


def tensor_join(part, others):
    return part + others if lax.axis_size("tensor") == 2 else others


def only_others(part, others):
    return others if lax.axis_size("tensor") == 2 else others - part


def after(value, *earlier):
    return lax.optimization_barrier((value, *earlier))[0]


def assemble_kernel(quarter_ref, first_ref, second_ref, third_ref, fourth_ref, whole_ref):
    rows = first_ref.shape[0]
    pieces = (first_ref, second_ref, third_ref, fourth_ref)
    for piece_ref, flip in zip(pieces, (0, 2, 1, 3)):
        place = jnp.bitwise_xor(quarter_ref[0], flip)
        part = pl.ds(pl.multiple_of(place * rows, rows), rows)
        whole_ref[part, :] = piece_ref[...].astype(whole_ref.dtype)


def gather_first(weight):
    rows, columns = weight.shape[0] // 4, weight.shape[1]
    quarter = lax.rem(lax.axis_index("dp"), 4)
    mine = lax.dynamic_slice(weight, (quarter * rows, 0), (rows, columns))
    mine = lax.optimization_barrier(mine.astype(jnp.float32))
    return lax.ppermute(mine, "tensor", [(0, 1), (1, 0)])


def along_dp(piece, flip):
    return lax.ppermute(piece, "dp", [(j, j ^ flip) for j in range(lax.axis_size("dp"))])


def assemble(weight, *pieces):
    quarter = lax.rem(lax.axis_index("dp"), 4)
    return pl.pallas_call(
        assemble_kernel,
        in_specs=[pl.BlockSpec(memory_space=pltpu.SMEM)]
        + [pl.BlockSpec(memory_space=pltpu.VMEM)] * 4,
        out_specs=pl.BlockSpec(memory_space=pltpu.VMEM),
        out_shape=jax.ShapeDtypeStruct(weight.shape, weight.dtype),
        compiler_params=pltpu.CompilerParams(vmem_limit_bytes=VMEM_BYTES),
        cost_estimate=pl.CostEstimate(
            flops=weight.size, bytes_accessed=6 * weight.size, transcendentals=0
        ),
        name="assemble",
    )(quarter.reshape(1), *pieces)


def sum_dp(value, *between):
    count = lax.axis_size("dp")
    if count & (count - 1) or not between:
        return lax.psum(value, "dp")
    flip, between = 1, list(between)
    while flip < count:
        arrived = along_dp(value, flip)
        if between:
            arrived = after(arrived, between.pop(0))
        value = value + arrived
        flip *= 2
    return value


def swap_small(arrays):
    flat = jnp.concatenate([a.astype(jnp.float32).reshape(-1) for a in arrays])
    flat = lax.ppermute(lax.optimization_barrier(flat), "tensor", [(0, 1), (1, 0)])
    flat = lax.optimization_barrier(flat)
    result, edge = [], 0
    for a in arrays:
        result.append(flat[edge : edge + a.size].reshape(a.shape).astype(a.dtype))
        edge += a.size
    return result


def unit_forward(weights, normed, cotangent, segments, states, earlier=()):
    step = in_product(weights["step"], normed)
    gate = in_product(weights["gate"], normed).astype(bf16)
    dout = in_product(weights["out"], cotangent).astype(bf16)
    raw = in_product(weights["value"], after(normed, *earlier)).astype(bf16)
    rows, masks = step_rows(
        step, weights["step_bias"], weights["decay_log"], weights["skip_gain"], segments
    )
    into, _, _, outt = states
    mixed, entry, sums = mix_forward(
        1, raw, gate, dout, rows, masks, into, outt, weights["conv"], weights["gain_wide"]
    )
    sums = sums[:, :2].transpose(1, 0, 2).reshape(2, normed.shape[0])
    return dict(
        step=step, gate=gate, raw=raw, dout=dout, rows=rows, masks=masks, mixed=mixed,
        entry=entry, sums=sums, states=states,
    )


def unit_middle(unit, weights, both, inner_total):
    return middle(
        unit["gate"], unit["mixed"], unit["dout"], both, weights["gain_wide"], inner_total
    )


def unit_backward(unit, weights, d_gate, d_mixed, state_back, between=()):
    d_value, d_rows, d_state, d_conv = mix_backward(
        1, unit["raw"], unit["mixed"], d_mixed, unit["entry"], unit["rows"], unit["masks"],
        *unit["states"], weights["conv"],
    )
    d_value, d_rows, d_state, d_conv = lax.optimization_barrier(
        (d_value, d_rows, d_state, d_conv, *between)
    )[:4]
    d_step, *step_params = step_grads(
        d_rows, unit["step"], weights["step_bias"], weights["decay_log"], 1
    )
    d_state, g_cs, g_csb = state_back(d_state.astype(bf16).astype(jnp.float32))
    d_state, d_step = d_state.astype(bf16), d_step.astype(bf16)
    return d_value, d_state, d_step, (d_conv, g_cs, g_csb, *step_params)


def normed_part(weights, d_gate, d_value, d_state, d_step):
    return (
        out_product(d_gate, weights["gate"])
        + out_product(d_value, weights["value"])
        + right_product(d_state, weights["state"])
        + out_product(d_step, weights["step"])
    )


def local(
    hidden,
    segment_ids,
    norm_gain,
    proj_gate,
    proj_value,
    proj_state,
    proj_step,
    conv_value,
    conv_value_bias,
    conv_state,
    conv_state_bias,
    step_bias,
    decay_log,
    skip_gain,
    gate_gain,
    proj_out,
    out_grad,
):
    seq_count, length, width = hidden.shape
    local_inner = proj_gate.shape[1]
    state_width = proj_state.shape[1]
    tensor_count = lax.axis_size("tensor")
    inner_total = local_inner * tensor_count
    every = range(seq_count)
    whole_from = seq_count
    if tensor_count == 2 and lax.axis_size("dp") % 4 == 0 and seq_count > 1:
        whole_from = seq_count - 1

    own = dict(
        gate=proj_gate, value=proj_value, out=proj_out, state=proj_state, step=proj_step,
        step_bias=step_bias, decay_log=decay_log, skip_gain=skip_gain, gate_gain=gate_gain,
    )
    own["conv"] = wide_lanes(jnp.concatenate([conv_value, conv_value_bias[None, :]], axis=0))
    own["gain_wide"] = wide_lanes(gate_gain)
    if whole_from < seq_count:
        c_w, c_b, step, s_b, d_l, s_g, g_g = swap_small(
            [conv_value, conv_value_bias, proj_step, step_bias, decay_log, skip_gain, gate_gain]
        )
        other = dict(
            state=proj_state, step=step, step_bias=s_b, decay_log=d_l, skip_gain=s_g, gate_gain=g_g
        )
        sent = dict(value=proj_value, gate=proj_gate, out=proj_out)
        first = {k: gather_first(w) for k, w in sent.items()}
        second = {k: along_dp(first[k], 2) for k in ("value", "gate")}
        other["conv"] = wide_lanes(jnp.concatenate([c_w, c_b[None, :]], axis=0))
        other["gain_wide"] = wide_lanes(g_g)

    normeds, states, state_backs, units, boths = [], [], [], [], []
    for s in every:
        wide = hidden[s].astype(jnp.float32)
        row_scale = lax.rsqrt(jnp.mean(wide * wide, axis=-1, keepdims=True) + epsilon)
        normeds.append((wide * row_scale * norm_gain[None, :]).astype(bf16))
        state_raw = jnp.dot(normeds[s], proj_state, preferred_element_type=jnp.float32)
        state_conv, back = jax.vjp(
            functools.partial(causal_conv, doc_masks=lag_masks(segment_ids[s])),
            state_raw,
            conv_state,
            conv_state_bias,
        )
        state_backs.append(back)
        low = state_conv.astype(bf16)
        into, out = low[:, :STATE], low[:, STATE:]
        states.append((into, into.T, out, out.T))
        units.append(unit_forward(own, normeds[s], out_grad[s], segment_ids[s : s + 1], states[s]))
        if s < whole_from:
            sums = units[s]["sums"]
            boths.append(tensor_join(sums, tensor_others(sums)))
    branches, received, output_ins, d_gates, d_mixeds = [], [], [], [], []
    grad_gate_gain = jnp.zeros((local_inner,), jnp.float32)
    extras, middles = {}, {}
    if whole_from < seq_count:
        third, fourth = {}, {}

    backs, parts, others = [], [], []

    def own_middle(s):
        output_in, d_gate, d_mixed, grad_gain = unit_middle(units[s], own, boths[s], inner_total)
        output_ins.append(output_in)
        d_gates.append(d_gate)
        d_mixeds.append(d_mixed)
        branches.append(lax.optimization_barrier(out_product(output_in, proj_out)))
        return grad_gain

    def own_backward(s, earlier, last_hops=False):
        d_mixed = after(d_mixeds[s], *earlier)
        between = tuple(second.values()) if last_hops else ()
        d_value, *rest = unit_backward(
            units[s], own, d_gates[s], d_mixed, state_backs[s], between
        )
        if last_hops:
            second["out"] = along_dp(after(first["out"], d_value), 2)
            for k in sent:
                third[k] = along_dp(after(first[k], d_value), 1)
                fourth[k] = along_dp(after(second[k], units[-1]["mixed"]), 1)
            d_value = after(d_value, second["out"])
        backs.append((d_value, *rest))
        parts.append(lax.optimization_barrier(normed_part(own, d_gates[s], *backs[s][:3])))

    for s in range(whole_from):
        grad_gate_gain = grad_gate_gain + own_middle(s)
        received.append(tensor_others(branches[s]))
        gathers = whole_from < seq_count and s == whole_from - 1
        own_backward(s, (branches[s],), gathers)
        others.append(tensor_others(parts[s]))
    if whole_from < seq_count:
        for k in sent:
            pieces = (first[k], second[k], third[k], fourth[k])
            pieces = lax.optimization_barrier((*pieces, parts[0]))[:4]
            other[k] = assemble(sent[k], *pieces)
    for s in range(whole_from, seq_count):
        extras[s] = unit_forward(
            other, normeds[s], out_grad[s], segment_ids[s : s + 1], states[s], (received[0],)
        )
        boths.append(units[s]["sums"] + extras[s]["sums"])
        grad_gate_gain = grad_gate_gain + own_middle(s)
        middles[s] = unit_middle(extras[s], other, boths[s], inner_total)
        received.append(lax.optimization_barrier(out_product(middles[s][0], other["out"])))

    normed_all = jnp.concatenate(normeds, axis=0)
    early_part = jnp.stack(
        [
            grad_product(normed_all, jnp.concatenate(d_gates, axis=1)),
            grad_product(
                out_grad.reshape(seq_count * length, width), jnp.concatenate(output_ins, axis=1)
            ),
        ]
    )
    early = lax.psum_scatter(early_part, "dp", scatter_dimension=1, tiled=True)

    for s in range(whole_from, seq_count):
        own_backward(s, (early_part, branches[s]))
    later_part = jnp.concatenate(
        [
            grad_product(normed_all, jnp.concatenate([b[0] for b in backs], axis=1)),
            token_product(normed_all, jnp.concatenate([b[1] for b in backs], axis=0)),
            grad_product(normed_all, jnp.concatenate([b[2] for b in backs], axis=1)),
        ],
        axis=1,
    )
    waits, extra_backs = (later_part,), []
    for s in range(whole_from, seq_count):
        d_gate = middles[s][1]
        back = unit_backward(
            extras[s], other, d_gate, after(middles[s][2], *waits), state_backs[s],
            tuple(others[:whole_from]),
        )
        extra_backs.append(back)
    later_part = after(later_part, early, *[back[0] for back in extra_backs])
    later = lax.psum_scatter(later_part, "dp", scatter_dimension=0, tiled=True)
    for s, back in zip(range(whole_from, seq_count), extra_backs):
        d_value = after(back[0], later_part)
        others.append(
            lax.optimization_barrier(normed_part(other, middles[s][1], d_value, *back[1:3]))
        )
    grad_norm_gain = jnp.zeros((width,), jnp.float32)
    for s in every:
        wide = hidden[s].astype(jnp.float32)
        row_scale = lax.rsqrt(jnp.mean(wide * wide, axis=-1, keepdims=True) + epsilon)
        grad_norm_gain = grad_norm_gain + jnp.sum(parts[s] * wide * row_scale, axis=0)
    param_grads = [sum(grads) for grads in zip(*[b[3] for b in backs])]
    d_conv, g_cs, g_csb, g_sb, g_dl, g_sg = param_grads
    d_conv = jnp.sum(d_conv, axis=-1)
    own_grads = [d_conv[:KERNEL], d_conv[KERNEL], g_sb, g_dl, g_sg, grad_gate_gain]
    shared = [g_cs, g_csb, grad_norm_gain]
    own_flat = jnp.concatenate([g.reshape(-1) for g in own_grads])
    shared_flat = jnp.concatenate([g.reshape(-1) for g in shared])
    arrived = tensor_others(shared_flat)
    between = []
    if whole_from < seq_count:
        arrived = after(arrived, *waits)
        between = [others[0], others[0], others[-1]]
    shared_flat = tensor_join(shared_flat, arrived)
    stacked = ()
    for s in reversed(every):
        stacked = finish(
            s, parts[s], only_others(parts[s], others[s]), branches[s],
            only_others(branches[s], received[s]), hidden, out_grad, norm_gain, stacked
        )
        if between and s == every[-1]:
            between.append(stacked[0])
    packed = sum_dp(jnp.concatenate([own_flat, shared_flat]), *between)
    own_sum, shared_sum = packed[: own_flat.shape[0]], packed[own_flat.shape[0] :]

    later = after(later, stacked[1])
    later_value = later[:, :local_inner]
    edge = local_inner + state_width
    state_part = later[:, local_inner:edge]
    grad_proj_state = tensor_join(state_part, tensor_others(state_part))

    def split(flat, like):
        result, edge = [], 0
        for g in like:
            result.append(flat[edge : edge + g.size].reshape(g.shape))
            edge += g.size
        return result

    r_cv, r_cvb, r_sb, r_dl, r_sg, r_gg = split(own_sum, own_grads)
    r_cs, r_csb, r_ng = split(shared_sum, shared)
    return (
        *stacked,
        r_ng,
        early[0],
        later_value,
        grad_proj_state,
        later[:, edge:],
        r_cv,
        r_cvb,
        r_cs,
        r_csb,
        r_sb,
        r_dl,
        r_sg,
        r_gg,
        early[1],
    )


def solution(mesh):
    in_specs = (
        P("dp", None, None),
        P("dp", None),
        P(),
        P(None, "tensor"),
        P(None, "tensor"),
        P(),
        P(None, "tensor"),
        P(None, "tensor"),
        P("tensor"),
        P(),
        P(),
        P("tensor"),
        P("tensor"),
        P("tensor"),
        P("tensor"),
        P(None, "tensor"),
        P("dp", None, None),
    )
    out_specs = (
        P("dp", None, None),
        P("dp", None, None),
        P(),
        P("dp", "tensor"),
        P("dp", "tensor"),
        P("dp", None),
        P("dp", "tensor"),
        P(None, "tensor"),
        P("tensor"),
        P(),
        P(),
        P("tensor"),
        P("tensor"),
        P("tensor"),
        P("tensor"),
        P("dp", "tensor"),
    )
    return jax.shard_map(local, mesh=mesh, in_specs=in_specs, out_specs=out_specs, check_vma=False)
```

```python
import functools

import jax
import jax.numpy as jnp
from jax import lax
from jax.experimental import pallas as pl
from jax.experimental.pallas import tpu as pltpu
from jax.sharding import PartitionSpec as P

HEAD_DIM = 64
STATE = 128
KERNEL = 4
VMEM_BYTES = 50 * 1024 * 1024

epsilon = 1e-05
precise = lax.Precision.HIGHEST


def lag_masks(segment_row):
    length = segment_row.shape[0]
    result = [jnp.ones((length,), jnp.float32)]
    for delay in range(1, KERNEL):
        earlier = jnp.concatenate(
            [jnp.full((delay,), -1, jnp.int32), segment_row[: length - delay]]
        )
        result.append((earlier == segment_row).astype(jnp.float32))
    return result


def causal_conv(values, weight, conv_bias, doc_masks):
    length = values.shape[0]
    summed = conv_bias[None, :] + weight[KERNEL - 1][None, :] * values
    for delay in range(1, KERNEL):
        earlier = jnp.concatenate(
            [jnp.zeros((delay, values.shape[1]), jnp.float32), values[: length - delay]], axis=0
        )
        summed = summed + weight[KERNEL - 1 - delay][None, :] * earlier * doc_masks[delay][:, None]
    return jax.nn.silu(summed)


CHUNK = 128
PAIR = 2 * HEAD_DIM
LOG2E = 1.4426950408889634
NN = (((1,), (0,)), ((), ()))
NT = (((1,), (1,)), ((), ()))
TN = (((0,), (0,)), ((), ()))
bf16 = jnp.bfloat16


def mxu(a, b, dims=NN):
    return lax.dot_general(a, b, dims, preferred_element_type=jnp.float32)


def sigmoid(z):
    return 0.5 * jnp.tanh(0.5 * z) + 0.5


def pair_wide(rows, at):
    top = jnp.broadcast_to(rows[at : at + 1], (HEAD_DIM, CHUNK))
    low = jnp.broadcast_to(rows[at + 1 : at + 2], (HEAD_DIM, CHUNK))
    return jnp.concatenate([top, low], axis=0)


def decay_block(rows, h):
    run = jnp.broadcast_to(rows[h : h + 1], (CHUNK, CHUNK))
    return jnp.exp2(jnp.minimum(run - run.T, 0.0))


def doc_block(masks):
    segment = jnp.broadcast_to(masks[3:4], (CHUNK, CHUNK))
    source = lax.broadcasted_iota(jnp.int32, (CHUNK, CHUNK), 0)
    target = lax.broadcasted_iota(jnp.int32, (CHUNK, CHUNK), 1)
    return ((segment == segment.T) & (source <= target)).astype(jnp.float32)


def shifted_taps(raw, before, masks):
    lane = lax.broadcasted_iota(jnp.int32, raw.shape, 1)
    taps = [raw]
    for k in range(1, KERNEL):
        moved = pltpu.roll(jnp.where(lane >= CHUNK - k, before, raw), k, 1)
        taps.append(moved * masks[k - 1 : k])
    return taps


def conv_sum(taps, conv_ref, part):
    total = conv_ref[KERNEL, part, :]
    for k in range(KERNEL):
        total = total + conv_ref[KERNEL - 1 - k, part, :] * taps[k]
    return total


def mix_kernel(
    raw_ref, gate_ref, dout_ref, rows_ref, mask_ref, into_ref, outt_ref, conv_ref, gain_ref,
    mixed_ref, entry_ref, sums_ref, held_ref, before_ref,
):
    @pl.when(pl.program_id(1) == 0)
    def _():
        held_ref[...] = jnp.zeros_like(held_ref)
        before_ref[...] = jnp.zeros_like(before_ref)

    masks = mask_ref[0]
    into, outt = into_ref[...], outt_ref[...]
    affinity = mxu(into, outt) * doc_block(masks)

    def body(p, sums):
        part = pl.ds(pl.multiple_of(p * PAIR, PAIR), PAIR)
        rows = rows_ref[0, p]
        raw = raw_ref[part, :].astype(jnp.float32)
        pre = conv_sum(shifted_taps(raw, before_ref[part, :], masks), conv_ref, part)
        value = pre * sigmoid(pre)
        scaled = value * pair_wide(rows, 2)
        low = scaled.astype(bf16)
        near = []
        for h in range(2):
            mixing = (decay_block(rows, h) * affinity).astype(bf16)
            near.append(mxu(low[h * HEAD_DIM : (h + 1) * HEAD_DIM], mixing))
        held = held_ref[part, :]
        held_low = held.astype(bf16)
        entry_ref[0, part, :] = held_low
        far = mxu(held_low, outt) * pair_wide(rows, 6)
        kept = (scaled * pair_wide(rows, 4)).astype(bf16)
        held_ref[part, :] = held * pair_wide(rows, 8) + mxu(kept, into)
        mixed = jnp.concatenate(near, axis=0) + far + pair_wide(rows, 10) * value
        mixed_ref[part, :] = mixed
        before_ref[part, :] = raw
        gate = gate_ref[part, :].astype(jnp.float32)
        gated = mixed * gate * sigmoid(gate)
        square = jnp.sum(gated * gated, axis=0, keepdims=True)
        inner = dout_ref[part, :].astype(jnp.float32) * gain_ref[part, :] * gated
        return sums[0] + square, sums[1] + jnp.sum(inner, axis=0, keepdims=True)

    zero = jnp.zeros((1, CHUNK), jnp.float32)
    pairs = raw_ref.shape[0] // PAIR
    square, inner = lax.fori_loop(0, pairs, body, (zero, zero), unroll=min(8, pairs))
    sums_ref[0, 0:1, :] = square
    sums_ref[0, 1:2, :] = inner


def back_kernel(
    raw_ref, before_ref, mixed_ref, dmix_ref, entry_ref, rows_ref, mask_ref, into_ref, intot_ref,
    out_ref, outt_ref, conv_ref,
    draw_ref, drows_ref, dstate_ref, dconv_ref, dheld_ref, later_ref, latermask_ref, dfar_ref,
):
    step = pl.program_id(1)

    @pl.when((pl.program_id(0) == 0) & (step == 0))
    def _():
        dconv_ref[...] = jnp.zeros_like(dconv_ref)

    @pl.when(step == 0)
    def _():
        dheld_ref[...] = jnp.zeros_like(dheld_ref)
        later_ref[...] = jnp.zeros_like(later_ref)
        latermask_ref[...] = jnp.zeros_like(latermask_ref)

    first = step == pl.num_programs(1) - 1
    masks, later_masks = mask_ref[0], latermask_ref[...]
    into, intot, out, outt = into_ref[...], intot_ref[...], out_ref[...], outt_ref[...]
    allowed = doc_block(masks)
    affinity = mxu(into, outt) * allowed
    dfar_ref[...] = jnp.zeros_like(dfar_ref)
    lane = lax.broadcasted_iota(jnp.int32, (PAIR, CHUNK), 1)
    head_row = lax.broadcasted_iota(jnp.int32, (PAIR, CHUNK), 0) < HEAD_DIM

    def body(p, daffinity):
        part = pl.ds(pl.multiple_of(p * PAIR, PAIR), PAIR)
        rows = rows_ref[0, p]
        raw = raw_ref[part, :].astype(jnp.float32)
        before = jnp.where(first, 0.0, before_ref[part, :].astype(jnp.float32))
        taps = shifted_taps(raw, before, masks)
        pre = conv_sum(taps, conv_ref, part)
        gate = sigmoid(pre)
        value = pre * gate
        step_wide = pair_wide(rows, 2)
        skip_wide = pair_wide(rows, 10)
        keep_wide = pair_wide(rows, 4)
        scaled = value * step_wide
        low = scaled.astype(bf16)
        dmix_low = dmix_ref[part, :]
        dmix = dmix_low.astype(jnp.float32)
        halves = jnp.concatenate(
            [jnp.where(head_row, dmix, 0.0).astype(bf16), jnp.where(head_row, 0.0, dmix).astype(bf16)],
            axis=1,
        )
        dmixing = mxu(low, halves, TN)
        dnear = []
        for h in range(2):
            decay = decay_block(rows, h)
            mixing = (decay * affinity).astype(bf16)
            daffinity = daffinity + dmixing[:, h * CHUNK : (h + 1) * CHUNK] * decay
            dnear.append(mxu(dmix_low[h * HEAD_DIM : (h + 1) * HEAD_DIM], mixing, NT))
        dnear = jnp.concatenate(dnear, axis=0)
        held_low = entry_ref[0, part, :]
        dheld = dheld_ref[part, :]
        dheld_low = dheld.astype(bf16)
        carried = dheld * pair_wide(rows, 8)
        dfar = mxu(dheld_low, intot) * keep_wide
        kept = (scaled * keep_wide).astype(bf16)
        read = (dmix * pair_wide(rows, 6)).astype(bf16)
        dfar_ref[:, :STATE] += mxu(kept, dheld_low, TN)
        dfar_ref[:, STATE:] += mxu(read, held_low, TN)
        dheld_ref[part, :] = carried + mxu(read, out)
        dscaled = dnear + dfar
        scaled_low = low.astype(jnp.float32)
        far_product = scaled * dfar
        running = (
            dmix * (mixed_ref[part, :] - skip_wide * value) - scaled_low * dnear - far_product
        )
        products = (
            running, far_product, carried * held_low.astype(jnp.float32), dscaled * value,
            dmix * value,
        )
        for q, product in enumerate(products):
            for h in range(2):
                drows_ref[0, p, 2 * q + h : 2 * q + h + 1, :] = jnp.sum(
                    product[h * HEAD_DIM : (h + 1) * HEAD_DIM], axis=0, keepdims=True
                )
        dvalue = dscaled * step_wide + skip_wide * dmix
        dpre = dvalue * (gate * (1.0 + pre * (1.0 - gate)))
        later = later_ref[part, :]
        dconv_ref[KERNEL, part, :] += dpre
        dconv_ref[KERNEL - 1, part, :] += dpre * raw
        draw = conv_ref[KERNEL - 1, part, :] * dpre
        for k in range(1, KERNEL):
            dconv_ref[KERNEL - 1 - k, part, :] += dpre * taps[k]
            joined = jnp.where(
                lane < k, later * later_masks[k - 1 : k], dpre * masks[k - 1 : k]
            )
            draw = draw + conv_ref[KERNEL - 1 - k, part, :] * pltpu.roll(joined, CHUNK - k, 1)
        later_ref[part, :] = dpre
        draw_ref[part, :] = draw.astype(bf16)
        return daffinity

    zero = jnp.zeros((CHUNK, CHUNK), jnp.float32)
    daffinity = lax.fori_loop(0, raw_ref.shape[0] // PAIR, body, zero, unroll=2)
    daffinity = (daffinity * allowed).astype(bf16)
    dstate_ref[:, :STATE] = dfar_ref[:, :STATE] + mxu(daffinity, out)
    dstate_ref[:, STATE:] = dfar_ref[:, STATE:] + mxu(daffinity, into, TN)
    latermask_ref[...] = masks


def spec(block, index):
    return pl.BlockSpec(block, index)


def mix_forward(seqs, raw, gate, dout, rows, masks, into, outt, conv, gain):
    ch, tokens = raw.shape
    chunks = tokens // seqs // CHUNK
    at = lambda s, c: (0, s * chunks + c)
    up = lambda s, c: (s * chunks + c, 0)
    slab = spec((ch, CHUNK), at)
    return pl.pallas_call(
        mix_kernel,
        grid=(seqs, chunks),
        in_specs=[
            slab, slab, slab,
            spec((1,) + rows.shape[1:], lambda s, c: (s * chunks + c, 0, 0, 0)),
            spec((1, 8, CHUNK), lambda s, c: (s * chunks + c, 0, 0)),
            spec((CHUNK, STATE), up),
            spec((STATE, CHUNK), at),
            spec(conv.shape, lambda s, c: (0, 0, 0)),
            spec((ch, CHUNK), lambda s, c: (0, 0)),
        ],
        out_specs=[
            slab,
            spec((1, ch, STATE), lambda s, c: (s * chunks + c, 0, 0)),
            spec((1, 8, CHUNK), lambda s, c: (s * chunks + c, 0, 0)),
        ],
        out_shape=[
            jax.ShapeDtypeStruct((ch, tokens), jnp.float32),
            jax.ShapeDtypeStruct((seqs * chunks, ch, STATE), bf16),
            jax.ShapeDtypeStruct((seqs * chunks, 8, CHUNK), jnp.float32),
        ],
        scratch_shapes=[
            pltpu.VMEM((ch, STATE), jnp.float32),
            pltpu.VMEM((ch, CHUNK), jnp.float32),
        ],
        compiler_params=pltpu.CompilerParams(vmem_limit_bytes=VMEM_BYTES),
        cost_estimate=pl.CostEstimate(
            flops=tokens, bytes_accessed=tokens, transcendentals=0
        ),
        name="mix_forward",
    )(raw, gate, dout, rows, masks, into, outt, conv, gain)


def mix_backward(seqs, raw, mixed, dmix, entry, rows, masks, into, intot, out, outt, conv):
    ch, tokens = raw.shape
    chunks = tokens // seqs // CHUNK
    place = lambda s, c: s * chunks + chunks - 1 - c
    at = lambda s, c: (0, place(s, c))
    up = lambda s, c: (place(s, c), 0)
    slab = spec((ch, CHUNK), at)
    row_spec = spec((1,) + rows.shape[1:], lambda s, c: (place(s, c), 0, 0, 0))
    return pl.pallas_call(
        back_kernel,
        grid=(seqs, chunks),
        in_specs=[
            slab,
            spec((ch, CHUNK), lambda s, c: (0, jnp.maximum(place(s, c) - 1, 0))),
            slab, slab,
            spec((1, ch, STATE), lambda s, c: (place(s, c), 0, 0)),
            row_spec,
            spec((1, 8, CHUNK), lambda s, c: (place(s, c), 0, 0)),
            spec((CHUNK, STATE), up),
            spec((STATE, CHUNK), at),
            spec((CHUNK, STATE), up),
            spec((STATE, CHUNK), at),
            spec(conv.shape, lambda s, c: (0, 0, 0)),
        ],
        out_specs=[
            slab,
            row_spec,
            spec((CHUNK, 2 * STATE), up),
            spec(conv.shape, lambda s, c: (0, 0, 0)),
        ],
        out_shape=[
            jax.ShapeDtypeStruct((ch, tokens), bf16),
            jax.ShapeDtypeStruct(rows.shape, jnp.float32),
            jax.ShapeDtypeStruct((tokens, 2 * STATE), jnp.float32),
            jax.ShapeDtypeStruct(conv.shape, jnp.float32),
        ],
        scratch_shapes=[
            pltpu.VMEM((ch, STATE), jnp.float32),
            pltpu.VMEM((ch, CHUNK), jnp.float32),
            pltpu.VMEM((8, CHUNK), jnp.float32),
            pltpu.VMEM((CHUNK, 2 * STATE), jnp.float32),
        ],
        compiler_params=pltpu.CompilerParams(vmem_limit_bytes=VMEM_BYTES),
        cost_estimate=pl.CostEstimate(
            flops=tokens, bytes_accessed=tokens, transcendentals=0
        ),
        name="mix_backward",
    )(raw, raw, mixed, dmix, entry, rows, masks, into, intot, out, outt, conv)


def wide_lanes(columns):
    return jnp.broadcast_to(columns[..., None], columns.shape + (CHUNK,))


def pair_rows(parts, seqs):
    heads, _, chunks, _ = parts[0].shape
    stacked = jnp.stack(parts + [jnp.zeros_like(parts[0])] * (8 - len(parts)))
    stacked = stacked.reshape(8, heads // 2, 2, seqs * chunks, CHUNK)
    return stacked.transpose(3, 1, 0, 2, 4).reshape(seqs * chunks, heads // 2, 16, CHUNK)


def unpair_rows(rows, q, seqs):
    steps, pairs = rows.shape[:2]
    part = rows[:, :, 2 * q : 2 * q + 2, :].transpose(1, 2, 0, 3)
    return part.reshape(2 * pairs, seqs, steps // seqs, CHUNK)


def step_rows(step_raw, step_bias, decay_log, skip_gain, segment_ids):
    seqs, length = segment_ids.shape
    chunks = length // CHUNK
    heads = step_raw.shape[0]
    rate = -jnp.exp(decay_log)
    size = jax.nn.softplus(step_raw + step_bias[:, None]).reshape(heads, seqs, chunks, CHUNK)
    places = jnp.arange(CHUNK)
    upper = (places[:, None] <= places[None, :]).astype(jnp.float32)
    running = jnp.einsum(
        "hqcs,st->hqct", size * rate[:, None, None, None], upper, precision=precise
    )
    segments = segment_ids.reshape(seqs, chunks, CHUNK)
    last = segments[:, :, -1]
    before = jnp.concatenate([jnp.full((seqs, 1), -1, jnp.int32), last[:, :-1]], axis=1)
    total = running[..., -1:]
    at_end = (segments == last[..., None]).astype(jnp.float32)
    from_start = (segments == before[..., None]).astype(jnp.float32)
    through = (last == before).astype(jnp.float32)[..., None]
    full = jnp.ones_like(running)
    parts = [
        running * LOG2E,
        size,
        jnp.exp(total - running) * at_end,
        jnp.exp(running) * from_start,
        jnp.exp(total) * through * full,
        skip_gain[:, None, None, None] * full,
    ]
    lags = [jnp.stack(lag_masks(row)[1:]) for row in segment_ids]
    lags = jnp.stack(lags).reshape(seqs, KERNEL - 1, chunks, CHUNK).transpose(0, 2, 1, 3)
    masks = jnp.concatenate(
        [
            lags,
            segments[:, :, None, :].astype(jnp.float32),
            jnp.zeros((seqs, chunks, 4, CHUNK), jnp.float32),
        ],
        axis=2,
    ).reshape(seqs * chunks, 8, CHUNK)
    return pair_rows(parts, seqs), masks


def step_grads(drows, step_raw, step_bias, decay_log, seqs):
    heads, tokens = step_raw.shape
    running, far, carried, direct, skip = [unpair_rows(drows, q, seqs) for q in range(5)]
    rate = -jnp.exp(decay_log)[:, None, None, None]
    biased = step_raw + step_bias[:, None]
    size = jax.nn.softplus(biased).reshape(running.shape)
    total = jnp.sum(far + carried, axis=-1, keepdims=True)
    places = jnp.arange(CHUNK)
    lower = (places[:, None] >= places[None, :]).astype(jnp.float32)
    ddrop = jnp.einsum("hqct,ts->hqcs", running, lower, precision=precise) + total
    dsize = direct + ddrop * rate
    draw = dsize.reshape(heads, tokens) * jax.nn.sigmoid(biased)
    every = (1, 2, 3)
    return (
        draw,
        jnp.sum(draw, axis=1),
        jnp.sum(ddrop * size * rate, axis=every),
        jnp.sum(skip, axis=every),
    )


def finish_kernel(
    part_ref, other_ref, branch_ref, received_ref, hidden_ref, cotangent_ref, gain_ref, *rest
):
    out_ref, grad_ref = rest[-2:]
    wide = hidden_ref[0].astype(jnp.float32)
    width = wide.shape[1]
    row_scale = lax.rsqrt(jnp.mean(wide * wide, axis=-1, keepdims=True) + epsilon)
    scaled = (part_ref[...] + other_ref[...]) * gain_ref[...]
    inner = jnp.sum(scaled * wide, axis=-1, keepdims=True)
    grad_ref[0] = (
        cotangent_ref[0].astype(jnp.float32)
        + row_scale * scaled
        - wide * (row_scale * row_scale * row_scale * inner / width)
    )
    out_ref[0] = (wide + (branch_ref[...] + received_ref[...])).astype(bf16)


def finish(s, part, other, branch, received, hidden, out_grad, norm_gain, earlier):
    seqs, length, width = hidden.shape
    tile = 256
    flat = spec((tile, width), lambda i: (i, 0))
    deep = spec((1, tile, width), lambda i: (s, i, 0))
    held = [pl.BlockSpec(memory_space=pl.ANY)] * len(earlier)
    return pl.pallas_call(
        finish_kernel,
        grid=(length // tile,),
        in_specs=[flat] * 4 + [deep, deep, spec((1, width), lambda i: (0, 0))] + held,
        out_specs=[deep, deep],
        out_shape=[
            jax.ShapeDtypeStruct((seqs, length, width), bf16),
            jax.ShapeDtypeStruct((seqs, length, width), jnp.float32),
        ],
        input_output_aliases={7 + i: i for i in range(len(earlier))},
        compiler_params=pltpu.CompilerParams(vmem_limit_bytes=VMEM_BYTES),
        cost_estimate=pl.CostEstimate(
            flops=length, bytes_accessed=length, transcendentals=0
        ),
        name="finish",
    )(part, other, branch, received, hidden, out_grad, norm_gain[None, :], *earlier)


def middle_kernel(scale, gate_ref, mixed_ref, dout_ref, both_ref, gain_ref, *out_refs):
    in_ref, dgate_ref, dmix_ref, dgain_ref = out_refs

    @pl.when(pl.program_id(0) == 0)
    def _():
        dgain_ref[...] = jnp.zeros_like(dgain_ref)

    gated_scale = lax.rsqrt(both_ref[0:1, :] * scale + epsilon)
    pull = gated_scale * gated_scale * gated_scale * both_ref[1:2, :] * scale

    def body(p, carry):
        part = pl.ds(pl.multiple_of(p * PAIR, PAIR), PAIR)
        gate = gate_ref[part, :].astype(jnp.float32)
        mixed = mixed_ref[part, :]
        gain = gain_ref[part, :]
        sigma = sigmoid(gate)
        active = gate * sigma
        gated = mixed * active
        scaled = gated * gated_scale
        dout = dout_ref[part, :].astype(jnp.float32)
        in_ref[part, :] = (scaled * gain).astype(bf16)
        dgain_ref[part, :] += dout * scaled
        d_gated = gated_scale * (dout * gain) - gated * pull
        dmix_ref[part, :] = (d_gated * active).astype(bf16)
        dgate_ref[part, :] = (d_gated * mixed * (sigma + active * (1.0 - sigma))).astype(bf16)
        return carry

    pairs = gate_ref.shape[0] // PAIR
    lax.fori_loop(0, pairs, body, 0, unroll=min(4, pairs))


def middle(gate, mixed, dout, both, gain_wide, inner_total):
    ch, tokens = gate.shape
    slab = spec((ch, CHUNK), lambda i: (0, i))
    still = spec((ch, CHUNK), lambda i: (0, 0))
    shape = jax.ShapeDtypeStruct((ch, tokens), bf16)
    *result, gain_grad = pl.pallas_call(
        functools.partial(middle_kernel, 1.0 / inner_total),
        grid=(tokens // CHUNK,),
        in_specs=[slab, slab, slab, spec((2, CHUNK), lambda i: (0, i)), still],
        out_specs=[slab, slab, slab, still],
        out_shape=[shape, shape, shape, jax.ShapeDtypeStruct((ch, CHUNK), jnp.float32)],
        compiler_params=pltpu.CompilerParams(vmem_limit_bytes=VMEM_BYTES),
        cost_estimate=pl.CostEstimate(flops=tokens, bytes_accessed=tokens, transcendentals=0),
        name="gated_middle",
    )(gate, mixed, dout, both, gain_wide)
    return (*result, jnp.sum(gain_grad, axis=1))


def out_product(left, weight):
    return lax.dot_general(left, weight, (((0,), (1,)), ((), ())), preferred_element_type=jnp.float32)


def in_product(weight, tokens):
    return lax.dot_general(weight, tokens, (((0,), (1,)), ((), ())), preferred_element_type=jnp.float32)


def grad_product(tokens, channels):
    return lax.dot_general(
        tokens, channels, (((0,), (1,)), ((), ())), preferred_element_type=jnp.float32
    )


def right_product(left, weight):
    return lax.dot_general(
        left, weight, (((1,), (1,)), ((), ())), preferred_element_type=jnp.float32
    )


def token_product(left, right):
    return lax.dot_general(
        left, right, (((0,), (0,)), ((), ())), preferred_element_type=jnp.float32
    )


def tensor_others(part):
    count = lax.axis_size("tensor")
    if count == 2:
        return lax.ppermute(part, "tensor", [(0, 1), (1, 0)])
    return lax.psum(part, "tensor")


def tensor_join(part, others):
    return part + others if lax.axis_size("tensor") == 2 else others


def only_others(part, others):
    return others if lax.axis_size("tensor") == 2 else others - part


def after(value, *earlier):
    return lax.optimization_barrier((value, *earlier))[0]


def assemble_kernel(quarter_ref, first_ref, second_ref, third_ref, fourth_ref, whole_ref):
    rows = first_ref.shape[0]
    pieces = (first_ref, second_ref, third_ref, fourth_ref)
    for piece_ref, flip in zip(pieces, (0, 2, 1, 3)):
        place = jnp.bitwise_xor(quarter_ref[0], flip)
        part = pl.ds(pl.multiple_of(place * rows, rows), rows)
        whole_ref[part, :] = piece_ref[...].astype(whole_ref.dtype)


def gather_first(weight, flip=0):
    rows, columns = weight.shape[0] // 4, weight.shape[1]
    quarter = jnp.bitwise_xor(lax.rem(lax.axis_index("dp"), 4), flip)
    mine = lax.dynamic_slice(weight, (quarter * rows, 0), (rows, columns))
    mine = lax.optimization_barrier(mine.astype(jnp.float32))
    return lax.ppermute(mine, "tensor", [(0, 1), (1, 0)])


def along_dp(piece, flip):
    return lax.ppermute(piece, "dp", [(j, j ^ flip) for j in range(lax.axis_size("dp"))])


def assemble(weight, *pieces):
    quarter = lax.rem(lax.axis_index("dp"), 4)
    return pl.pallas_call(
        assemble_kernel,
        in_specs=[pl.BlockSpec(memory_space=pltpu.SMEM)]
        + [pl.BlockSpec(memory_space=pltpu.VMEM)] * 4,
        out_specs=pl.BlockSpec(memory_space=pltpu.VMEM),
        out_shape=jax.ShapeDtypeStruct(weight.shape, weight.dtype),
        compiler_params=pltpu.CompilerParams(vmem_limit_bytes=VMEM_BYTES),
        cost_estimate=pl.CostEstimate(
            flops=weight.size, bytes_accessed=6 * weight.size, transcendentals=0
        ),
        name="assemble",
    )(quarter.reshape(1), *pieces)


def sum_dp(value, *between):
    count = lax.axis_size("dp")
    if count & (count - 1) or not between:
        return lax.psum(value, "dp")
    flip, between = 1, list(between)
    while flip < count:
        arrived = along_dp(value, flip)
        if between:
            arrived = after(arrived, between.pop(0))
        value = value + arrived
        flip *= 2
    return value


def swap_small(arrays):
    flat = jnp.concatenate([a.astype(jnp.float32).reshape(-1) for a in arrays])
    flat = lax.ppermute(lax.optimization_barrier(flat), "tensor", [(0, 1), (1, 0)])
    flat = lax.optimization_barrier(flat)
    result, edge = [], 0
    for a in arrays:
        result.append(flat[edge : edge + a.size].reshape(a.shape).astype(a.dtype))
        edge += a.size
    return result


def unit_forward(weights, normed, cotangent, segments, states, earlier=()):
    step = in_product(weights["step"], normed)
    gate = in_product(weights["gate"], normed).astype(bf16)
    dout = in_product(weights["out"], cotangent).astype(bf16)
    raw = in_product(weights["value"], after(normed, *earlier)).astype(bf16)
    rows, masks = step_rows(
        step, weights["step_bias"], weights["decay_log"], weights["skip_gain"], segments
    )
    into, _, _, outt = states
    mixed, entry, sums = mix_forward(
        1, raw, gate, dout, rows, masks, into, outt, weights["conv"], weights["gain_wide"]
    )
    sums = sums[:, :2].transpose(1, 0, 2).reshape(2, normed.shape[0])
    return dict(
        step=step, gate=gate, raw=raw, dout=dout, rows=rows, masks=masks, mixed=mixed,
        entry=entry, sums=sums, states=states,
    )


def unit_middle(unit, weights, both, inner_total):
    return middle(
        unit["gate"], unit["mixed"], unit["dout"], both, weights["gain_wide"], inner_total
    )


def unit_backward(unit, weights, d_gate, d_mixed, state_back, between=()):
    d_value, d_rows, d_state, d_conv = mix_backward(
        1, unit["raw"], unit["mixed"], d_mixed, unit["entry"], unit["rows"], unit["masks"],
        *unit["states"], weights["conv"],
    )
    d_value, d_rows, d_state, d_conv = lax.optimization_barrier(
        (d_value, d_rows, d_state, d_conv, *between)
    )[:4]
    d_step, *step_params = step_grads(
        d_rows, unit["step"], weights["step_bias"], weights["decay_log"], 1
    )
    d_state, g_cs, g_csb = state_back(d_state.astype(bf16).astype(jnp.float32))
    d_state, d_step = d_state.astype(bf16), d_step.astype(bf16)
    return d_value, d_state, d_step, (d_conv, g_cs, g_csb, *step_params)


def normed_part(weights, d_gate, d_value, d_state, d_step):
    return (
        out_product(d_gate, weights["gate"])
        + out_product(d_value, weights["value"])
        + right_product(d_state, weights["state"])
        + out_product(d_step, weights["step"])
    )


def local(
    hidden,
    segment_ids,
    norm_gain,
    proj_gate,
    proj_value,
    proj_state,
    proj_step,
    conv_value,
    conv_value_bias,
    conv_state,
    conv_state_bias,
    step_bias,
    decay_log,
    skip_gain,
    gate_gain,
    proj_out,
    out_grad,
):
    seq_count, length, width = hidden.shape
    local_inner = proj_gate.shape[1]
    state_width = proj_state.shape[1]
    tensor_count = lax.axis_size("tensor")
    inner_total = local_inner * tensor_count
    every = range(seq_count)
    whole_from = seq_count
    if tensor_count == 2 and lax.axis_size("dp") % 4 == 0 and seq_count > 1:
        whole_from = seq_count - 1

    own = dict(
        gate=proj_gate, value=proj_value, out=proj_out, state=proj_state, step=proj_step,
        step_bias=step_bias, decay_log=decay_log, skip_gain=skip_gain, gate_gain=gate_gain,
    )
    own["conv"] = wide_lanes(jnp.concatenate([conv_value, conv_value_bias[None, :]], axis=0))
    own["gain_wide"] = wide_lanes(gate_gain)
    if whole_from < seq_count:
        c_w, c_b, step, s_b, d_l, s_g, g_g = swap_small(
            [conv_value, conv_value_bias, proj_step, step_bias, decay_log, skip_gain, gate_gain]
        )
        other = dict(
            state=proj_state, step=step, step_bias=s_b, decay_log=d_l, skip_gain=s_g, gate_gain=g_g
        )
        sent = dict(value=proj_value, gate=proj_gate, out=proj_out)
        first = {k: gather_first(w) for k, w in sent.items()}
        second = {k: along_dp(first[k], 2) for k in ("value", "gate")}
        second["out"] = gather_first(proj_out, 2)
        other["conv"] = wide_lanes(jnp.concatenate([c_w, c_b[None, :]], axis=0))
        other["gain_wide"] = wide_lanes(g_g)

    normeds, states, state_backs, units, boths = [], [], [], [], []
    for s in every:
        wide = hidden[s].astype(jnp.float32)
        row_scale = lax.rsqrt(jnp.mean(wide * wide, axis=-1, keepdims=True) + epsilon)
        normeds.append((wide * row_scale * norm_gain[None, :]).astype(bf16))
        state_raw = jnp.dot(normeds[s], proj_state, preferred_element_type=jnp.float32)
        state_conv, back = jax.vjp(
            functools.partial(causal_conv, doc_masks=lag_masks(segment_ids[s])),
            state_raw,
            conv_state,
            conv_state_bias,
        )
        state_backs.append(back)
        low = state_conv.astype(bf16)
        into, out = low[:, :STATE], low[:, STATE:]
        states.append((into, into.T, out, out.T))
        units.append(unit_forward(own, normeds[s], out_grad[s], segment_ids[s : s + 1], states[s]))
        if s < whole_from:
            sums = units[s]["sums"]
            boths.append(tensor_join(sums, tensor_others(sums)))
    branches, received, output_ins, d_gates, d_mixeds = [], [], [], [], []
    grad_gate_gain = jnp.zeros((local_inner,), jnp.float32)
    extras, middles = {}, {}
    if whole_from < seq_count:
        third, fourth = {}, {}

    backs, parts, others = [], [], []

    def own_middle(s):
        output_in, d_gate, d_mixed, grad_gain = unit_middle(units[s], own, boths[s], inner_total)
        output_ins.append(output_in)
        d_gates.append(d_gate)
        d_mixeds.append(d_mixed)
        branches.append(lax.optimization_barrier(out_product(output_in, proj_out)))
        return grad_gain

    def own_backward(s, earlier, last_hops=False):
        d_mixed = after(d_mixeds[s], *earlier)
        between = (second["value"], second["gate"]) if last_hops else ()
        d_value, *rest = unit_backward(
            units[s], own, d_gates[s], d_mixed, state_backs[s], between
        )
        if last_hops:
            for k in sent:
                third[k] = along_dp(after(first[k], d_value), 1)
                fourth[k] = along_dp(after(second[k], units[-1]["mixed"]), 1)
        backs.append((d_value, *rest))
        parts.append(lax.optimization_barrier(normed_part(own, d_gates[s], *backs[s][:3])))

    for s in range(whole_from):
        grad_gate_gain = grad_gate_gain + own_middle(s)
        received.append(tensor_others(branches[s]))
        gathers = whole_from < seq_count and s == whole_from - 1
        own_backward(s, (branches[s],), gathers)
        others.append(tensor_others(parts[s]))
    if whole_from < seq_count:
        for k in sent:
            pieces = (first[k], second[k], third[k], fourth[k])
            pieces = lax.optimization_barrier((*pieces, parts[0]))[:4]
            other[k] = assemble(sent[k], *pieces)
    for s in range(whole_from, seq_count):
        extras[s] = unit_forward(
            other, normeds[s], out_grad[s], segment_ids[s : s + 1], states[s], (received[0],)
        )
        boths.append(units[s]["sums"] + extras[s]["sums"])
        grad_gate_gain = grad_gate_gain + own_middle(s)
        middles[s] = unit_middle(extras[s], other, boths[s], inner_total)
        received.append(lax.optimization_barrier(out_product(middles[s][0], other["out"])))

    normed_all = jnp.concatenate(normeds, axis=0)
    early_part = jnp.stack(
        [
            grad_product(normed_all, jnp.concatenate(d_gates, axis=1)),
            grad_product(
                out_grad.reshape(seq_count * length, width), jnp.concatenate(output_ins, axis=1)
            ),
        ]
    )
    early = lax.psum_scatter(early_part, "dp", scatter_dimension=1, tiled=True)

    for s in range(whole_from, seq_count):
        own_backward(s, (early_part, branches[s]))
    later_part = jnp.concatenate(
        [
            grad_product(normed_all, jnp.concatenate([b[0] for b in backs], axis=1)),
            token_product(normed_all, jnp.concatenate([b[1] for b in backs], axis=0)),
            grad_product(normed_all, jnp.concatenate([b[2] for b in backs], axis=1)),
        ],
        axis=1,
    )
    waits, extra_backs = (later_part,), []
    for s in range(whole_from, seq_count):
        d_gate = middles[s][1]
        back = unit_backward(
            extras[s], other, d_gate, after(middles[s][2], *waits), state_backs[s],
            tuple(others[:whole_from]),
        )
        extra_backs.append(back)
    later_part = after(later_part, early, *[back[0] for back in extra_backs])
    later = lax.psum_scatter(later_part, "dp", scatter_dimension=0, tiled=True)
    for s, back in zip(range(whole_from, seq_count), extra_backs):
        d_value = after(back[0], later_part)
        others.append(
            lax.optimization_barrier(normed_part(other, middles[s][1], d_value, *back[1:3]))
        )
    grad_norm_gain = jnp.zeros((width,), jnp.float32)
    for s in every:
        wide = hidden[s].astype(jnp.float32)
        row_scale = lax.rsqrt(jnp.mean(wide * wide, axis=-1, keepdims=True) + epsilon)
        grad_norm_gain = grad_norm_gain + jnp.sum(parts[s] * wide * row_scale, axis=0)
    param_grads = [sum(grads) for grads in zip(*[b[3] for b in backs])]
    d_conv, g_cs, g_csb, g_sb, g_dl, g_sg = param_grads
    d_conv = jnp.sum(d_conv, axis=-1)
    own_grads = [d_conv[:KERNEL], d_conv[KERNEL], g_sb, g_dl, g_sg, grad_gate_gain]
    shared = [g_cs, g_csb, grad_norm_gain]
    own_flat = jnp.concatenate([g.reshape(-1) for g in own_grads])
    shared_flat = jnp.concatenate([g.reshape(-1) for g in shared])
    arrived = tensor_others(shared_flat)
    between = []
    if whole_from < seq_count:
        arrived = after(arrived, *waits)
        between = [others[0], others[0], others[-1]]
    shared_flat = tensor_join(shared_flat, arrived)
    stacked = ()
    for s in reversed(every):
        stacked = finish(
            s, parts[s], only_others(parts[s], others[s]), branches[s],
            only_others(branches[s], received[s]), hidden, out_grad, norm_gain, stacked
        )
        if between and s == every[-1]:
            between.append(stacked[0])
    packed = sum_dp(jnp.concatenate([own_flat, shared_flat]), *between)
    own_sum, shared_sum = packed[: own_flat.shape[0]], packed[own_flat.shape[0] :]

    later = after(later, stacked[1])
    later_value = later[:, :local_inner]
    edge = local_inner + state_width
    state_part = later[:, local_inner:edge]
    grad_proj_state = tensor_join(state_part, tensor_others(state_part))

    def split(flat, like):
        result, edge = [], 0
        for g in like:
            result.append(flat[edge : edge + g.size].reshape(g.shape))
            edge += g.size
        return result

    r_cv, r_cvb, r_sb, r_dl, r_sg, r_gg = split(own_sum, own_grads)
    r_cs, r_csb, r_ng = split(shared_sum, shared)
    return (
        *stacked,
        r_ng,
        early[0],
        later_value,
        grad_proj_state,
        later[:, edge:],
        r_cv,
        r_cvb,
        r_cs,
        r_csb,
        r_sb,
        r_dl,
        r_sg,
        r_gg,
        early[1],
    )


def solution(mesh):
    in_specs = (
        P("dp", None, None),
        P("dp", None),
        P(),
        P(None, "tensor"),
        P(None, "tensor"),
        P(),
        P(None, "tensor"),
        P(None, "tensor"),
        P("tensor"),
        P(),
        P(),
        P("tensor"),
        P("tensor"),
        P("tensor"),
        P("tensor"),
        P(None, "tensor"),
        P("dp", None, None),
    )
    out_specs = (
        P("dp", None, None),
        P("dp", None, None),
        P(),
        P("dp", "tensor"),
        P("dp", "tensor"),
        P("dp", None),
        P("dp", "tensor"),
        P(None, "tensor"),
        P("tensor"),
        P(),
        P(),
        P("tensor"),
        P("tensor"),
        P("tensor"),
        P("tensor"),
        P("dp", "tensor"),
    )
    return jax.shard_map(local, mesh=mesh, in_specs=in_specs, out_specs=out_specs, check_vma=False)
```
